32 devices in a mesh: section: 2 (over core), grp: 4 (over y, x), dp: 4 (over z).
Axes of the slice: x: 2, y: 2, z: 4, core: 2. Of those that a mesh axis runs over, the one named last changes fastest.
Arguments:
- boundary: bfloat16 [2, 2, 16, 128, 2048], P('section', None, ('grp', 'dp')), may hold values from -6 to 6
- doc_lengths: int32 [2, 16, 3], P(None, ('grp', 'dp')), may hold values from 1 to 64, as said below
- norm_gain: bfloat16 [2, 2048], P('section', 'dp'), may hold values from 0.5 to 1.5
- in_weight: bfloat16 [2, 2048, 8192], P('section', 'dp'), may hold values from -0.125 to 0.125
- conv_weight: bfloat16 [2, 4, 4096], P('section', None, 'dp'), may hold values from -3 to 3
- conv_bias: bfloat16 [2, 4096], P('section', 'dp'), may hold values from -3 to 3
- down_weight: bfloat16 [2, 4096, 128], P('section', 'dp'), may hold values from -0.09375 to 0.09375
- kq_weight: bfloat16 [2, 32, 4096], P('section', None, 'dp'), may hold values from -0.09375 to 0.09375
- dt_weight: bfloat16 [2, 128, 4096], P('section', None, 'dp'), may hold values from -0.5 to 0.5
- dt_bias: bfloat16 [2, 4096], P('section', 'dp'), may hold values from -3 to 1
- skip_weight: bfloat16 [2, 4096], P('section', 'dp'), may hold values from 0.5 to 1.5
- out_weight: bfloat16 [2, 4096, 2048], P('section', 'dp'), may hold values from -0.25 to 0.25
Outputs:
- result: float32 [2, 2, 16, 128, 2048], P('section', None, ('grp', 'dp'))
- grad_norm_gain: float32 [2, 2048], P('section', 'dp')
- grad_in_weight: float32 [2, 2048, 8192], P('section', 'dp')
- grad_conv_weight: float32 [2, 4, 4096], P('section', None, 'dp')
- grad_conv_bias: float32 [2, 4096], P('section', 'dp')
- grad_down_weight: float32 [2, 4096, 128], P('section', 'dp')
- grad_kq_weight: float32 [2, 32, 4096], P('section', None, 'dp')
- grad_dt_weight: float32 [2, 128, 4096], P('section', None, 'dp')
- grad_dt_bias: float32 [2, 4096], P('section', 'dp')
- grad_skip_weight: float32 [2, 4096], P('section', 'dp')
- grad_out_weight: float32 [2, 4096, 2048], P('section', 'dp')
The draws below stay inside these ranges and needn't reach their ends.
Inputs may be any that keep to these rules, and one draw needn't show every extreme that they name: `doc_lengths`: in every slot one document, at a place drawn from the seed, has exactly 64 positions and the others 1 to 32, so a slot never overflows.
All inputs are finite; a program needn't handle non-finite values.
Results may differ from the reference program's by a relative error of at most 0.02.
Values may be sent and summed in bfloat16 or wider, within the bound.
No kernel may reach another device: no remote copies, remote signals or barrier semaphores. Data moves between devices by JAX's collectives and lax.ppermute only.
A program may use at most 448 MiB of HBM per device.

```python
import jax
import jax.numpy as jnp
from jax import lax

D = 2048
INNER = 4096
STATE = 16
CONV = 4
RANK = 128
SLOT = 128
MB = 2
DOCS = 3
BLOCK = 16
BATCH = 16
N_SECTION = 2


def draw_doc_lengths(key, part):
    key = jax.random.fold_in(key, 7)
    first_key, second_key = jax.random.split(key)
    shorter = jax.random.randint(first_key, (MB, BATCH, DOCS), 1, SLOT // 4 + 1)
    long_slot = jax.random.randint(second_key, (MB, BATCH, 1), 0, DOCS)
    position = jnp.arange(DOCS)[None, None, :]
    return jnp.where(position == long_slot, SLOT // 2, shorter).astype(jnp.int32)


def spiked(values, key, source, target, parts, factor):
    owner, partner = [(jnp.arange(values.shape[dim]) // (values.shape[dim] // parts)).reshape([-1 if axis == dim else 1 for axis in range(values.ndim)]) for dim in (source, target)]
    chosen = jax.random.permutation(key, parts)[partner]
    strong = (owner == chosen) | (owner == (partner + parts // 2) % parts)
    return jnp.where(strong, factor * values, values)


def level_of(rng, extent, cuts, smallest, largest):
    def one(dim, blocks):
        steps = jax.random.uniform(jax.random.fold_in(jax.random.fold_in(rng, 6), dim), (blocks,), jnp.float32, smallest / len(cuts), largest / len(cuts))
        return jnp.repeat(jnp.exp(steps), extent[dim] // blocks).reshape((-1,) + (1,) * (len(extent) - dim - 1))

    level = one(*cuts[0])
    for cut in cuts[1:]:
        level = level * one(*cut)
    return level


def normal_values(key, shape, spread, reach, cuts=(), kind=jnp.bfloat16):
    loudness = level_of(key, shape, cuts, -0.22, 0.18) if cuts else 1.0
    values = jax.random.normal(key, shape, jnp.float32) * spread * loudness
    return jnp.minimum(jnp.maximum(values, -reach), reach).astype(kind)


def heavy_noise(rng, dims, scale, limit, cuts, heavy, kind=jnp.bfloat16):
    drawn = scale * jax.random.normal(rng, dims, jnp.float32)
    if cuts:
        drawn = drawn * level_of(rng, dims, cuts, -0.22, 0.18)
    return jnp.clip(spiked(drawn, jax.random.fold_in(rng, 3), *heavy), -limit, limit).astype(kind)


def setup_inputs(seed: int = 0) -> dict:
    arg_keys = jax.random.split(jax.random.key(seed), 13)
    return {
        "boundary": heavy_noise(arg_keys[0], (N_SECTION, MB, BATCH, SLOT, D), 1.0, 6.0, ((0, 2), (2, 16)), (2, 4, 16, 2.0)),
        "doc_lengths": draw_doc_lengths(jax.random.fold_in(arg_keys[12], 71), 0),
        "norm_gain": jnp.clip(1.0 + 0.1 * jax.random.normal(arg_keys[2], (N_SECTION, D), jnp.float32), 0.5, 1.5).astype(jnp.bfloat16),
        "in_weight": normal_values(arg_keys[3], (N_SECTION, D, 2 * INNER), D ** -0.5, 0.125, ((0, 2), (1, 4))),
        "conv_weight": normal_values(arg_keys[4], (N_SECTION, CONV, INNER), CONV ** -0.5, 3.0, ((0, 2), (2, 4))),
        "conv_bias": normal_values(arg_keys[5], (N_SECTION, INNER), 0.5, 3.0, ((0, 2), (1, 4))),
        "down_weight": normal_values(arg_keys[6], (N_SECTION, INNER, RANK), INNER ** -0.5, 0.09375, ((0, 2), (1, 4))),
        "kq_weight": normal_values(arg_keys[7], (N_SECTION, 2 * STATE, INNER), INNER ** -0.5, 0.09375, ((0, 2), (2, 4))),
        "dt_weight": normal_values(arg_keys[8], (N_SECTION, RANK, INNER), RANK ** -0.5, 0.5, ((0, 2), (2, 4))),
        "dt_bias": jnp.clip(-3.0 + 4.0 * jax.random.uniform(arg_keys[9], (N_SECTION, INNER), jnp.float32) ** level_of(arg_keys[9], (N_SECTION, INNER), ((0, 2), (1, 4)), -0.2, 0.2), -3.0, 1.0).astype(jnp.bfloat16),
        "skip_weight": jnp.clip(0.5 + 1.0 * jax.random.uniform(arg_keys[10], (N_SECTION, INNER), jnp.float32) ** level_of(arg_keys[10], (N_SECTION, INNER), ((0, 2), (1, 4)), -0.2, 0.2), 0.5, 1.5).astype(jnp.bfloat16),
        "out_weight": normal_values(arg_keys[11], (N_SECTION, INNER, D), (INNER // 8) ** -0.5, 0.25, ((0, 2), (1, 4))),
    }


@jax.custom_vjp
def low(v):
    return lax.optimization_barrier(v.astype(jnp.bfloat16)).astype(jnp.float32)

@jax.custom_vjp
def low_back(v):
    return v

def low_keep(v):
    return (low(v), None)

def low_pass(kept, grad):
    return (grad,)

def back_keep(v):
    return (v, None)

def back_low(kept, grad):
    return (low(grad),)
low.defvjp(low_keep, low_pass)
low_back.defvjp(back_keep, back_low)
EPSILON = 1e-05

def highest_dot(left_op, right_op):
    return jnp.dot(left_op, right_op, precision=lax.Precision.HIGHEST)

def doc_layout(lengths):
    doc_ends = jnp.cumsum(lengths).astype(jnp.int32)
    position = jnp.arange(SLOT, dtype=jnp.int32)
    segment = lax.optimization_barrier(jnp.sum((position[:, None] >= doc_ends[None, :]).astype(jnp.int32), axis=1)).astype(jnp.int32)
    row_valid = (position < doc_ends[-1]).astype(jnp.float32)
    previous = jnp.concatenate([jnp.full((1,), -1, jnp.int32), segment[:-1]])
    carry_on = (previous == segment).astype(jnp.float32)
    return (segment, row_valid, carry_on)

def causal_conv(source, segment, conv_taps, conv_bias):
    summed = conv_bias[None, :] + conv_taps[0][None, :] * source
    for offset in range(1, conv_taps.shape[0]):
        earlier = jnp.concatenate([jnp.zeros((offset, source.shape[1]), source.dtype), source[:-offset]], axis=0)
        before = jnp.concatenate([jnp.full((offset,), -1, jnp.int32), segment[:-offset]])
        same_doc = (before == segment).astype(source.dtype)
        summed = summed + conv_taps[offset][None, :] * earlier * same_doc[:, None]
    return summed

def block_scan(carried, pieces):
    step_size, key_vec, queries, values, carry_on = pieces
    key_sq = key_vec * key_vec
    state = carried
    readouts = []
    for position in range(step_size.shape[0]):
        decay = carry_on[position] * (1.0 - key_sq[position][:, None] * step_size[position][None, :])
        drive = key_vec[position][:, None] * (step_size[position] * values[position])[None, :]
        state = decay * state + drive
        readouts.append(lax.optimization_barrier(jnp.sum(state * queries[position][:, None], axis=0)))
    return (state, jnp.stack(readouts))

def recurrence(step_size, key_vec, queries, values, carry_on):
    length, channels = values.shape
    blocks = length // BLOCK

    def blocked(array):
        return array.reshape((blocks, BLOCK) + array.shape[1:])
    initial = jnp.zeros((key_vec.shape[1], channels), values.dtype)
    final_state, readout = lax.scan(jax.checkpoint(block_scan), initial, (blocked(step_size), blocked(key_vec), blocked(queries), blocked(values), blocked(carry_on)))
    return readout.reshape(length, channels)

def mixer(carry_on, rate_in, kq_rows, values, gate_rows, rate_bias, skip_gain):
    state_dim = kq_rows.shape[1] // 2
    key_vec, queries = (kq_rows[:, :state_dim], kq_rows[:, state_dim:])
    strength = jax.nn.sigmoid(rate_in + rate_bias[None, :])
    step_size = strength / (1.0 + strength * lax.optimization_barrier(jnp.sum(key_vec * key_vec, axis=1, keepdims=True)))
    combined = recurrence(step_size, key_vec, queries, values, carry_on) + skip_gain[None, :] * values
    return combined * jax.nn.silu(gate_rows)

def layer(hidden, segment, row_valid, carry_on, weights):
    norm_gain, w_in, conv_taps, conv_bias, w_down, w_kq, w_rate, rate_bias, skip_gain, w_out = weights
    channels = w_kq.shape[1]
    inv_rms = lax.rsqrt(lax.optimization_barrier(jnp.mean(hidden * hidden, axis=1, keepdims=True)) + EPSILON)
    normed = low(hidden * inv_rms * norm_gain[None, :])
    projected = low_back(highest_dot(normed, w_in))
    inner_act = low(jax.nn.silu(causal_conv(projected[:, :channels], segment, conv_taps, conv_bias)))
    low_rank = low_back(highest_dot(inner_act, w_down))
    kq_rows = low_back(highest_dot(inner_act, w_kq.T))
    rate_pre = low_back(highest_dot(low(low_rank), w_rate))
    gated_out = low(mixer(carry_on, rate_pre, kq_rows, inner_act, projected[:, channels:], rate_bias, skip_gain))
    branch = low_back(highest_dot(gated_out, w_out))
    return hidden + row_valid[:, None] * branch

def reference(boundary, doc_lengths, norm_gain, in_weight, conv_weight, conv_bias, down_weight, kq_weight, dt_weight, dt_bias, skip_weight, out_weight):
    inputs = boundary[0].astype(jnp.float32).reshape(MB * BATCH, SLOT, D)
    cotangent = boundary[1].astype(jnp.float32).reshape(MB * BATCH, SLOT, D)
    lengths = doc_lengths.reshape(MB * BATCH, DOCS)
    weights = tuple((weight.astype(jnp.float32) for weight in (norm_gain, in_weight, conv_weight, conv_bias, down_weight, kq_weight, dt_weight, dt_bias, skip_weight, out_weight)))

    def forward(slot_inputs, layer_weights):

        def one_slot(pair):
            hidden, slot_lengths = pair
            segment, row_valid, carry_on = doc_layout(slot_lengths)
            first_layer = tuple((weight[0] for weight in layer_weights))
            second_layer = tuple((weight[1] for weight in layer_weights))
            middle = low_back(low(layer(hidden, segment, row_valid, carry_on, first_layer)))
            return layer(middle, segment, row_valid, carry_on, second_layer)
        return lax.map(jax.checkpoint(one_slot), (slot_inputs, lengths))
    outputs, pullback = jax.vjp(forward, inputs, weights)
    grad_inputs, gradients = pullback(cotangent)
    result = jnp.stack([grad_inputs, outputs]).reshape(2, MB, BATCH, SLOT, D)
    return (result, gradients[0], gradients[1], gradients[2], gradients[3], gradients[4], gradients[5], gradients[6], gradients[7], gradients[8], gradients[9])
```

```python
from functools import partial

import jax
import jax.numpy as jnp
from jax import lax
from jax.experimental import pallas as pl
from jax.experimental.pallas import tpu as pltpu
from jax.sharding import PartitionSpec as P

EPSILON = 1e-05
BF = jnp.bfloat16
F32 = jnp.float32
STATE = 16
RANK = 128
LANES = 128
ROWS = 8
MIB = 1024 * 1024


def dot(left, right, left_axis, right_axis, kind=F32):
    return lax.dot_general(
        left, right, (((left_axis,), (right_axis,)), ((), ())), preferred_element_type=kind
    )


def sig(value):
    return 1.0 / (1.0 + jnp.exp(-value))


def swap(value, axis, shift):
    return lax.ppermute(value, axis, [(i, i ^ shift) for i in range(lax.axis_size(axis))])


def peers(value):
    return [swap(value, "grp", d) for d in range(1, lax.axis_size("grp"))]


def call(body, out_shape, **kwargs):
    limit = kwargs.pop("vmem", 48)
    return pl.pallas_call(
        body,
        out_shape=out_shape,
        compiler_params=pltpu.CompilerParams(vmem_limit_bytes=limit * MIB),
        **kwargs,
    )


def shape(dims, kind):
    return jax.ShapeDtypeStruct(dims, kind)


def conv_of(x_ref, pad_ref, mask_ref, vec_ref, cols):
    length = x_ref.shape[0]
    pad_ref[0:ROWS, :] = jnp.zeros((ROWS, LANES), F32)
    pad_ref[ROWS : ROWS + length, :] = x_ref[:, cols]
    total = vec_ref[4:5, cols] + vec_ref[0:1, cols] * x_ref[:, cols]
    shifted = []
    for j in (1, 2, 3):
        earlier = pad_ref[ROWS - j : ROWS - j + length, :] * mask_ref[:, j * LANES : (j + 1) * LANES]
        shifted.append(earlier)
        total = total + vec_ref[j : j + 1, cols] * earlier
    return total, shifted


def conv_fwd_body(x_ref, mask_ref, vec_ref, wdk_ref, inner_ref, part_ref, pad_ref):
    channels = x_ref.shape[1]
    for b in range(channels // LANES):
        cols = slice(b * LANES, (b + 1) * LANES)
        c, _ = conv_of(x_ref, pad_ref, mask_ref, vec_ref, cols)
        inner_ref[:, cols] = (c * sig(c)).astype(BF)
    both = dot(inner_ref[...], wdk_ref[...], 1, 1)
    part_ref[...] = pack(both[:, :RANK], both[:, RANK:])


def pack(low_rank, kq):
    high = kq.astype(BF).astype(F32)
    rest = pltpu.roll(kq - high, 64, axis=1)
    return jnp.concatenate([low_rank, high + rest], axis=1).astype(BF)


def conv_fwd(x, masks, vec, wdk):
    rows, channels = x.shape
    length = 128
    return call(
        conv_fwd_body,
        (shape((rows, channels), BF), shape((rows, 2 * LANES), BF)),
        grid=(rows // length,),
        in_specs=[
            pl.BlockSpec((length, channels), lambda j: (j, 0)),
            pl.BlockSpec((length, 4 * LANES), lambda j: (j, 0)),
            pl.BlockSpec(vec.shape, lambda j: (0, 0)),
            pl.BlockSpec(wdk.shape, lambda j: (0, 0)),
        ],
        out_specs=(
            pl.BlockSpec((length, channels), lambda j: (j, 0)),
            pl.BlockSpec((length, 2 * LANES), lambda j: (j, 0)),
        ),
        scratch_shapes=[pltpu.VMEM((ROWS + length, LANES), F32)],
    )(x, masks, vec, wdk)


def summed_parts(parts, j, length):
    low_rank = jnp.zeros((length, RANK), F32)
    kq = jnp.zeros((length, LANES), F32)
    for d, part in enumerate(parts):
        rows = slice((j ^ d) * length, ((j ^ d) + 1) * length)
        low_rank = low_rank + part[rows, :RANK].astype(F32)
        kq = kq + part[rows, RANK:].astype(F32)
    kq = kq + pltpu.roll(kq, 64, axis=1)
    lane = lax.broadcasted_iota(jnp.int32, (1, LANES), 1)
    return low_rank, jnp.where(lane < 2 * STATE, kq, 0.0)


def rec_body(backward, n_slots, length, width, *refs):
    n_parts = n_slots
    parts, refs = refs[:n_parts], refs[n_parts:]
    if backward:
        (inner, gate, dgated, wdt, vec, mask, gated_out, lr_out, dgate_out, drate_out, dstate_out,
         dpart_out, ddt_out, dvec_out,
         kq_n, kq_i, c_i, lr_n, step_i, p_i, y_i, str_n, hist, dy_i, a_i, b_i, h_scr, dkq_i,
         dlr_n, corr_n) = refs
    else:
        (inner, gate, wdt, vec, mask, gated_out,
         kq_n, kq_i, c_i, lr_n, step_i, p_i, y_i, state) = refs
    nb = width // (2 * LANES)
    first = pl.program_id(0) == 0
    last = pl.program_id(0) == pl.num_programs(0) - 1
    lane = lax.broadcasted_iota(jnp.int32, (1, LANES), 1)
    pieces = [(hh, b, slice((hh * nb + b) * LANES, (hh * nb + b + 1) * LANES)) for hh in (0, 1) for b in range(nb)]

    def rows_of(j):
        return slice(j * length, (j + 1) * length)

    def spread(j, hh):
        return pl.ds(hh * n_slots + j, length, stride=ROWS)

    @pl.when(first)
    def _():
        for j in range(n_slots):
            low_rank, kq = summed_parts(parts, j, length)
            lr_n[rows_of(j), :] = low_rank.astype(BF)
            if backward:
                lr_out[rows_of(j), :] = low_rank.astype(BF)
            kq_n[rows_of(j), :] = kq
            for hh in (0, 1):
                kq_i[spread(j, hh), :] = kq
                c_i[spread(j, hh), :] = mask[rows_of(j), 0:LANES]
        if backward:
            dkq_i[...] = jnp.zeros(dkq_i.shape, F32)
            dlr_n[...] = jnp.zeros(dlr_n.shape, F32)
            corr_n[...] = jnp.zeros(corr_n.shape, F32)

    for j in range(n_slots):
        rows = rows_of(j)
        rate = dot(lr_n[rows, :], wdt[...], 1, 0)
        kq = kq_n[rows, :]
        ks = jnp.sum(jnp.where(lane < STATE, kq * kq, 0.0), axis=1, keepdims=True)
        for hh, b, cols in pieces:
            strength = sig(rate[:, cols] + vec[0:1, cols])
            step = strength / (1.0 + strength * ks)
            step_i[b, spread(j, hh), :] = step
            p_i[b, spread(j, hh), :] = step * inner[rows, cols].astype(F32)
            if backward:
                str_n[rows, cols] = strength
                g = gate[rows, cols]
                dy_i[b, spread(j, hh), :] = dgated[rows, cols] * (g * sig(g))

    def lanes_of(kq, n):
        return jnp.broadcast_to(kq[:, n : n + 1], (ROWS, LANES))

    if backward:
        hist[0] = jnp.zeros(hist.shape[1:], F32)
    else:
        state[...] = jnp.zeros(state.shape, F32)

    def forward_step(t, carry):
        now = pl.ds(pl.multiple_of(t * ROWS, ROWS), ROWS)
        kq, c = kq_i[now, :], c_i[now, :]
        steps = [step_i[b, now, :] for b in range(nb)]
        ps = [p_i[b, now, :] for b in range(nb)]
        ys = [jnp.zeros((ROWS, LANES), F32) for _ in range(nb)]
        for n in range(STATE):
            k, q = lanes_of(kq, n), lanes_of(kq, STATE + n)
            ck2 = c * k * k
            for b in range(nb):
                before = hist[t, n * nb + b] if backward else state[n * nb + b]
                after = (c - ck2 * steps[b]) * before + k * ps[b]
                if backward:
                    hist[t + 1, n * nb + b] = after
                else:
                    state[n * nb + b] = after
                ys[b] = ys[b] + q * after
        for b in range(nb):
            y_i[b, now, :] = ys[b]
        return carry

    lax.fori_loop(0, length, forward_step, 0)

    if not backward:
        for j in range(n_slots):
            rows = rows_of(j)
            for hh, b, cols in pieces:
                y = y_i[b, spread(j, hh), :] + vec[1:2, cols] * inner[rows, cols].astype(F32)
                g = gate[rows, cols]
                gated_out[rows, cols] = (y * (g * sig(g))).astype(BF)
        return

    h_scr[...] = jnp.zeros(h_scr.shape, F32)

    def backward_step(i, carry):
        t = length - 1 - i
        now = pl.ds(pl.multiple_of(t * ROWS, ROWS), ROWS)
        kq, c = kq_i[now, :], c_i[now, :]
        steps = [step_i[b, now, :] for b in range(nb)]
        ps = [p_i[b, now, :] for b in range(nb)]
        dys = [dy_i[b, now, :] for b in range(nb)]
        a_sum = [jnp.zeros((ROWS, LANES), F32) for _ in range(nb)]
        b_sum = [jnp.zeros((ROWS, LANES), F32) for _ in range(nb)]
        out = jnp.zeros((ROWS, LANES), F32)
        for n in range(STATE):
            k, q = lanes_of(kq, n), lanes_of(kq, STATE + n)
            ck = c * k
            ck2 = ck * k
            dk1 = dk2 = dq = None
            for b in range(nb):
                before, after = hist[t, n * nb + b], hist[t + 1, n * nb + b]
                grad = dys[b] * q + h_scr[n * nb + b]
                a_sum[b] = a_sum[b] + grad * k
                both = grad * before
                b_sum[b] = b_sum[b] + ck2 * both
                h_scr[n * nb + b] = (c - ck2 * steps[b]) * grad
                one, two, three = ps[b] * grad, steps[b] * both, dys[b] * after
                dk1 = one if dk1 is None else dk1 + one
                dk2 = two if dk2 is None else dk2 + two
                dq = three if dq is None else dq + three
            dk = dk1 - (2.0 * ck) * dk2
            out = jnp.where(lane == n, jnp.sum(dk, axis=1, keepdims=True), out)
            out = jnp.where(lane == STATE + n, jnp.sum(dq, axis=1, keepdims=True), out)
        for b in range(nb):
            a_i[b, now, :] = a_sum[b]
            b_i[b, now, :] = b_sum[b]
        dkq_i[now, :] = dkq_i[now, :] + out
        return carry

    lax.fori_loop(0, length, backward_step, 0)

    ddt = [jnp.zeros((1, LANES), F32) for _ in pieces]
    dskip = [jnp.zeros((1, LANES), F32) for _ in pieces]
    for j in range(n_slots):
        rows = rows_of(j)
        kq = kq_n[rows, :]
        ks = jnp.sum(jnp.where(lane < STATE, kq * kq, 0.0), axis=1, keepdims=True)
        corr = jnp.zeros((length, 1), F32)
        for i, (hh, b, cols) in enumerate(pieces):
            at = spread(j, hh)
            inn = inner[rows, cols].astype(F32)
            a, step, dy = a_i[b, at, :], step_i[b, at, :], dy_i[b, at, :]
            skip = vec[1:2, cols]
            dstep = inn * a - b_i[b, at, :]
            strength = str_n[rows, cols]
            inv = 1.0 / (1.0 + strength * ks)
            drate = (dstep * (inv * inv) * (strength * (1.0 - strength))).astype(BF)
            drate_out[rows, cols] = drate
            dstate_out[rows, cols] = step * a + skip * dy
            corr = corr + jnp.sum(dstep * (step * step), axis=1, keepdims=True)
            y = y_i[b, at, :] + skip * inn
            g = gate[rows, cols]
            s = sig(g)
            gated_out[rows, cols] = (y * (g * s)).astype(BF)
            dgate_out[rows, cols] = (dgated[rows, cols] * y * (s * (1.0 + g * (1.0 - s)))).astype(BF)
            ddt[i] = ddt[i] + jnp.sum(drate.astype(F32), axis=0, keepdims=True)
            dskip[i] = dskip[i] + jnp.sum(dy * inn, axis=0, keepdims=True)
        corr_n[rows, :] = corr_n[rows, :] + corr
        dlr_n[rows, :] = dlr_n[rows, :] + dot(drate_out[rows, :], wdt[...], 1, 1)
    ddt_out[...] = dot(lr_n[...], drate_out[...], 0, 0)
    dvec_out[...] = jnp.concatenate(
        [jnp.concatenate(ddt, axis=1), jnp.concatenate(dskip, axis=1), jnp.zeros((6, width), F32)], axis=0
    )

    @pl.when(last)
    def _():
        for j in range(n_slots):
            rows = rows_of(j)
            dkq = dkq_i[spread(j, 0), :] + dkq_i[spread(j, 1), :]
            dkq = dkq - jnp.where(lane < STATE, 2.0 * kq_n[rows, :] * corr_n[rows, :], 0.0)
            dpart_out[rows, :] = pack(dlr_n[rows, :], dkq)


def rec(backward, parts, inner, gate, dgated, wdt, vec, masks):
    rows, channels = inner.shape
    n_slots = len(parts)
    length = rows // n_slots
    width = channels // 2
    nb = width // (2 * LANES)

    def whole(a):
        return pl.BlockSpec(a.shape, lambda i: (0,) * a.ndim)

    def block(n):
        return pl.BlockSpec((n, width), lambda i: (0, i))

    wide = pltpu.VMEM((nb, ROWS * length, LANES), F32)
    row = pltpu.VMEM((rows, LANES), F32)
    spread = pltpu.VMEM((ROWS * length, LANES), F32)
    scratch = [row, spread, spread, pltpu.VMEM((rows, RANK), BF), wide, wide, wide]
    if not backward:
        scratch += [pltpu.VMEM((STATE * nb, ROWS, LANES), F32)]
        return call(
            partial(rec_body, False, n_slots, length, width),
            shape((rows, channels), BF),
            grid=(2,),
            in_specs=[whole(p) for p in parts] + [block(rows), block(rows), block(RANK), block(vec.shape[0]), whole(masks)],
            out_specs=block(rows),
            scratch_shapes=scratch,
        )(*parts, inner, gate, wdt, vec, masks)
    scratch += [
        pltpu.VMEM((rows, width), F32),
        pltpu.VMEM((length + 1, STATE * nb, ROWS, LANES), F32),
        wide,
        wide,
        wide,
        pltpu.VMEM((STATE * nb, ROWS, LANES), F32),
        spread,
        pltpu.VMEM((rows, RANK), F32),
        row,
    ]
    lr_like = shape((rows, RANK), BF)
    part_like = shape((rows, 2 * LANES), BF)
    return call(
        partial(rec_body, True, n_slots, length, width),
        (
            shape((rows, channels), BF),
            lr_like,
            shape((rows, channels), BF),
            shape((rows, channels), BF),
            shape((rows, channels), F32),
            part_like,
            shape((RANK, channels), F32),
            shape((ROWS, channels), F32),
        ),
        grid=(2,),
        in_specs=[whole(p) for p in parts]
        + [block(rows), block(rows), block(rows), block(RANK), block(vec.shape[0]), whole(masks)],
        out_specs=(block(rows), whole(lr_like), block(rows), block(rows), block(rows), whole(part_like), block(RANK), block(ROWS)),
        scratch_shapes=scratch,
        vmem=60,
    )(*parts, inner, gate, dgated, wdt, vec, masks)


def conv_bwd_body(n_slots, p0, p1, p2, p3, x_ref, inner, dstate, mask_ref, vec_ref, wdk_ref,
                  dx_out, dsmall_out, dvec_out, pad_ref, late_ref, dcat):
    j = pl.program_id(0)
    length, channels = x_ref.shape
    lane = lax.broadcasted_iota(jnp.int32, (1, LANES), 1)

    @pl.when(j == 0)
    def _():
        dsmall_out[...] = jnp.zeros(dsmall_out.shape, F32)
        dvec_out[...] = jnp.zeros(dvec_out.shape, F32)

    low_rank = jnp.zeros((length, RANK), F32)
    kq = jnp.zeros((length, LANES), F32)
    for d, part in enumerate((p0, p1, p2, p3)):
        rows = pl.ds(pl.multiple_of((j ^ d) * length, length), length)
        low_rank = low_rank + part[rows, :RANK].astype(F32)
        kq = kq + part[rows, RANK:].astype(F32)
    kq = kq + pltpu.roll(kq, 64, axis=1)
    dcat[:, :RANK] = low_rank.astype(BF)
    dcat[:, RANK:] = jnp.where(lane < 2 * STATE, kq, 0.0).astype(BF)
    dsmall_out[...] += dot(dcat[...], inner[...], 0, 0)
    late_ref[length : length + ROWS, :] = jnp.zeros((ROWS, LANES), F32)
    for b in range(channels // LANES):
        cols = slice(b * LANES, (b + 1) * LANES)
        c, earlier = conv_of(x_ref, pad_ref, mask_ref, vec_ref, cols)
        dinner = dstate[:, cols] + dot(dcat[...], wdk_ref[:, cols], 1, 0)
        s = sig(c)
        dc = dinner * (s * (1.0 + c * (1.0 - s)))
        dx = vec_ref[0:1, cols] * dc
        sums = [jnp.sum(dc * x_ref[:, cols], axis=0, keepdims=True)]
        for lag in (1, 2, 3):
            sums.append(jnp.sum(dc * earlier[lag - 1], axis=0, keepdims=True))
            late_ref[0:length, :] = dc * mask_ref[:, lag * LANES : (lag + 1) * LANES]
            dx = dx + vec_ref[lag : lag + 1, cols] * late_ref[lag : lag + length, :]
        sums.append(jnp.sum(dc, axis=0, keepdims=True))
        dx_out[:, cols] = dx.astype(BF)
        for i, value in enumerate(sums):
            dvec_out[i : i + 1, cols] += value


def conv_bwd(parts, x, inner, dstate, masks, vec, wdk):
    rows, channels = x.shape
    n_slots = len(parts)
    length = rows // n_slots

    def whole(a):
        return pl.BlockSpec(a.shape, lambda i: (0,) * a.ndim)

    slot = pl.BlockSpec((length, channels), lambda j: (j, 0))
    small = shape((2 * LANES, channels), F32)
    vecs = shape((ROWS, channels), F32)
    return call(
        partial(conv_bwd_body, n_slots),
        (shape((rows, channels), BF), small, vecs),
        grid=(n_slots,),
        in_specs=[whole(p) for p in parts]
        + [slot, slot, slot, pl.BlockSpec((length, 4 * LANES), lambda j: (j, 0)), whole(vec), whole(wdk)],
        out_specs=(slot, whole(small), whole(vecs)),
        scratch_shapes=[
            pltpu.VMEM((ROWS + length, LANES), F32),
            pltpu.VMEM((ROWS + length, LANES), F32),
            pltpu.VMEM((length, 2 * LANES), BF),
        ],
    )(*parts, x, inner, dstate, masks, vec, wdk)


def norm(hidden, gain):
    rms = lax.rsqrt(jnp.mean(hidden * hidden, axis=1, keepdims=True) + EPSILON)
    return (hidden * rms * gain[None, :]).astype(BF), rms


def norm_back(hidden, rms, gain, dnormed, dout):
    a = hidden * rms
    scaled = dnormed * gain[None, :]
    dh = dout + rms * (scaled - a * jnp.mean(scaled * a, axis=1, keepdims=True))
    return dh, jnp.sum(dnormed * a, axis=0)


def slot_masks(lengths, length):
    ends = jnp.cumsum(lengths, axis=1)
    position = jnp.arange(length, dtype=jnp.int32)
    segment = jnp.sum((position[None, :, None] >= ends[:, None, :]).astype(jnp.int32), axis=2)
    valid = (position[None, :] < ends[:, -1:]).astype(F32)
    same = []
    for lag in (1, 2, 3):
        before = jnp.concatenate([jnp.full((segment.shape[0], lag), -1, jnp.int32), segment[:, :-lag]], axis=1)
        same.append((before == segment).astype(F32))
    stack = jnp.stack([same[0]] + same, axis=2).reshape(-1, 4, 1)
    spread = jnp.broadcast_to(stack, stack.shape[:2] + (LANES,)).reshape(-1, 4 * LANES)
    return spread, valid


def on_device(boundary, doc_lengths, norm_gain, in_weight, conv_weight, conv_bias, down_weight, kq_weight,
              dt_weight, dt_bias, skip_weight, out_weight):
    s = lax.axis_index("section")
    g = lax.axis_index("grp")
    z = lax.axis_index("dp")
    n_grp = lax.axis_size("grp")
    n_dp = lax.axis_size("dp")
    length, width = boundary.shape[3], boundary.shape[4]
    inner = in_weight.shape[2] // 2
    block = inner // n_dp
    sub = block // (2 * n_grp)
    half = sub * n_dp
    mine_first = s == 0

    def pick(first, second):
        return jnp.where(mine_first, first, second)

    small = jnp.concatenate(
        [down_weight[0].T, kq_weight[0], jnp.zeros((2 * LANES - RANK - 2 * STATE, block), BF), dt_weight[0],
         conv_weight[0], conv_bias, dt_bias, skip_weight], axis=0)

    def columns(array, which):
        blocks = array.shape[1] // block
        view = array.reshape(array.shape[0], blocks, n_grp, 2, sub)
        view = lax.dynamic_index_in_dim(view, g, 2, keepdims=False)
        return lax.dynamic_index_in_dim(view, which, 2, keepdims=False).reshape(array.shape[0], blocks * sub)

    def out_rows(which):
        view = out_weight[0].reshape(n_grp, 2, sub, width)
        view = lax.dynamic_index_in_dim(view, g, 0, keepdims=False)
        return lax.dynamic_index_in_dim(view, which, 0, keepdims=False)

    def shards(which):
        w_x = columns(in_weight[0, :, :inner], which)
        w_g = columns(in_weight[0, :, inner:], which)
        return w_x, w_g, columns(small, which), out_rows(which)

    keep, send = shards(s), shards(1 - s)
    come = [swap(piece, "section", 1) for piece in send]
    layers = []
    gains = lax.all_gather(norm_gain[0], "dp", axis=0, tiled=True)
    gains_other = swap(gains, "section", 1)
    for l in (0, 1):
        w_x, w_g, w_s, w_o = [pick(a, b) if l == 0 else pick(b, a) for a, b in zip(keep, come)]
        w_x = lax.all_gather(w_x, "dp", axis=0, tiled=True)
        w_g = lax.all_gather(w_g, "dp", axis=0, tiled=True)
        w_s = lax.all_gather(w_s, "dp", axis=1, tiled=True)
        w_o = lax.all_gather(w_o, "dp", axis=0, tiled=True)
        w_x = jnp.concatenate([w_x, swap(w_x, "section", 1)], axis=1)
        w_g = jnp.concatenate([w_g, swap(w_g, "section", 1)], axis=1)
        w_s = jnp.concatenate([w_s, swap(w_s, "section", 1)], axis=1)
        w_o = jnp.concatenate([w_o, swap(w_o, "section", 1)], axis=0)
        gain = (pick(gains, gains_other) if l == 0 else pick(gains_other, gains)).astype(F32)
        cat = w_s[: 2 * LANES]
        wdt = w_s[2 * LANES : 2 * LANES + RANK]
        tail = w_s[2 * LANES + RANK :].astype(F32)
        conv_vec = jnp.concatenate([tail[:5], jnp.zeros((3, tail.shape[1]), F32)], axis=0)
        rate_vec = jnp.concatenate([tail[5:7], jnp.zeros((6, tail.shape[1]), F32)], axis=0)
        layers.append((gain, w_x, w_g, w_o, cat, wdt, conv_vec, rate_vec))

    rows = boundary[0, :, 0]
    traded = swap(pick(rows[1], rows[0]), "section", 1)
    hidden = pick(rows[0], traded)
    cotangent = pick(traded, rows[1])
    lengths = lax.dynamic_index_in_dim(doc_lengths[:, 0], s, 0, keepdims=True)
    all_lengths = jnp.concatenate([lengths] + peers(lengths), axis=0)
    masks, valid = slot_masks(all_lengths, length)
    valid = valid[0][:, None]

    def group(value):
        return jnp.concatenate([value] + peers(value), axis=0)

    def scatter(value):
        total = value[:length].astype(F32)
        for d in range(1, n_grp):
            total = total + swap(value[d * length : (d + 1) * length], "grp", d).astype(F32)
        return total

    def forward(h, layer):
        gain, w_x, w_g, w_o, cat, wdt, conv_vec, rate_vec = layer
        normed, rms = norm(h, gain)
        normed = group(normed)
        x = dot(normed, w_x, 1, 0)
        gate = dot(normed, w_g, 1, 0)
        act, part = conv_fwd(x, masks, conv_vec, cat)
        return rms, normed, x, gate, act, [part] + peers(part)

    def backward(h, dout, dbranch, layer, saved, dgated, rec_out):
        gain, w_x, w_g, w_o, cat, wdt, conv_vec, rate_vec = layer
        rms, normed, x, gate, act, parts = saved
        gated, lr, dgate, drate, dstate, dpart, ddt, dvec = rec_out
        dx, dsmall, dconv = conv_bwd([dpart] + peers(dpart), x, act, dstate, masks, conv_vec, cat)
        dnormed = (dot(dx, w_x, 1, 1) + dot(dgate, w_g, 1, 1)).astype(BF)
        dnormed = scatter(dnormed)
        dh, dgain = norm_back(h, rms, gain, dnormed, dout)

        def both(left, right, left_own, right_own):
            left_far = swap(left[:, half:] if left_own else left, "section", 1)
            right_far = swap(right[:, half:] if right_own else right, "section", 1)
            left_near = left[:, :half] if left_own else left
            right_near = right[:, :half] if right_own else right
            return (dot(left_near, right_near, 0, 0) + dot(left_far, right_far, 0, 0)).astype(BF)

        grad_x = both(normed, dx, False, True)
        grad_g = both(normed, dgate, False, True)
        grad_o = both(gated, dbranch, True, False)
        grad_s = jnp.concatenate([dsmall, ddt, dconv[:5], dvec[:2], jnp.zeros((1, ddt.shape[1]), F32)], axis=0)
        grad_s = (grad_s[:, :half] + swap(grad_s[:, half:].astype(BF), "section", 1).astype(F32)).astype(BF)
        return dh, dgain, (grad_x, grad_g, grad_o, grad_s)

    h0 = hidden.astype(F32)
    saved0 = forward(h0, layers[0])
    gated0 = rec(False, saved0[5], saved0[4], saved0[3], None, layers[0][5], layers[0][7], masks)
    branch0 = scatter(dot(gated0, layers[0][3], 1, 0, BF))
    h1 = (h0 + valid * branch0).astype(BF).astype(F32)
    saved1 = forward(h1, layers[1])
    dout1 = cotangent.astype(F32)
    dbranch1 = group((valid * dout1).astype(BF))
    dgated1 = dot(dbranch1, layers[1][3], 1, 1)
    rec1 = rec(True, saved1[5], saved1[4], saved1[3], dgated1, layers[1][5], layers[1][7], masks)
    branch1 = scatter(dot(rec1[0], layers[1][3], 1, 0, BF))
    out1 = h1 + valid * branch1
    dh1, dgain1, grads1 = backward(h1, dout1, dbranch1, layers[1], saved1, dgated1, rec1)
    dout0 = dh1.astype(BF).astype(F32)
    dbranch0 = group((valid * dout0).astype(BF))
    dgated0 = dot(dbranch0, layers[0][3], 1, 1)
    rec0 = rec(True, saved0[5], saved0[4], saved0[3], dgated0, layers[0][5], layers[0][7], masks)
    dh0, dgain0, grads0 = backward(h0, dout0, dbranch0, layers[0], saved0, dgated0, rec0)

    far = swap(pick(out1, dh0), "section", 1)
    result = pick(jnp.stack([dh0, far]), jnp.stack([far, out1]))
    result = result.reshape(1, 2, 1, length, width)

    def reduced(grads):
        grad_x, grad_g, grad_o, grad_s = grads
        return (
            lax.psum_scatter(grad_x, "dp", scatter_dimension=0, tiled=True),
            lax.psum_scatter(grad_g, "dp", scatter_dimension=0, tiled=True),
            lax.psum_scatter(grad_o, "dp", scatter_dimension=0, tiled=True),
            lax.psum_scatter(grad_s, "dp", scatter_dimension=1, tiled=True),
        )

    red0, red1 = reduced(grads0), reduced(grads1)
    collected = []
    for first, second in zip(red0, red1):
        near, away = pick(first, second), pick(second, first)
        far = swap(away, "section", 1)
        halves = pick(jnp.stack([near, far]), jnp.stack([far, near]))
        collected.append(lax.all_gather(halves, "grp", axis=0).astype(F32))
    g_x, g_g, g_o, g_s = collected
    rows_in = g_x.shape[2]

    def side(value):
        value = value.reshape(n_grp, 2, rows_in, n_dp, sub)
        return value.transpose(2, 3, 0, 1, 4).reshape(rows_in, inner)

    grad_in = jnp.concatenate([side(g_x), side(g_g)], axis=1)
    grad_out = g_o.reshape(block, width)
    grad_small = g_s.transpose(2, 0, 1, 3).reshape(g_s.shape[2], block)
    gain_sum = lax.psum(jnp.stack([dgain0, dgain1]), ("section", "grp", "dp"))
    gain_sum = lax.dynamic_index_in_dim(gain_sum, s, 0, keepdims=False)
    grad_gain = lax.dynamic_slice_in_dim(gain_sum, z * norm_gain.shape[1], norm_gain.shape[1], 0)
    base = 2 * LANES + RANK
    return (
        result,
        grad_gain[None],
        grad_in[None],
        grad_small[None, base : base + 4],
        grad_small[base + 4][None],
        grad_small[:RANK].T[None],
        grad_small[None, RANK : RANK + 2 * STATE],
        grad_small[None, 2 * LANES : base],
        grad_small[base + 5][None],
        grad_small[base + 6][None],
        grad_out[None],
    )


def solution(mesh):
    return jax.shard_map(
        on_device,
        mesh=mesh,
        in_specs=(
            P("section", None, ("grp", "dp"), None, None),
            P(None, ("grp", "dp"), None),
            P("section", "dp"),
            P("section", "dp", None),
            P("section", None, "dp"),
            P("section", "dp"),
            P("section", "dp", None),
            P("section", None, "dp"),
            P("section", None, "dp"),
            P("section", "dp"),
            P("section", "dp"),
            P("section", "dp", None),
        ),
        out_specs=(
            P("section", None, ("grp", "dp"), None, None),
            P("section", "dp"),
            P("section", "dp", None),
            P("section", None, "dp"),
            P("section", "dp"),
            P("section", "dp", None),
            P("section", None, "dp"),
            P("section", None, "dp"),
            P("section", "dp"),
            P("section", "dp"),
            P("section", "dp", None),
        ),
        check_vma=False,
    )
```

```python
from functools import partial

import jax
import jax.numpy as jnp
from jax import lax
from jax.experimental import pallas as pl
from jax.experimental.pallas import tpu as pltpu
from jax.sharding import PartitionSpec as P

EPSILON = 1e-05
BF = jnp.bfloat16
F32 = jnp.float32
STATE = 16
RANK = 128
LANES = 128
ROWS = 8
MIB = 1024 * 1024


def dot(left, right, left_axis, right_axis, kind=F32):
    return lax.dot_general(
        left, right, (((left_axis,), (right_axis,)), ((), ())), preferred_element_type=kind
    )


def sig(value):
    return 1.0 / (1.0 + jnp.exp(-value))


def swap(value, axis, shift):
    return lax.ppermute(value, axis, [(i, i ^ shift) for i in range(lax.axis_size(axis))])


def directed(value, axis, pairs):
    return lax.ppermute(value, axis, pairs)


def peers(value):
    return [swap(value, "grp", d) for d in range(1, lax.axis_size("grp"))]


def call(body, out_shape, **kwargs):
    limit = kwargs.pop("vmem", 48)
    return pl.pallas_call(
        body,
        out_shape=out_shape,
        compiler_params=pltpu.CompilerParams(vmem_limit_bytes=limit * MIB),
        **kwargs,
    )


def cost(flops):
    return pl.CostEstimate(flops=int(flops), bytes_accessed=0, transcendentals=0)


def shape(dims, kind):
    return jax.ShapeDtypeStruct(dims, kind)


def proj_body(a_ref, near_ref, far_ref, out_ref, *, w_axis):
    @pl.when(pl.program_id(0) == 0)
    def _():
        out_ref[...] = dot(a_ref[...], near_ref[...], 1, w_axis)

    @pl.when(pl.program_id(0) == 1)
    def _():
        out_ref[...] = dot(a_ref[...], far_ref[...], 1, w_axis)


def proj(a, near, far, w_axis):
    rows = a.shape[0]
    half = near.shape[1 - w_axis]

    def whole(v):
        return pl.BlockSpec(v.shape, lambda i: (0,) * v.ndim)

    return call(
        partial(proj_body, w_axis=w_axis),
        shape((rows, 2 * half), F32),
        grid=(2,),
        in_specs=[whole(a), whole(near), whole(far)],
        out_specs=pl.BlockSpec((rows, half), lambda i: (0, i)),
        cost_estimate=cost(4 * rows * half * a.shape[1]),
    )(a, near, far)


def total_body(n, w_axis, *refs):
    lefts, rights, out_ref = refs[:n], refs[n : 2 * n], refs[2 * n]
    total = dot(lefts[0][...], rights[0][...], 1, w_axis)
    for left, right in zip(lefts[1:], rights[1:]):
        total = total + dot(left[...], right[...], 1, w_axis)
    out_ref[...] = total.astype(BF)


def total_of(lefts, rights, w_axis):
    rows = lefts[0].shape[0]
    width = rights[0].shape[1 - w_axis]
    step = 512

    def left_spec(v):
        return pl.BlockSpec(v.shape, lambda i: (0, 0))

    def right_spec(v):
        if w_axis == 0:
            return pl.BlockSpec((v.shape[0], step), lambda i: (0, i))
        return pl.BlockSpec((step, v.shape[1]), lambda i: (i, 0))

    return call(
        partial(total_body, len(lefts), w_axis),
        shape((rows, width), BF),
        grid=(width // step,),
        in_specs=[left_spec(v) for v in lefts] + [right_spec(v) for v in rights],
        out_specs=pl.BlockSpec((rows, step), lambda i: (0, i)),
        cost_estimate=cost(2 * rows * width * sum(v.shape[1] for v in lefts)),
    )(*lefts, *rights)


def conv_of(x_ref, rows, pad_ref, mask_ref, vec_ref, cols):
    length = pad_ref.shape[0] - ROWS
    x = x_ref[rows, cols]
    pad_ref[0:ROWS, :] = jnp.zeros((ROWS, LANES), F32)
    pad_ref[ROWS : ROWS + length, :] = x
    total = vec_ref[4:5, cols] + vec_ref[0:1, cols] * x
    shifted = []
    for j in (1, 2, 3):
        earlier = pad_ref[ROWS - j : ROWS - j + length, :] * mask_ref[rows, j * LANES : (j + 1) * LANES]
        shifted.append(earlier)
        total = total + vec_ref[j : j + 1, cols] * earlier
    return total, shifted


def proj_conv_body(n_slots, a_ref, near_ref, far_ref, mask_ref, vec_ref, cat_ref, x_ref, inner_ref, part_ref,
                   pad_ref, sum_ref):
    i = pl.program_id(0)
    rows_all, half = x_ref.shape
    length = rows_all // n_slots

    @pl.when(i == 0)
    def _():
        x_ref[...] = dot(a_ref[...], near_ref[...], 1, 0)

    @pl.when(i == 1)
    def _():
        x_ref[...] = dot(a_ref[...], far_ref[...], 1, 0)

    for j in range(n_slots):
        rows = slice(j * length, (j + 1) * length)
        for b in range(half // LANES):
            cols = slice(b * LANES, (b + 1) * LANES)
            c, _ = conv_of(x_ref, rows, pad_ref, mask_ref, vec_ref, cols)
            inner_ref[rows, cols] = (c * sig(c)).astype(BF)
    both = dot(inner_ref[...], cat_ref[...], 1, 1)

    @pl.when(i == 0)
    def _():
        sum_ref[...] = both

    @pl.when(i == 1)
    def _():
        total = sum_ref[...] + both
        part_ref[...] = pack(total[:, :RANK], total[:, RANK:])


def proj_conv(n_slots, a, near, far, masks, vec, cat):
    rows = a.shape[0]
    half = near.shape[1]

    def whole(v):
        return pl.BlockSpec(v.shape, lambda i: (0,) * v.ndim)

    def block(n):
        return pl.BlockSpec((n, half), lambda i: (0, i))

    part_like = shape((rows, 2 * LANES), BF)
    return call(
        partial(proj_conv_body, n_slots),
        (shape((rows, 2 * half), F32), shape((rows, 2 * half), BF), part_like),
        grid=(2,),
        in_specs=[whole(a), whole(near), whole(far), whole(masks), block(vec.shape[0]), block(cat.shape[0])],
        out_specs=(block(rows), block(rows), whole(part_like)),
        scratch_shapes=[pltpu.VMEM((ROWS + rows // n_slots, LANES), F32), pltpu.VMEM((rows, 2 * LANES), F32)],
        cost_estimate=cost(4 * rows * half * a.shape[1]),
    )(a, near, far, masks, vec, cat)


def pack(low_rank, kq):
    high = kq.astype(BF).astype(F32)
    rest = pltpu.roll(kq - high, 64, axis=1)
    return jnp.concatenate([low_rank, high + rest], axis=1).astype(BF)


def summed_parts(parts, j, length):
    low_rank = jnp.zeros((length, RANK), F32)
    kq = jnp.zeros((length, LANES), F32)
    for d, part in enumerate(parts):
        rows = slice((j ^ d) * length, ((j ^ d) + 1) * length)
        low_rank = low_rank + part[rows, :RANK].astype(F32)
        kq = kq + part[rows, RANK:].astype(F32)
    kq = kq + pltpu.roll(kq, 64, axis=1)
    lane = lax.broadcasted_iota(jnp.int32, (1, LANES), 1)
    return low_rank, jnp.where(lane < 2 * STATE, kq, 0.0)


def rec_body(backward, n_slots, length, width, *refs):
    n_parts = n_slots
    parts, refs = refs[:n_parts], refs[n_parts:]
    if backward:
        (inner, gate, dgated, wdt, vec, mask, gated_near, gated_far, lr_out, dgate_near, dgate_far,
         dstate_out, dpart_out, ddt_out, dvec_out,
         kq_n, kq_i, c_i, lr_n, step_i, p_i, y_i, kb, str_n, hist, dy_i, a_i, b_i, h_scr, dkq_i,
         dlr_n, corr_n, prod, gated_tmp, dgate_tmp, drate_out) = refs
    else:
        (inner, gate, wdt, vec, mask, gated_out,
         kq_n, kq_i, c_i, lr_n, step_i, p_i, y_i, kb, state) = refs
    nb = width // (2 * LANES)
    first = pl.program_id(0) == 0
    last = pl.program_id(0) == pl.num_programs(0) - 1
    lane = lax.broadcasted_iota(jnp.int32, (1, LANES), 1)
    pieces = [(hh, b, slice((hh * nb + b) * LANES, (hh * nb + b + 1) * LANES)) for hh in (0, 1) for b in range(nb)]

    def rows_of(j):
        return slice(j * length, (j + 1) * length)

    def spread(j, hh):
        return pl.ds(hh * n_slots + j, length, stride=ROWS)

    @pl.when(first)
    def _():
        for j in range(n_slots):
            low_rank, kq = summed_parts(parts, j, length)
            lr_n[rows_of(j), :] = low_rank.astype(BF)
            if backward:
                lr_out[rows_of(j), :] = low_rank.astype(BF)
            kq_n[rows_of(j), :] = kq
            for hh in (0, 1):
                kq_i[spread(j, hh), :] = kq
                c_i[spread(j, hh), :] = mask[rows_of(j), 0:LANES]
        kq = kq_i[...]
        high = kq.astype(BF).astype(F32)
        split = (high + pltpu.roll(kq - high, 64, axis=1)).astype(BF)
        source = lax.broadcasted_iota(jnp.int32, (LANES, 2 * LANES), 0) % 64
        column = lax.broadcasted_iota(jnp.int32, (LANES, 2 * LANES), 1) // LANES
        for n in range(0, 2 * STATE, 2):
            copied = dot(split, jnp.where(source == n + column, 1.0, 0.0).astype(BF), 1, 0)
            kb[n] = copied[:, :LANES]
            kb[n + 1] = copied[:, LANES:]
        if backward:
            dkq_i[...] = jnp.zeros(dkq_i.shape, F32)
            dlr_n[...] = jnp.zeros(dlr_n.shape, F32)
            corr_n[...] = jnp.zeros(corr_n.shape, F32)

    for j in range(n_slots):
        rows = rows_of(j)
        rate = dot(lr_n[rows, :], wdt[...], 1, 0)
        kq = kq_n[rows, :]
        ks = jnp.sum(jnp.where(lane < STATE, kq * kq, 0.0), axis=1, keepdims=True)
        for hh, b, cols in pieces:
            strength = sig(rate[:, cols] + vec[0:1, cols])
            step = strength / (1.0 + strength * ks)
            step_i[b, spread(j, hh), :] = step
            p_i[b, spread(j, hh), :] = step * inner[rows, cols].astype(F32)
            if backward:
                str_n[rows, cols] = strength
                g = gate[rows, cols]
                dy_i[b, spread(j, hh), :] = dgated[rows, cols] * (g * sig(g))

    if backward:
        hist[0] = jnp.zeros(hist.shape[1:], F32)
    else:
        state[...] = jnp.zeros(state.shape, F32)

    def forward_step(t, carry):
        now = pl.ds(pl.multiple_of(t * ROWS, ROWS), ROWS)
        c = c_i[now, :]
        steps = [step_i[b, now, :] for b in range(nb)]
        ps = [p_i[b, now, :] for b in range(nb)]
        ys = [jnp.zeros((ROWS, LANES), F32) for _ in range(nb)]
        for n in range(STATE):
            k, q = kb[n, now, :], kb[STATE + n, now, :]
            ck2 = c * k * k
            for b in range(nb):
                before = hist[t, n * nb + b] if backward else state[n * nb + b]
                after = (c - ck2 * steps[b]) * before + k * ps[b]
                if backward:
                    hist[t + 1, n * nb + b] = after
                else:
                    state[n * nb + b] = after
                ys[b] = ys[b] + q * after
        for b in range(nb):
            y_i[b, now, :] = ys[b]
        return carry

    lax.fori_loop(0, length, forward_step, 0)

    if not backward:
        for j in range(n_slots):
            rows = rows_of(j)
            for hh, b, cols in pieces:
                y = y_i[b, spread(j, hh), :] + vec[1:2, cols] * inner[rows, cols].astype(F32)
                g = gate[rows, cols]
                gated_out[rows, cols] = (y * (g * sig(g))).astype(BF)
        return

    h_scr[...] = jnp.zeros(h_scr.shape, F32)

    def backward_step(start, i, carry):
        t = length - 1 - i
        at = pl.ds(pl.multiple_of((piece - 1 - (i - start)) * 2 * ROWS, 2 * ROWS), 2 * ROWS)
        now = pl.ds(pl.multiple_of(t * ROWS, ROWS), ROWS)
        c = c_i[now, :]
        steps = [step_i[b, now, :] for b in range(nb)]
        ps = [p_i[b, now, :] for b in range(nb)]
        dys = [dy_i[b, now, :] for b in range(nb)]
        a_sum = [jnp.zeros((ROWS, LANES), F32) for _ in range(nb)]
        b_sum = [jnp.zeros((ROWS, LANES), F32) for _ in range(nb)]
        for n in range(STATE):
            k, q = kb[n, now, :], kb[STATE + n, now, :]
            ck = c * k
            ck2 = ck * k
            dk1 = dk2 = dq = None
            for b in range(nb):
                before, after = hist[t, n * nb + b], hist[t + 1, n * nb + b]
                grad = dys[b] * q + h_scr[n * nb + b]
                a_sum[b] = a_sum[b] + grad * k
                both = grad * before
                b_sum[b] = b_sum[b] + ck2 * both
                h_scr[n * nb + b] = (c - ck2 * steps[b]) * grad
                one, two, three = ps[b] * grad, steps[b] * both, dys[b] * after
                dk1 = one if dk1 is None else dk1 + one
                dk2 = two if dk2 is None else dk2 + two
                dq = three if dq is None else dq + three
            dk = dk1 - (2.0 * ck) * dk2
            prod[at, n * LANES : (n + 1) * LANES] = jnp.concatenate([dk, dq], axis=0).astype(BF)
        for b in range(nb):
            a_i[b, now, :] = a_sum[b]
            b_i[b, now, :] = b_sum[b]
        return carry

    piece = prod.shape[0] // (2 * ROWS)
    source = lax.broadcasted_iota(jnp.int32, (STATE * LANES, LANES), 0) // LANES
    sums = jnp.where(source == lax.broadcasted_iota(jnp.int32, (STATE * LANES, LANES), 1), 1.0, 0.0).astype(BF)
    for part in range(length // piece):
        lax.fori_loop(part * piece, (part + 1) * piece, partial(backward_step, part * piece), 0)
        at = pl.ds((length - (part + 1) * piece) * 2 * ROWS, prod.shape[0])
        dkq_i[at, :] = dkq_i[at, :] + dot(prod[...], sums, 1, 0)

    ddt = [jnp.zeros((1, LANES), F32) for _ in pieces]
    dskip = [jnp.zeros((1, LANES), F32) for _ in pieces]
    for j in range(n_slots):
        rows = rows_of(j)
        kq = kq_n[rows, :]
        ks = jnp.sum(jnp.where(lane < STATE, kq * kq, 0.0), axis=1, keepdims=True)
        corr = jnp.zeros((length, 1), F32)
        for i, (hh, b, cols) in enumerate(pieces):
            at = spread(j, hh)
            inn = inner[rows, cols].astype(F32)
            a, step, dy = a_i[b, at, :], step_i[b, at, :], dy_i[b, at, :]
            skip = vec[1:2, cols]
            dstep = inn * a - b_i[b, at, :]
            strength = str_n[rows, cols]
            inv = 1.0 / (1.0 + strength * ks)
            drate = (dstep * (inv * inv) * (strength * (1.0 - strength))).astype(BF)
            drate_out[rows, cols] = drate
            dstate_out[rows, cols] = step * a + skip * dy
            corr = corr + jnp.sum(dstep * (step * step), axis=1, keepdims=True)
            y = y_i[b, at, :] + skip * inn
            g = gate[rows, cols]
            s = sig(g)
            gated_tmp[rows, cols] = (y * (g * s)).astype(BF)
            dgate_tmp[rows, cols] = (dgated[rows, cols] * y * (s * (1.0 + g * (1.0 - s)))).astype(BF)
            ddt[i] = ddt[i] + jnp.sum(drate.astype(F32), axis=0, keepdims=True)
            dskip[i] = dskip[i] + jnp.sum(dy * inn, axis=0, keepdims=True)
        corr_n[rows, :] = corr_n[rows, :] + corr
        dlr_n[rows, :] = dlr_n[rows, :] + dot(drate_out[rows, :], wdt[...], 1, 1)
    ddt_out[...] = dot(lr_n[...], drate_out[...], 0, 0)
    dvec_out[...] = jnp.concatenate(
        [jnp.concatenate(ddt, axis=1), jnp.concatenate(dskip, axis=1), jnp.zeros((6, width), F32)], axis=0
    )

    @pl.when(first)
    def _():
        gated_near[...] = gated_tmp[...]
        dgate_near[...] = dgate_tmp[...]

    @pl.when(last)
    def _():
        gated_far[...] = gated_tmp[...]
        dgate_far[...] = dgate_tmp[...]
        for j in range(n_slots):
            rows = rows_of(j)
            dk, dq = [
                dkq_i[pl.ds(m * ROWS + j, length, stride=2 * ROWS), :]
                + dkq_i[pl.ds(m * ROWS + n_slots + j, length, stride=2 * ROWS), :]
                for m in (0, 1)
            ]
            dkq = dk + pltpu.roll(dq, STATE, axis=1)
            dkq = dkq - jnp.where(lane < STATE, 2.0 * kq_n[rows, :] * corr_n[rows, :], 0.0)
            dpart_out[rows, :] = pack(dlr_n[rows, :], dkq)


def rec(backward, parts, inner, gate, dgated, wdt, vec, masks):
    rows, channels = inner.shape
    n_slots = len(parts)
    length = rows // n_slots
    width = channels // 2
    nb = width // (2 * LANES)

    def whole(a):
        return pl.BlockSpec(a.shape, lambda i: (0,) * a.ndim)

    def block(n):
        return pl.BlockSpec((n, width), lambda i: (0, i))

    wide = pltpu.VMEM((nb, ROWS * length, LANES), F32)
    row = pltpu.VMEM((rows, LANES), F32)
    spread = pltpu.VMEM((ROWS * length, LANES), F32)
    scratch = [row, spread, spread, pltpu.VMEM((rows, RANK), BF), wide, wide, wide]
    scratch += [pltpu.VMEM((2 * STATE, ROWS * length, LANES), F32)]
    if not backward:
        scratch += [pltpu.VMEM((STATE * nb, ROWS, LANES), F32)]
        return call(
            partial(rec_body, False, n_slots, length, width),
            shape((rows, channels), BF),
            grid=(2,),
            in_specs=[whole(p) for p in parts] + [block(rows), block(rows), block(RANK), block(vec.shape[0]), whole(masks)],
            out_specs=block(rows),
            scratch_shapes=scratch,
            cost_estimate=cost(25e9),
        )(*parts, inner, gate, wdt, vec, masks)
    scratch += [
        pltpu.VMEM((rows, width), F32),
        pltpu.VMEM((length + 1, STATE * nb, ROWS, LANES), F32),
        wide,
        wide,
        wide,
        pltpu.VMEM((STATE * nb, ROWS, LANES), F32),
        pltpu.VMEM((2 * ROWS * length, LANES), F32),
        pltpu.VMEM((rows, RANK), F32),
        row,
        pltpu.VMEM((4 * ROWS * ROWS * 2, STATE * LANES), BF),
        pltpu.VMEM((rows, width), BF),
        pltpu.VMEM((rows, width), BF),
        pltpu.VMEM((rows, width), BF),
    ]
    side = shape((rows, width), BF)
    lr_like = shape((rows, RANK), BF)
    part_like = shape((rows, 2 * LANES), BF)
    return call(
        partial(rec_body, True, n_slots, length, width),
        (
            side,
            side,
            lr_like,
            side,
            side,
            shape((rows, channels), F32),
            part_like,
            shape((RANK, channels), F32),
            shape((ROWS, channels), F32),
        ),
        grid=(2,),
        in_specs=[whole(p) for p in parts]
        + [block(rows), block(rows), block(rows), block(RANK), block(vec.shape[0]), whole(masks)],
        out_specs=(whole(side), whole(side), whole(lr_like), whole(side), whole(side), block(rows), whole(part_like), block(RANK), block(ROWS)),
        scratch_shapes=scratch,
        cost_estimate=cost(50e9),
        vmem=62,
    )(*parts, inner, gate, dgated, wdt, vec, masks)


def conv_bwd_body(n_slots, p0, p1, p2, p3, x_ref, inner, dstate, mask_ref, vec_ref, wdk_ref,
                  dx_near, dx_far, dsmall_out, dvec_out, pad_ref, late_ref, dcat):
    j = pl.program_id(0)
    length, channels = x_ref.shape
    lane = lax.broadcasted_iota(jnp.int32, (1, LANES), 1)

    @pl.when(j == 0)
    def _():
        dsmall_out[...] = jnp.zeros(dsmall_out.shape, F32)
        dvec_out[...] = jnp.zeros(dvec_out.shape, F32)

    low_rank = jnp.zeros((length, RANK), F32)
    kq = jnp.zeros((length, LANES), F32)
    for d, part in enumerate((p0, p1, p2, p3)):
        rows = pl.ds(pl.multiple_of((j ^ d) * length, length), length)
        low_rank = low_rank + part[rows, :RANK].astype(F32)
        kq = kq + part[rows, RANK:].astype(F32)
    kq = kq + pltpu.roll(kq, 64, axis=1)
    dcat[:, :RANK] = low_rank.astype(BF)
    dcat[:, RANK:] = jnp.where(lane < 2 * STATE, kq, 0.0).astype(BF)
    dsmall_out[...] += dot(dcat[...], inner[...], 0, 0)
    late_ref[length : length + ROWS, :] = jnp.zeros((ROWS, LANES), F32)
    for b in range(channels // LANES):
        cols = slice(b * LANES, (b + 1) * LANES)
        c, earlier = conv_of(x_ref, slice(0, length), pad_ref, mask_ref, vec_ref, cols)
        dinner = dstate[:, cols] + dot(dcat[...], wdk_ref[:, cols], 1, 0)
        s = sig(c)
        dc = dinner * (s * (1.0 + c * (1.0 - s)))
        dx = vec_ref[0:1, cols] * dc
        sums = [jnp.sum(dc * x_ref[:, cols], axis=0, keepdims=True)]
        for lag in (1, 2, 3):
            sums.append(jnp.sum(dc * earlier[lag - 1], axis=0, keepdims=True))
            late_ref[0:length, :] = dc * mask_ref[:, lag * LANES : (lag + 1) * LANES]
            dx = dx + vec_ref[lag : lag + 1, cols] * late_ref[lag : lag + length, :]
        sums.append(jnp.sum(dc, axis=0, keepdims=True))
        half = channels // 2
        dx_out = dx_near if b * LANES < half else dx_far
        dx_out[:, (b * LANES) % half : (b * LANES) % half + LANES] = dx.astype(BF)
        for i, value in enumerate(sums):
            dvec_out[i : i + 1, cols] += value


def conv_bwd(parts, x, inner, dstate, masks, vec, wdk):
    rows, channels = x.shape
    n_slots = len(parts)
    length = rows // n_slots

    def whole(a):
        return pl.BlockSpec(a.shape, lambda i: (0,) * a.ndim)

    slot = pl.BlockSpec((length, channels), lambda j: (j, 0))
    slot_half = pl.BlockSpec((length, channels // 2), lambda j: (j, 0))
    side = shape((rows, channels // 2), BF)
    small = shape((2 * LANES, channels), F32)
    vecs = shape((ROWS, channels), F32)
    return call(
        partial(conv_bwd_body, n_slots),
        (side, side, small, vecs),
        grid=(n_slots,),
        in_specs=[whole(p) for p in parts]
        + [slot, slot, slot, pl.BlockSpec((length, 4 * LANES), lambda j: (j, 0)), whole(vec), whole(wdk)],
        out_specs=(slot_half, slot_half, whole(small), whole(vecs)),
        scratch_shapes=[
            pltpu.VMEM((ROWS + length, LANES), F32),
            pltpu.VMEM((ROWS + length, LANES), F32),
            pltpu.VMEM((length, 2 * LANES), BF),
        ],
    )(*parts, x, inner, dstate, masks, vec, wdk)


def cut_body(where_ref, w_ref, gain_ref, keep_ref, send_ref):
    half = w_ref.shape[1] // 2
    scaled = w_ref[...].astype(F32) * gain_ref[...]
    first, second = scaled[:, :half].astype(BF), scaled[:, half:].astype(BF)
    mine = where_ref[1] == 0
    keep_ref[...] = jnp.where(mine, first, second)
    send_ref[...] = jnp.where(mine, second, first)


def cut(where, weight, gain, side, n_dp, n_grp, sub):
    rows = weight.shape[0]
    out = shape((rows, n_dp * sub), BF)
    return call(
        cut_body,
        (out, out),
        grid_spec=pltpu.PrefetchScalarGridSpec(
            num_scalar_prefetch=1,
            grid=(n_dp,),
            in_specs=[
                pl.BlockSpec((rows, 2 * sub), lambda i, w: (0, (side * n_dp + i) * n_grp + w[0])),
                pl.BlockSpec((rows, 1), lambda i, w: (0, 0)),
            ],
            out_specs=[pl.BlockSpec((rows, sub), lambda i, w: (0, i))] * 2,
        ),
        cost_estimate=cost(2e9),
    )(where, weight, gain)


def join_body(where_ref, w_ref, gain_ref, *refs):
    parts, out_ref, sum_ref = refs[:-3], refs[-2], refs[-1]
    n = len(parts) // 2
    sub = parts[0].shape[2]
    mine = where_ref[1] == 0

    @pl.when(pl.program_id(0) == 0)
    def _():
        sum_ref[...] = jnp.zeros(sum_ref.shape, F32)

    for d in range(n):
        for h in (0, 1):
            value = jnp.where(mine, parts[d][h], parts[n + d][h]).astype(F32)
            at = pl.ds(pl.multiple_of(((where_ref[0] ^ d) * 2 + h) * sub, sub), sub)
            out_ref[:, at] = value * gain_ref[...]
            sum_ref[...] += value * w_ref[:, at].astype(F32)


def join(where, weight, gain, parts, before, side, n_dp):
    rows = weight.shape[0]
    sub = parts[0].shape[2] // n_dp
    wide = 2 * (len(parts) // 2) * sub
    part = pl.BlockSpec((2, rows, sub), lambda i, w: (0, 0, i))
    return call(
        join_body,
        (shape(weight.shape, F32), shape((rows, sub), F32)),
        grid_spec=pltpu.PrefetchScalarGridSpec(
            num_scalar_prefetch=1,
            grid=(n_dp,),
            in_specs=[
                pl.BlockSpec((rows, wide), lambda i, w: (0, side * n_dp + i)),
                pl.BlockSpec((rows, 1), lambda i, w: (0, 0)),
            ]
            + [part] * len(parts)
            + [pl.BlockSpec(memory_space=pl.ANY)],
            out_specs=[
                pl.BlockSpec((rows, wide), lambda i, w: (0, side * n_dp + i)),
                pl.BlockSpec((rows, sub), lambda i, w: (0, 0)),
            ],
        ),
        input_output_aliases={3 + len(parts): 0} if before.shape == weight.shape else {},
        cost_estimate=cost(5e9),
    )(where, weight, gain, *parts, before)


def join_rows_body(where_ref, *refs):
    parts, out_ref = refs[:-1], refs[-1]
    n = len(parts) // 2
    sub = parts[0].shape[1]
    mine = where_ref[1] == 0
    for d in range(n):
        for h in (0, 1):
            value = jnp.where(mine, parts[d][h], parts[n + d][h]).astype(F32)
            out_ref[pl.ds(pl.multiple_of(((where_ref[0] ^ d) * 2 + h) * sub, sub), sub), :] = value


def join_rows(where, parts, width):
    sub = parts[0].shape[1]
    rows = len(parts) * sub
    step = 512
    return call(
        join_rows_body,
        shape((rows, width), F32),
        grid_spec=pltpu.PrefetchScalarGridSpec(
            num_scalar_prefetch=1,
            grid=(width // step,),
            in_specs=[pl.BlockSpec((2, sub, step), lambda i, w: (0, 0, i))] * len(parts),
            out_specs=pl.BlockSpec((rows, step), lambda i, w: (0, i)),
        ),
        cost_estimate=cost(4e9),
    )(where, *parts)


def rms_of(hidden):
    return lax.rsqrt(jnp.mean(hidden * hidden, axis=1, keepdims=True) + EPSILON)


def slot_masks(lengths, length):
    ends = jnp.cumsum(lengths, axis=1)
    position = jnp.arange(length, dtype=jnp.int32)
    segment = jnp.sum((position[None, :, None] >= ends[:, None, :]).astype(jnp.int32), axis=2)
    valid = (position[None, :] < ends[:, -1:]).astype(F32)
    same = []
    for lag in (1, 2, 3):
        before = jnp.concatenate([jnp.full((segment.shape[0], lag), -1, jnp.int32), segment[:, :-lag]], axis=1)
        same.append((before == segment).astype(F32))
    stack = jnp.stack([same[0]] + same, axis=2).reshape(-1, 4, 1)
    spread = jnp.broadcast_to(stack, stack.shape[:2] + (LANES,)).reshape(-1, 4 * LANES)
    return spread, valid


def gathered(value, axis):
    n_dp = lax.axis_size("dp")
    if n_dp != 4:
        return lax.all_gather(value, "dp", axis=axis, tiled=True)
    z = lax.axis_index("dp")
    left = lax.ppermute(value, "dp", [(i, (i + 1) % 4) for i in range(4)])
    right = lax.ppermute(value, "dp", [(i, (i - 1) % 4) for i in range(4)])
    up = lax.ppermute(left, "dp", [(1, 2), (2, 3)])
    down = lax.ppermute(right, "dp", [(1, 0), (2, 1)])
    across = jnp.where(z < 2, down, up)
    size = value.shape[axis]
    dims = list(value.shape)
    dims[axis] = 4 * size
    out = jnp.zeros(dims, value.dtype)
    for shift, piece in ((0, value), (3, left), (1, right), (2, across)):
        out = lax.dynamic_update_slice_in_dim(out, piece, (z + shift) % 4 * size, axis)
    return out


def on_device(boundary, doc_lengths, norm_gain, in_weight, conv_weight, conv_bias, down_weight, kq_weight,
              dt_weight, dt_bias, skip_weight, out_weight):
    s = lax.axis_index("section")
    g = lax.axis_index("grp")
    n_grp = lax.axis_size("grp")
    n_dp = lax.axis_size("dp")
    length, width = boundary.shape[3], boundary.shape[4]
    inner = in_weight.shape[2] // 2
    block = inner // n_dp
    sub = block // (2 * n_grp)
    half = sub * n_dp
    aligned = sub % LANES == 0
    mine_first = s == 0
    where = jnp.stack([g, s]).astype(jnp.int32)
    gain = norm_gain[0].astype(F32)[:, None]

    def pick(first, second):
        return jnp.where(mine_first, first, second)

    rows = boundary[0, :, 0]
    traded = swap(pick(rows[1], rows[0]), "section", 1)
    hidden = pick(rows[0], traded)
    cotangent = pick(traded, rows[1])
    lengths = lax.dynamic_index_in_dim(doc_lengths[:, 0], s, 0, keepdims=True)
    all_lengths = jnp.concatenate([lengths] + peers(lengths), axis=0)
    masks, valid = slot_masks(all_lengths, length)
    valid = valid[0][:, None]

    def columns(array):
        blocks = array.shape[1] // block
        view = array.reshape(array.shape[0], blocks, n_grp, 2, sub)
        view = lax.dynamic_index_in_dim(view, g, 2, keepdims=False)
        halves = [view[:, :, h].reshape(array.shape[0], blocks * sub) for h in (0, 1)]
        return pick(*halves), pick(halves[1], halves[0])

    def side(which):
        if aligned:
            return cut(where, in_weight[0], gain, which, n_dp, n_grp, sub)
        part = in_weight[0, :, which * inner : (which + 1) * inner]
        return columns((part.astype(F32) * gain).astype(BF))

    def out_side():
        view = lax.dynamic_slice_in_dim(out_weight[0], g * 2 * sub, 2 * sub, 0)
        return pick(view[:sub], view[sub:]), pick(view[sub:], view[:sub])

    def small_side():
        def lanes(array):
            return lax.dynamic_slice_in_dim(array, g * 2 * sub, 2 * sub, 1)

        down = lax.dynamic_slice_in_dim(down_weight[0], g * 2 * sub, 2 * sub, 0).T
        view = jnp.concatenate(
            [down, lanes(kq_weight[0]), jnp.zeros((2 * LANES - RANK - 2 * STATE, 2 * sub), BF), lanes(dt_weight[0]),
             lanes(conv_weight[0]), lanes(conv_bias), lanes(dt_bias), lanes(skip_weight)], axis=0)
        return pick(view[:, :sub], view[:, sub:]), pick(view[:, sub:], view[:, :sub])

    def two_layers(keep, send):
        come = swap(send, "section", 1)
        return pick(keep, come), pick(come, keep)

    x_sides, s_sides = two_layers(*side(0)), two_layers(*small_side())
    g_sides, o_sides = two_layers(*side(1)), two_layers(*out_side())

    def with_far(near):
        return near, swap(near, "section", 1)

    layers = []
    for l in (0, 1):
        w_s = jnp.concatenate(with_far(gathered(s_sides[l], 1)), axis=1)
        w_x = with_far(gathered(x_sides[l], 0))
        w_g = with_far(gathered(g_sides[l], 0))
        w_o = with_far(gathered(o_sides[l], 0))
        cat = w_s[: 2 * LANES]
        wdt = w_s[2 * LANES : 2 * LANES + RANK]
        tail = w_s[2 * LANES + RANK :].astype(F32)
        conv_vec = jnp.concatenate([tail[:5], jnp.zeros((3, tail.shape[1]), F32)], axis=0)
        rate_vec = jnp.concatenate([tail[5:7], jnp.zeros((6, tail.shape[1]), F32)], axis=0)
        layers.append((w_x, w_g, w_o, cat, wdt, conv_vec, rate_vec))

    def group(value):
        return jnp.concatenate([value] + peers(value), axis=0)

    def scatter(value):
        total = value[:length].astype(F32)
        for d in range(1, n_grp):
            total = total + swap(value[d * length : (d + 1) * length], "grp", d).astype(F32)
        return total

    def forward(h, layer):
        w_x, w_g, w_o, cat, wdt, conv_vec, rate_vec = layer
        a = group((h * rms_of(h)).astype(BF))
        x, act, part = proj_conv(n_grp, a, *w_x, masks, conv_vec, cat)
        gate = proj(a, *w_g, 0)
        return a, x, gate, act, [part] + peers(part)

    def backward(h, dout, dbranch, layer, saved, rec_out):
        w_x, w_g, w_o, cat, wdt, conv_vec, rate_vec = layer
        a, x, gate, act, parts = saved
        gated_near, gated_far, lr, dgate_near, dgate_far, dstate, dpart, ddt, dvec = rec_out
        dx_near, dx_far, dsmall, dconv = conv_bwd([dpart] + peers(dpart), x, act, dstate, masks, conv_vec, cat)
        scaled = scatter(total_of([dx_near, dx_far, dgate_near, dgate_far], [*w_x, *w_g], 1))
        rms = rms_of(h)
        own = h * rms
        dh = dout + rms * (scaled - own * jnp.mean(scaled * own, axis=1, keepdims=True))

        a_far, dbranch_far = swap(a, "section", 1), swap(dbranch, "section", 1)
        dgate_come, gated_come = swap(dgate_far, "section", 1), swap(gated_far, "section", 1)
        dx_come = swap(dx_far, "section", 1)

        def both(left, right, left_come, right_come):
            return (dot(left, right, 0, 0) + dot(left_come, right_come, 0, 0)).astype(BF)

        grad_g = both(a, dgate_near, a_far, dgate_come)
        grad_o = both(gated_near, dbranch, gated_come, dbranch_far)
        grad_x = both(a, dx_near, a_far, dx_come)
        grad_s = jnp.concatenate([dsmall, ddt, dconv[:5], dvec[:2], jnp.zeros((1, ddt.shape[1]), F32)], axis=0)
        grad_s = grad_s[:, :half] + swap(grad_s[:, half:].astype(BF), "section", 1).astype(F32)
        grad_o = jnp.concatenate([grad_o, grad_s.T.astype(BF)], axis=1)
        return dh, (grad_g, grad_o, grad_x)

    h0 = hidden.astype(F32)
    saved0 = forward(h0, layers[0])
    gated0 = rec(False, saved0[4], saved0[3], saved0[2], None, layers[0][4], layers[0][6], masks)
    branch0 = scatter(total_of([gated0[:, :half], gated0[:, half:]], layers[0][2], 0))
    h1 = (h0 + valid * branch0).astype(BF).astype(F32)
    saved1 = forward(h1, layers[1])
    dout1 = cotangent.astype(F32)
    dbranch1 = group((valid * dout1).astype(BF))
    dgated1 = proj(dbranch1, *layers[1][2], 1)
    rec1 = rec(True, saved1[4], saved1[3], saved1[2], dgated1, layers[1][4], layers[1][6], masks)
    branch1 = scatter(total_of(rec1[:2], layers[1][2], 0))
    out1 = h1 + valid * branch1
    dh1, grads1 = backward(h1, dout1, dbranch1, layers[1], saved1, rec1)
    dout0 = dh1.astype(BF).astype(F32)
    dbranch0 = group((valid * dout0).astype(BF))
    dgated0 = proj(dbranch0, *layers[0][2], 1)
    rec0 = rec(True, saved0[4], saved0[3], saved0[2], dgated0, layers[0][4], layers[0][6], masks)
    dh0, grads0 = backward(h0, dout0, dbranch0, layers[0], saved0, rec0)

    far = swap(pick(out1, dh0), "section", 1)
    result = pick(jnp.stack([dh0, far]), jnp.stack([far, out1]))
    result = result.reshape(1, 2, 1, length, width)

    def collected(l, grad):
        near = lax.psum_scatter(grad, "dp", scatter_dimension=0, tiled=True)
        far = directed(near, "section", [(1 - l, l)])
        halves = jnp.stack([near, far] if l == 0 else [far, near])
        out = [halves]
        for d in range(1, n_grp):
            pairs = [(l * n_grp + i, l * n_grp + (i ^ d)) for i in range(n_grp)]
            out.append(directed(halves, ("section", "grp"), pairs))
        return out

    (g1, o1, x1), (g0, o0, x0) = [[collected(l, grad) for grad in grads] for l, grads in ((1, grads1), (0, grads0))]

    def in_order(firsts, seconds):
        return jnp.stack([pick(a, b) for a, b in zip(firsts, seconds)])[jnp.arange(n_grp) ^ g]

    smalls = in_order([v[:, :, width:] for v in o0], [v[:, :, width:] for v in o1]).astype(F32)
    grad_small = smalls.transpose(3, 0, 1, 2).reshape(smalls.shape[3], block)
    if aligned:
        grad_in, sum_g = join(where, in_weight[0], gain, g0 + g1, gain, 1, n_dp)
        grad_in, sum_x = join(where, in_weight[0], gain, x0 + x1, grad_in, 0, n_dp)
        grad_gain = jnp.sum(sum_g + sum_x, axis=1)
        grad_out = join_rows(where, o0 + o1, width)
    else:
        sides = []
        for first, second in ((x0, x1), (g0, g1)):
            value = in_order(first, second).reshape(n_grp, 2, -1, n_dp, sub)
            sides.append(value.transpose(2, 3, 0, 1, 4).reshape(value.shape[2], inner))
        product = jnp.concatenate(sides, axis=1).astype(F32)
        grad_in = product * gain
        grad_gain = jnp.sum(product * in_weight[0].astype(F32), axis=1)
        grad_out = in_order([v[:, :, :width] for v in o0], [v[:, :, :width] for v in o1]).astype(F32).reshape(block, width)
    base = 2 * LANES + RANK
    return (
        result,
        grad_gain[None],
        grad_in[None],
        grad_small[None, base : base + 4],
        grad_small[base + 4][None],
        grad_small[:RANK].T[None],
        grad_small[None, RANK : RANK + 2 * STATE],
        grad_small[None, 2 * LANES : base],
        grad_small[base + 5][None],
        grad_small[base + 6][None],
        grad_out[None],
    )


def solution(mesh):
    return jax.shard_map(
        on_device,
        mesh=mesh,
        in_specs=(
            P("section", None, ("grp", "dp"), None, None),
            P(None, ("grp", "dp"), None),
            P("section", "dp"),
            P("section", "dp", None),
            P("section", None, "dp"),
            P("section", "dp"),
            P("section", "dp", None),
            P("section", None, "dp"),
            P("section", None, "dp"),
            P("section", "dp"),
            P("section", "dp"),
            P("section", "dp", None),
        ),
        out_specs=(
            P("section", None, ("grp", "dp"), None, None),
            P("section", "dp"),
            P("section", "dp", None),
            P("section", None, "dp"),
            P("section", "dp"),
            P("section", "dp", None),
            P("section", None, "dp"),
            P("section", None, "dp"),
            P("section", "dp"),
            P("section", "dp"),
            P("section", "dp", None),
        ),
        check_vma=False,
    )
```

```python
from functools import partial

import jax
import jax.numpy as jnp
from jax import lax
from jax.experimental import pallas as pl
from jax.experimental.pallas import tpu as pltpu
from jax.sharding import PartitionSpec as P

EPSILON = 1e-05
BF = jnp.bfloat16
F32 = jnp.float32
STATE = 16
RANK = 128
LANES = 128
ROWS = 8
MIB = 1024 * 1024


def dot(left, right, left_axis, right_axis, kind=F32):
    return lax.dot_general(
        left, right, (((left_axis,), (right_axis,)), ((), ())), preferred_element_type=kind
    )


def sig(value):
    return 1.0 / (1.0 + jnp.exp(-value))


def swap(value, axis, shift):
    return lax.ppermute(value, axis, [(i, i ^ shift) for i in range(lax.axis_size(axis))])


def directed(value, axis, pairs):
    return lax.ppermute(value, axis, pairs)


def peers(value):
    return [swap(value, "grp", d) for d in range(1, lax.axis_size("grp"))]


def call(body, out_shape, **kwargs):
    limit = kwargs.pop("vmem", 48)
    return pl.pallas_call(
        body,
        out_shape=out_shape,
        compiler_params=pltpu.CompilerParams(vmem_limit_bytes=limit * MIB),
        **kwargs,
    )


def cost(flops):
    return pl.CostEstimate(flops=int(3 * flops), bytes_accessed=0, transcendentals=0)


def shape(dims, kind):
    return jax.ShapeDtypeStruct(dims, kind)


def proj_body(a_ref, near_ref, far_ref, out_ref, *, w_axis):
    @pl.when(pl.program_id(0) == 0)
    def _():
        out_ref[...] = dot(a_ref[...], near_ref[...], 1, w_axis)

    @pl.when(pl.program_id(0) == 1)
    def _():
        out_ref[...] = dot(a_ref[...], far_ref[...], 1, w_axis)


def proj(a, near, far, w_axis):
    rows = a.shape[0]
    half = near.shape[1 - w_axis]

    def whole(v):
        return pl.BlockSpec(v.shape, lambda i: (0,) * v.ndim)

    return call(
        partial(proj_body, w_axis=w_axis),
        shape((rows, 2 * half), F32),
        grid=(2,),
        in_specs=[whole(a), whole(near), whole(far)],
        out_specs=pl.BlockSpec((rows, half), lambda i: (0, i)),
        cost_estimate=cost(4 * rows * half * a.shape[1]),
    )(a, near, far)


def total_body(n, w_axis, *refs):
    lefts, rights, out_ref = refs[:n], refs[n : 2 * n], refs[2 * n]
    total = dot(lefts[0][...], rights[0][...], 1, w_axis)
    for left, right in zip(lefts[1:], rights[1:]):
        total = total + dot(left[...], right[...], 1, w_axis)
    out_ref[...] = total.astype(BF)


def total_of(lefts, rights, w_axis):
    rows = lefts[0].shape[0]
    width = rights[0].shape[1 - w_axis]
    step = 512

    def left_spec(v):
        return pl.BlockSpec(v.shape, lambda i: (0, 0))

    def right_spec(v):
        if w_axis == 0:
            return pl.BlockSpec((v.shape[0], step), lambda i: (0, i))
        return pl.BlockSpec((step, v.shape[1]), lambda i: (i, 0))

    return call(
        partial(total_body, len(lefts), w_axis),
        shape((rows, width), BF),
        grid=(width // step,),
        in_specs=[left_spec(v) for v in lefts] + [right_spec(v) for v in rights],
        out_specs=pl.BlockSpec((rows, step), lambda i: (0, i)),
        cost_estimate=cost(2 * rows * width * sum(v.shape[1] for v in lefts)),
    )(*lefts, *rights)


def conv_of(x_ref, rows, pad_ref, mask_ref, vec_ref, cols):
    length = pad_ref.shape[0] - ROWS
    x = x_ref[rows, cols]
    pad_ref[0:ROWS, :] = jnp.zeros((ROWS, LANES), F32)
    pad_ref[ROWS : ROWS + length, :] = x
    total = vec_ref[4:5, cols] + vec_ref[0:1, cols] * x
    shifted = []
    for j in (1, 2, 3):
        earlier = pad_ref[ROWS - j : ROWS - j + length, :] * mask_ref[rows, j * LANES : (j + 1) * LANES]
        shifted.append(earlier)
        total = total + vec_ref[j : j + 1, cols] * earlier
    return total, shifted


def proj_conv_body(n_slots, a_ref, near_ref, far_ref, mask_ref, vec_ref, cat_ref, x_ref, inner_ref, part_ref,
                   pad_ref, sum_ref):
    i = pl.program_id(0)
    rows_all, half = x_ref.shape
    length = rows_all // n_slots

    @pl.when(i == 0)
    def _():
        x_ref[...] = dot(a_ref[...], near_ref[...], 1, 0)

    @pl.when(i == 1)
    def _():
        x_ref[...] = dot(a_ref[...], far_ref[...], 1, 0)

    for j in range(n_slots):
        rows = slice(j * length, (j + 1) * length)
        for b in range(half // LANES):
            cols = slice(b * LANES, (b + 1) * LANES)
            c, _ = conv_of(x_ref, rows, pad_ref, mask_ref, vec_ref, cols)
            inner_ref[rows, cols] = (c * sig(c)).astype(BF)
    both = dot(inner_ref[...], cat_ref[...], 1, 1)

    @pl.when(i == 0)
    def _():
        sum_ref[...] = both

    @pl.when(i == 1)
    def _():
        total = sum_ref[...] + both
        part_ref[...] = pack(total[:, :RANK], total[:, RANK:])


def proj_conv(n_slots, a, near, far, masks, vec, cat):
    rows = a.shape[0]
    half = near.shape[1]

    def whole(v):
        return pl.BlockSpec(v.shape, lambda i: (0,) * v.ndim)

    def block(n):
        return pl.BlockSpec((n, half), lambda i: (0, i))

    part_like = shape((rows, 2 * LANES), BF)
    return call(
        partial(proj_conv_body, n_slots),
        (shape((rows, 2 * half), F32), shape((rows, 2 * half), BF), part_like),
        grid=(2,),
        in_specs=[whole(a), whole(near), whole(far), whole(masks), block(vec.shape[0]), block(cat.shape[0])],
        out_specs=(block(rows), block(rows), whole(part_like)),
        scratch_shapes=[pltpu.VMEM((ROWS + rows // n_slots, LANES), F32), pltpu.VMEM((rows, 2 * LANES), F32)],
        cost_estimate=cost(4 * rows * half * a.shape[1]),
    )(a, near, far, masks, vec, cat)


def pack(low_rank, kq):
    high = kq.astype(BF).astype(F32)
    rest = pltpu.roll(kq - high, 64, axis=1)
    return jnp.concatenate([low_rank, high + rest], axis=1).astype(BF)


def summed_parts(parts, j, length):
    low_rank = jnp.zeros((length, RANK), F32)
    kq = jnp.zeros((length, LANES), F32)
    for d, part in enumerate(parts):
        rows = slice((j ^ d) * length, ((j ^ d) + 1) * length)
        low_rank = low_rank + part[rows, :RANK].astype(F32)
        kq = kq + part[rows, RANK:].astype(F32)
    kq = kq + pltpu.roll(kq, 64, axis=1)
    lane = lax.broadcasted_iota(jnp.int32, (1, LANES), 1)
    return low_rank, jnp.where(lane < 2 * STATE, kq, 0.0)


def rec_body(backward, keep_y, n_slots, length, width, *refs):
    parts, refs = refs[:n_slots], refs[n_slots:]
    y_out = None
    if backward:
        (inner, dy_ref, wdt, vec, mask, lr_out, dstate_out, dpart_out, ddt_out, dvec_out), refs = refs[:10], refs[10:]
        if keep_y:
            y_out, refs = refs[0], refs[1:]
        (kq_n, kq_i, c_i, lr_n, step_i, p_i, y_i, kb, str_n, hist, dy_i, a_i, b_i, h_scr, dkq_i,
         dlr_n, corr_n, prod, drate_n) = refs
    else:
        (inner, wdt, vec, mask, y_out, kq_n, kq_i, c_i, lr_n, step_i, p_i, y_i, kb, state) = refs
    nb = width // (2 * LANES)
    first = pl.program_id(0) == 0
    last = pl.program_id(0) == pl.num_programs(0) - 1
    lane = lax.broadcasted_iota(jnp.int32, (1, LANES), 1)
    pieces = [(hh, b, slice((hh * nb + b) * LANES, (hh * nb + b + 1) * LANES)) for hh in (0, 1) for b in range(nb)]

    def rows_of(j):
        return slice(j * length, (j + 1) * length)

    def spread(j, hh):
        return pl.ds(hh * n_slots + j, length, stride=ROWS)

    @pl.when(first)
    def _():
        for j in range(n_slots):
            low_rank, kq = summed_parts(parts, j, length)
            lr_n[rows_of(j), :] = low_rank.astype(BF)
            if backward:
                lr_out[rows_of(j), :] = low_rank.astype(BF)
            kq_n[rows_of(j), :] = kq
            for hh in (0, 1):
                kq_i[spread(j, hh), :] = kq
                c_i[spread(j, hh), :] = mask[rows_of(j), 0:LANES]
        kq = kq_i[...]
        high = kq.astype(BF).astype(F32)
        split = (high + pltpu.roll(kq - high, 64, axis=1)).astype(BF)
        source = lax.broadcasted_iota(jnp.int32, (LANES, 2 * LANES), 0) % 64
        column = lax.broadcasted_iota(jnp.int32, (LANES, 2 * LANES), 1) // LANES
        for n in range(0, 2 * STATE, 2):
            copied = dot(split, jnp.where(source == n + column, 1.0, 0.0).astype(BF), 1, 0)
            kb[n] = copied[:, :LANES]
            kb[n + 1] = copied[:, LANES:]
        if backward:
            dkq_i[...] = jnp.zeros(dkq_i.shape, F32)
            dlr_n[...] = jnp.zeros(dlr_n.shape, F32)
            corr_n[...] = jnp.zeros(corr_n.shape, F32)

    for j in range(n_slots):
        rows = rows_of(j)
        rate = dot(lr_n[rows, :], wdt[...], 1, 0)
        kq = kq_n[rows, :]
        ks = jnp.sum(jnp.where(lane < STATE, kq * kq, 0.0), axis=1, keepdims=True)
        for hh, b, cols in pieces:
            strength = sig(rate[:, cols] + vec[5:6, cols])
            step = strength / (1.0 + strength * ks)
            step_i[b, spread(j, hh), :] = step
            p_i[b, spread(j, hh), :] = step * inner[rows, cols].astype(F32)
            if backward:
                str_n[rows, cols] = strength
                dy_i[b, spread(j, hh), :] = dy_ref[rows, cols]

    if backward:
        hist[0] = jnp.zeros(hist.shape[1:], F32)
    else:
        state[...] = jnp.zeros(state.shape, F32)

    def forward_step(t, carry):
        now = pl.ds(pl.multiple_of(t * ROWS, ROWS), ROWS)
        c = c_i[now, :]
        steps = [step_i[b, now, :] for b in range(nb)]
        ps = [p_i[b, now, :] for b in range(nb)]
        ys = [jnp.zeros((ROWS, LANES), F32) for _ in range(nb)]
        for n in range(STATE):
            k = kb[n, now, :]
            ck2 = c * k * k
            if y_out is not None:
                q = kb[STATE + n, now, :]
            for b in range(nb):
                before = hist[t, n * nb + b] if backward else state[n * nb + b]
                after = (c - ck2 * steps[b]) * before + k * ps[b]
                if backward:
                    hist[t + 1, n * nb + b] = after
                else:
                    state[n * nb + b] = after
                if y_out is not None:
                    ys[b] = ys[b] + q * after
        if y_out is not None:
            for b in range(nb):
                y_i[b, now, :] = ys[b]
        return carry

    lax.fori_loop(0, length, forward_step, 0)

    if y_out is not None:
        for j in range(n_slots):
            rows = rows_of(j)
            for hh, b, cols in pieces:
                y_out[rows, cols] = y_i[b, spread(j, hh), :] + vec[6:7, cols] * inner[rows, cols].astype(F32)
    if not backward:
        return

    h_scr[...] = jnp.zeros(h_scr.shape, F32)

    def backward_step(start, i, carry):
        t = length - 1 - i
        at = pl.ds(pl.multiple_of((piece - 1 - (i - start)) * 2 * ROWS, 2 * ROWS), 2 * ROWS)
        now = pl.ds(pl.multiple_of(t * ROWS, ROWS), ROWS)
        c = c_i[now, :]
        steps = [step_i[b, now, :] for b in range(nb)]
        ps = [p_i[b, now, :] for b in range(nb)]
        dys = [dy_i[b, now, :] for b in range(nb)]
        a_sum = [jnp.zeros((ROWS, LANES), F32) for _ in range(nb)]
        b_sum = [jnp.zeros((ROWS, LANES), F32) for _ in range(nb)]
        for n in range(STATE):
            k, q = kb[n, now, :], kb[STATE + n, now, :]
            ck = c * k
            ck2 = ck * k
            dk1 = dk2 = dq = None
            for b in range(nb):
                before, after = hist[t, n * nb + b], hist[t + 1, n * nb + b]
                grad = dys[b] * q + h_scr[n * nb + b]
                a_sum[b] = a_sum[b] + grad * k
                both = grad * before
                b_sum[b] = b_sum[b] + ck2 * both
                h_scr[n * nb + b] = (c - ck2 * steps[b]) * grad
                one, two, three = ps[b] * grad, steps[b] * both, dys[b] * after
                dk1 = one if dk1 is None else dk1 + one
                dk2 = two if dk2 is None else dk2 + two
                dq = three if dq is None else dq + three
            dk = dk1 - (2.0 * ck) * dk2
            prod[at, n * LANES : (n + 1) * LANES] = jnp.concatenate([dk, dq], axis=0).astype(BF)
        for b in range(nb):
            a_i[b, now, :] = a_sum[b]
            b_i[b, now, :] = b_sum[b]
        return carry

    piece = prod.shape[0] // (2 * ROWS)
    source = lax.broadcasted_iota(jnp.int32, (STATE * LANES, LANES), 0) // LANES
    sums = jnp.where(source == lax.broadcasted_iota(jnp.int32, (STATE * LANES, LANES), 1), 1.0, 0.0).astype(BF)
    for part in range(length // piece):
        lax.fori_loop(part * piece, (part + 1) * piece, partial(backward_step, part * piece), 0)
        at = pl.ds((length - (part + 1) * piece) * 2 * ROWS, prod.shape[0])
        dkq_i[at, :] = dkq_i[at, :] + dot(prod[...], sums, 1, 0)

    ddt = [jnp.zeros((1, LANES), F32) for _ in pieces]
    dskip = [jnp.zeros((1, LANES), F32) for _ in pieces]
    for j in range(n_slots):
        rows = rows_of(j)
        kq = kq_n[rows, :]
        ks = jnp.sum(jnp.where(lane < STATE, kq * kq, 0.0), axis=1, keepdims=True)
        corr = jnp.zeros((length, 1), F32)
        for i, (hh, b, cols) in enumerate(pieces):
            at = spread(j, hh)
            inn = inner[rows, cols].astype(F32)
            a, step, dy = a_i[b, at, :], step_i[b, at, :], dy_ref[rows, cols]
            dstep = inn * a - b_i[b, at, :]
            strength = str_n[rows, cols]
            inv = 1.0 / (1.0 + strength * ks)
            drate = (dstep * (inv * inv) * (strength * (1.0 - strength))).astype(BF)
            drate_n[rows, cols] = drate
            dstate_out[rows, cols] = step * a + vec[6:7, cols] * dy
            corr = corr + jnp.sum(dstep * (step * step), axis=1, keepdims=True)
            ddt[i] = ddt[i] + jnp.sum(drate.astype(F32), axis=0, keepdims=True)
            dskip[i] = dskip[i] + jnp.sum(dy * inn, axis=0, keepdims=True)
        corr_n[rows, :] = corr_n[rows, :] + corr
        dlr_n[rows, :] = dlr_n[rows, :] + dot(drate_n[rows, :], wdt[...], 1, 1)
    ddt_out[...] = dot(lr_n[...], drate_n[...], 0, 0)
    dvec_out[...] = jnp.concatenate(
        [jnp.concatenate(ddt, axis=1), jnp.concatenate(dskip, axis=1), jnp.zeros((6, width), F32)], axis=0
    )

    @pl.when(last)
    def _():
        for j in range(n_slots):
            rows = rows_of(j)
            dk, dq = [
                dkq_i[pl.ds(m * ROWS + j, length, stride=2 * ROWS), :]
                + dkq_i[pl.ds(m * ROWS + n_slots + j, length, stride=2 * ROWS), :]
                for m in (0, 1)
            ]
            dkq = dk + pltpu.roll(dq, STATE, axis=1)
            dkq = dkq - jnp.where(lane < STATE, 2.0 * kq_n[rows, :] * corr_n[rows, :], 0.0)
            dpart_out[rows, :] = pack(dlr_n[rows, :], dkq)


def rec(parts, inner, dy, wdt, vec, masks, keep_y):
    rows, channels = inner.shape
    n_slots = len(parts)
    length = rows // n_slots
    width = channels // 2
    nb = width // (2 * LANES)

    def whole(a):
        return pl.BlockSpec(a.shape, lambda i: (0,) * a.ndim)

    def block(n):
        return pl.BlockSpec((n, width), lambda i: (0, i))

    wide = pltpu.VMEM((nb, ROWS * length, LANES), F32)
    row = pltpu.VMEM((rows, LANES), F32)
    spread = pltpu.VMEM((ROWS * length, LANES), F32)
    y_like = shape((rows, channels), F32)
    scratch = [row, spread, spread, pltpu.VMEM((rows, RANK), BF), wide, wide, wide]
    scratch += [pltpu.VMEM((2 * STATE, ROWS * length, LANES), F32)]
    if dy is None:
        scratch += [pltpu.VMEM((STATE * nb, ROWS, LANES), F32)]
        return call(
            partial(rec_body, False, True, n_slots, length, width),
            y_like,
            grid=(2,),
            in_specs=[whole(p) for p in parts] + [block(rows), block(RANK), block(vec.shape[0]), whole(masks)],
            out_specs=block(rows),
            scratch_shapes=scratch,
            cost_estimate=cost(20e9),
        )(*parts, inner, wdt, vec, masks)
    scratch += [
        pltpu.VMEM((rows, width), F32),
        pltpu.VMEM((length + 1, STATE * nb, ROWS, LANES), F32),
        wide,
        wide,
        wide,
        pltpu.VMEM((STATE * nb, ROWS, LANES), F32),
        pltpu.VMEM((2 * ROWS * length, LANES), F32),
        pltpu.VMEM((rows, RANK), F32),
        row,
        pltpu.VMEM((4 * ROWS * ROWS * 2, STATE * LANES), BF),
        pltpu.VMEM((rows, width), BF),
    ]
    lr_like = shape((rows, RANK), BF)
    part_like = shape((rows, 2 * LANES), BF)
    outs = [lr_like, y_like, part_like, shape((RANK, channels), F32), shape((ROWS, channels), F32)]
    specs = [whole(lr_like), block(rows), whole(part_like), block(RANK), block(ROWS)]
    if keep_y:
        outs, specs = outs + [y_like], specs + [block(rows)]
    return call(
        partial(rec_body, True, keep_y, n_slots, length, width),
        tuple(outs),
        grid=(2,),
        in_specs=[whole(p) for p in parts] + [block(rows), block(rows), block(RANK), block(vec.shape[0]), whole(masks)],
        out_specs=tuple(specs),
        scratch_shapes=scratch,
        cost_estimate=cost(55e9),
        vmem=62,
    )(*parts, inner, dy, wdt, vec, masks)


def gate_values(y, gate):
    s = sig(gate)
    return y * (gate * s), y * (s * (1.0 + gate * (1.0 - s)))


def gate_back_body(y_ref, gate_ref, dgated_ref, gated_near, gated_far, dgate_near, dgate_far):
    half = gated_near.shape[1]
    for h, (gated, dgate) in enumerate([(gated_near, dgate_near), (gated_far, dgate_far)]):
        for b in range(half // LANES):
            cols = slice(b * LANES, (b + 1) * LANES)
            at = slice(h * half + b * LANES, h * half + (b + 1) * LANES)
            one, two = gate_values(y_ref[:, at], gate_ref[:, at])
            gated[:, cols] = one.astype(BF)
            dgate[:, cols] = (dgated_ref[:, at] * two).astype(BF)


def gate_back(n_slots, y, gate, dgated):
    rows, channels = y.shape
    length = rows // n_slots
    side = shape((rows, channels // 2), BF)
    return call(
        gate_back_body,
        (side,) * 4,
        grid=(n_slots,),
        in_specs=[pl.BlockSpec((length, channels), lambda j: (j, 0))] * 3,
        out_specs=[pl.BlockSpec((length, channels // 2), lambda j: (j, 0))] * 4,
        cost_estimate=cost(3e9),
    )(y, gate, dgated)


def conv_bwd_body(n_slots, p0, p1, p2, p3, x_ref, inner, dstate, mask_ref, vec_ref, wdk_ref,
                  dx_near, dx_far, dsmall_out, dvec_out, pad_ref, late_ref, dcat):
    j = pl.program_id(0)
    length, channels = x_ref.shape
    lane = lax.broadcasted_iota(jnp.int32, (1, LANES), 1)

    @pl.when(j == 0)
    def _():
        dsmall_out[...] = jnp.zeros(dsmall_out.shape, F32)
        dvec_out[...] = jnp.zeros(dvec_out.shape, F32)

    low_rank = jnp.zeros((length, RANK), F32)
    kq = jnp.zeros((length, LANES), F32)
    for d, part in enumerate((p0, p1, p2, p3)):
        rows = pl.ds(pl.multiple_of((j ^ d) * length, length), length)
        low_rank = low_rank + part[rows, :RANK].astype(F32)
        kq = kq + part[rows, RANK:].astype(F32)
    kq = kq + pltpu.roll(kq, 64, axis=1)
    dcat[:, :RANK] = low_rank.astype(BF)
    dcat[:, RANK:] = jnp.where(lane < 2 * STATE, kq, 0.0).astype(BF)
    dsmall_out[...] += dot(dcat[...], inner[...], 0, 0)
    late_ref[length : length + ROWS, :] = jnp.zeros((ROWS, LANES), F32)
    for b in range(channels // LANES):
        cols = slice(b * LANES, (b + 1) * LANES)
        c, earlier = conv_of(x_ref, slice(0, length), pad_ref, mask_ref, vec_ref, cols)
        dinner = dstate[:, cols] + dot(dcat[...], wdk_ref[:, cols], 1, 0)
        s = sig(c)
        dc = dinner * (s * (1.0 + c * (1.0 - s)))
        dx = vec_ref[0:1, cols] * dc
        sums = [jnp.sum(dc * x_ref[:, cols], axis=0, keepdims=True)]
        for lag in (1, 2, 3):
            sums.append(jnp.sum(dc * earlier[lag - 1], axis=0, keepdims=True))
            late_ref[0:length, :] = dc * mask_ref[:, lag * LANES : (lag + 1) * LANES]
            dx = dx + vec_ref[lag : lag + 1, cols] * late_ref[lag : lag + length, :]
        sums.append(jnp.sum(dc, axis=0, keepdims=True))
        half = channels // 2
        dx_out = dx_near if b * LANES < half else dx_far
        dx_out[:, (b * LANES) % half : (b * LANES) % half + LANES] = dx.astype(BF)
        for i, value in enumerate(sums):
            dvec_out[i : i + 1, cols] += value


def conv_bwd(parts, x, inner, dstate, masks, vec, wdk):
    rows, channels = x.shape
    n_slots = len(parts)
    length = rows // n_slots

    def whole(a):
        return pl.BlockSpec(a.shape, lambda i: (0,) * a.ndim)

    slot = pl.BlockSpec((length, channels), lambda j: (j, 0))
    slot_half = pl.BlockSpec((length, channels // 2), lambda j: (j, 0))
    side = shape((rows, channels // 2), BF)
    small = shape((2 * LANES, channels), F32)
    vecs = shape((ROWS, channels), F32)
    return call(
        partial(conv_bwd_body, n_slots),
        (side, side, small, vecs),
        grid=(n_slots,),
        in_specs=[whole(p) for p in parts]
        + [slot, slot, slot, pl.BlockSpec((length, 4 * LANES), lambda j: (j, 0)), whole(vec), whole(wdk)],
        out_specs=(slot_half, slot_half, whole(small), whole(vecs)),
        scratch_shapes=[
            pltpu.VMEM((ROWS + length, LANES), F32),
            pltpu.VMEM((ROWS + length, LANES), F32),
            pltpu.VMEM((length, 2 * LANES), BF),
        ],
    )(*parts, x, inner, dstate, masks, vec, wdk)


SMALL = 448
DOWN, KQ, DT, VEC = 0, 128, 160, 288


def cut_small_body(where_ref, w_ref, gain_ref, *refs):
    sources, (keep_ref, send_ref, small), fetched, sems = refs[:7], refs[7:10], refs[10:17], refs[17]
    i = pl.program_id(0)
    rows, sub = w_ref.shape[0], keep_ref.shape[1]
    part = keep_ref.shape[0] - rows
    copies = [pltpu.make_async_copy(v, f, sems.at[n]) for n, (v, f) in enumerate(zip(sources, fetched))]

    @pl.when(i == 0)
    def _():
        for copy in copies:
            copy.start()

    mine = where_ref[1] == 0
    scaled = w_ref[...].astype(F32) * gain_ref[...]
    first, second = scaled[:, :sub].astype(BF), scaled[:, sub:].astype(BF)
    keep_ref[0:rows, :] = jnp.where(mine, first, second)
    send_ref[0:rows, :] = jnp.where(mine, second, first)

    @pl.when(i == 0)
    def _():
        for copy in copies:
            copy.wait()
        down, kq, dt, conv, conv_bias, dt_bias, skip = fetched
        at = pl.ds(pl.multiple_of(where_ref[0] * 2 * sub, 2 * sub), 2 * sub)
        small[DOWN:KQ, :] = down[at, :].astype(F32).T.astype(BF)
        small[KQ:DT, :] = kq[:, at]
        small[DT:VEC, :] = dt[:, at]
        last = [v[:, at].astype(F32) for v in (conv, conv_bias, dt_bias, skip)] + [jnp.zeros((9, 2 * sub), F32)]
        small[VEC : VEC + 16, :] = jnp.concatenate(last, axis=0).astype(BF)
        small[VEC + 16 :, :] = jnp.zeros((SMALL - VEC - 16, 2 * sub), BF)

    piece = small[pl.ds(pl.multiple_of(i * part, 16), part), :]
    first, second = piece[:, :sub], piece[:, sub:]
    keep_ref[rows:, :] = jnp.where(mine, first, second)
    send_ref[rows:, :] = jnp.where(mine, second, first)


def cut_small(where, weight, gain, down, kq, dt, conv, conv_bias, dt_bias, skip, n_dp, n_grp, sub):
    rows = weight.shape[0]
    part = SMALL // n_dp
    out = shape((rows + part, n_dp * sub), BF)
    smalls = [down, kq, dt, conv, conv_bias, dt_bias, skip]
    return call(
        cut_small_body,
        (out, out),
        grid_spec=pltpu.PrefetchScalarGridSpec(
            num_scalar_prefetch=1,
            grid=(n_dp,),
            in_specs=[
                pl.BlockSpec((rows, 2 * sub), lambda i, w: (0, i * n_grp + w[0])),
                pl.BlockSpec((rows, 1), lambda i, w: (0, 0)),
            ]
            + [pl.BlockSpec(memory_space=pltpu.HBM)] * 7,
            out_specs=[pl.BlockSpec((rows + part, sub), lambda i, w: (0, i))] * 2,
            scratch_shapes=[pltpu.VMEM((SMALL, 2 * sub), BF)]
            + [pltpu.VMEM(v.shape, BF) for v in smalls]
            + [pltpu.SemaphoreType.DMA((7,))],
        ),
        cost_estimate=cost(3e9),
    )(where, weight, gain, *smalls)


def cut_out_body(where_ref, w_ref, gain_ref, o_ref, keep_ref, send_ref):
    i = pl.program_id(0)
    rows, sub = w_ref.shape[0], keep_ref.shape[1]
    mine = where_ref[1] == 0
    scaled = w_ref[...].astype(F32) * gain_ref[...]
    first, second = scaled[:, :sub].astype(BF), scaled[:, sub:].astype(BF)
    keep_ref[0:rows, :] = jnp.where(mine, first, second)
    send_ref[0:rows, :] = jnp.where(mine, second, first)
    n = pl.num_programs(0)
    wide = o_ref.shape[1] // 4
    for c in range(4):
        lanes = pl.ds(pl.multiple_of(c * wide + i * sub, sub), sub)
        first, second = o_ref[0:sub, lanes], o_ref[sub:, lanes]
        at = slice(rows + c * sub, rows + (c + 1) * sub)
        keep_ref[at, :] = jnp.where(mine, first, second)
        send_ref[at, :] = jnp.where(mine, second, first)


def cut_out(where, weight, gain, out_weight, n_dp, n_grp, sub):
    rows = weight.shape[0]
    out = shape((rows + 4 * sub, n_dp * sub), BF)
    return call(
        cut_out_body,
        (out, out),
        grid_spec=pltpu.PrefetchScalarGridSpec(
            num_scalar_prefetch=1,
            grid=(n_dp,),
            in_specs=[
                pl.BlockSpec((rows, 2 * sub), lambda i, w: (0, (n_dp + i) * n_grp + w[0])),
                pl.BlockSpec((rows, 1), lambda i, w: (0, 0)),
                pl.BlockSpec((2 * sub, out_weight.shape[1]), lambda i, w: (w[0], 0)),
            ],
            out_specs=[pl.BlockSpec((rows + 4 * sub, sub), lambda i, w: (0, i))] * 2,
        ),
        cost_estimate=cost(3e9),
    )(where, weight, gain, out_weight)


def flat_call(body, out_shape, arrays, specs=None, scratch=(), flops=0, vmem=48):
    def whole(v):
        return pl.BlockSpec(v.shape, lambda i: (0,) * len(v.shape))

    outs = out_shape if isinstance(out_shape, tuple) else (out_shape,)
    out_specs = tuple(whole(v) for v in outs)
    return call(
        body,
        out_shape,
        grid=(1,),
        in_specs=[(specs or {}).get(n, whole(v)) for n, v in enumerate(arrays)],
        out_specs=out_specs if isinstance(out_shape, tuple) else out_specs[0],
        scratch_shapes=list(scratch),
        cost_estimate=cost(flops),
        vmem=vmem,
    )(*arrays)


def q_block(q, which, rows):
    return pl.BlockSpec((q.shape[0], rows, q.shape[2]), lambda i: (0, which, 0))


def blocks_sum(a_ref, w_ref, rows):
    total = None
    for p in range(w_ref.shape[0]):
        term = dot(a_ref[:, p * rows : (p + 1) * rows], w_ref[p, 0:rows, :], 1, 0)
        total = term if total is None else total + term
    return total


def first_body(n_slots, rows, a_ref, mask_ref, near_ref, far_ref, *refs):
    x_ref, inner_ref, part_ref, cat_ref, wdt_ref, vec_ref, pad_ref, small = refs
    half = x_ref.shape[1] // 2
    n_dp = near_ref.shape[0]
    sub = half // n_dp
    length = x_ref.shape[0] // n_slots
    part = SMALL // n_dp
    for h, w_ref in enumerate((near_ref, far_ref)):
        for p in range(n_dp):
            lanes = slice(h * half + p * sub, h * half + (p + 1) * sub)
            for i in range(n_dp):
                small[i * part : (i + 1) * part, lanes] = w_ref[p, rows:, i * sub : (i + 1) * sub]
    cat_ref[0:DT, :] = small[0:DT, :]
    cat_ref[DT:, :] = jnp.zeros((cat_ref.shape[0] - DT, 2 * half), BF)
    wdt_ref[...] = small[DT:VEC, :]
    vec_ref[...] = small[VEC : VEC + 16, :].astype(F32)
    both = jnp.zeros((x_ref.shape[0], 2 * LANES), F32)
    for h, w_ref in enumerate((near_ref, far_ref)):
        lanes = slice(h * half, (h + 1) * half)
        x_ref[:, lanes] = blocks_sum(a_ref, w_ref, rows)
        for j in range(n_slots):
            at = slice(j * length, (j + 1) * length)
            for b in range(half // LANES):
                cols = slice(h * half + b * LANES, h * half + (b + 1) * LANES)
                c, _ = conv_of(x_ref, at, pad_ref, mask_ref, vec_ref, cols)
                inner_ref[at, cols] = (c * sig(c)).astype(BF)
        both = both + dot(inner_ref[:, lanes], cat_ref[:, lanes], 1, 1)
    part_ref[...] = pack(both[:, :RANK], both[:, RANK:])


def first_products(n_slots, a, masks, near, far, rows):
    n, half = a.shape[0], near.shape[2]
    return flat_call(
        partial(first_body, n_slots, rows),
        (
            shape((n, 2 * half), F32),
            shape((n, 2 * half), BF),
            shape((n, 2 * LANES), BF),
            shape((2 * LANES, 2 * half), BF),
            shape((RANK, 2 * half), BF),
            shape((16, 2 * half), F32),
        ),
        [a, masks, near, far],
        scratch=[pltpu.VMEM((ROWS + n // n_slots, LANES), F32), pltpu.VMEM((SMALL, 2 * half), BF)],
        flops=8e9,
    )


def gate_body(rows, a_ref, y_ref, near_ref, far_ref, gate_ref, gated_near, gated_far):
    half = gated_near.shape[1]
    for h, (w_ref, gated) in enumerate([(near_ref, gated_near), (far_ref, gated_far)]):
        at = slice(h * half, (h + 1) * half)
        gate = blocks_sum(a_ref, w_ref, rows)
        gate_ref[:, at] = gate
        gated[...] = (y_ref[:, at] * (gate * sig(gate))).astype(BF)


def gate_product(a, y, near, far, rows):
    half = near.shape[2]
    side = shape((a.shape[0], half), BF)
    return flat_call(
        partial(gate_body, rows),
        (shape(y.shape, F32), side, side),
        [a, y, near, far],
        specs={2: q_block(near, 0, rows), 3: q_block(far, 0, rows)},
        flops=6e9,
    )


def out_weight_of(near_ref, far_ref, w_scr):
    half = w_scr.shape[0] // 2
    n_dp = near_ref.shape[0]
    sub = half // n_dp
    wide = w_scr.shape[1] // 4
    for h, w_ref in enumerate((near_ref, far_ref)):
        for p in range(n_dp):
            for c in range(4):
                block = w_ref[p, c * sub : (c + 1) * sub, :]
                w_scr[h * half + p * sub : h * half + (p + 1) * sub, c * wide : (c + 1) * wide] = block


def branch_body(left_near, left_far, near_ref, far_ref, out_ref, w_scr):
    out_weight_of(near_ref, far_ref, w_scr)
    half = left_near.shape[1]
    wide = w_scr.shape[1] // 4
    for c in range(4):
        lanes = slice(c * wide, (c + 1) * wide)
        total = dot(left_near[...], w_scr[:half, lanes], 1, 0) + dot(left_far[...], w_scr[half:, lanes], 1, 0)
        out_ref[:, lanes] = total.astype(BF)


def branch_product(left_near, left_far, near, far, rows):
    half = near.shape[2]
    return flat_call(
        branch_body,
        shape((left_near.shape[0], 4 * half), BF),
        [left_near, left_far, near, far],
        specs={2: q_block(near, 1, rows), 3: q_block(far, 1, rows)},
        scratch=[pltpu.VMEM((2 * half, 4 * half), BF)],
        flops=5e9,
    )


def dgated_body(d_ref, y_ref, gate_ref, near_ref, far_ref, dy_ref, dgate_near, dgate_far, w_scr):
    out_weight_of(near_ref, far_ref, w_scr)
    half = dgate_near.shape[1]
    for h, dgate in enumerate((dgate_near, dgate_far)):
        at = slice(h * half, (h + 1) * half)
        dgated = dot(d_ref[...], w_scr[at, :], 1, 1)
        gate = gate_ref[:, at]
        dy_ref[:, at] = dgated * (gate * sig(gate))
        dgate[...] = (dgated * gate_values(y_ref[:, at], gate)[1]).astype(BF)


def dgated_product(dbranch, y, gate, near, far, rows):
    half = near.shape[2]
    side = shape((dbranch.shape[0], half), BF)
    return flat_call(
        dgated_body,
        (shape(y.shape, F32), side, side),
        [dbranch, y, gate, near, far],
        specs={3: q_block(near, 1, rows), 4: q_block(far, 1, rows)},
        scratch=[pltpu.VMEM((2 * half, dbranch.shape[1]), BF)],
        flops=6e9,
    )


def dnormed_body(rows, dx_near, dx_far, dg_near, dg_far, p_near, p_far, q_near, q_far, out_ref):
    for p in range(p_near.shape[0]):
        total = dot(dx_near[...], p_near[p, 0:rows, :], 1, 1) + dot(dx_far[...], p_far[p, 0:rows, :], 1, 1)
        total = total + dot(dg_near[...], q_near[p], 1, 1) + dot(dg_far[...], q_far[p], 1, 1)
        out_ref[:, p * rows : (p + 1) * rows] = total.astype(BF)


def dnormed_product(lefts, p_near, p_far, q_near, q_far, rows):
    n_dp = p_near.shape[0]
    return flat_call(
        partial(dnormed_body, rows),
        shape((lefts[0].shape[0], n_dp * rows), BF),
        [*lefts, p_near, p_far, q_near, q_far],
        specs={6: q_block(q_near, 0, rows), 7: q_block(q_far, 0, rows)},
        flops=8e9,
    )


def grad_p_body(a_ref, a_far, dx_ref, dx_come, small_ref, small_come, out_ref):
    rows = a_ref.shape[1]
    value = dot(a_ref[...], dx_ref[...], 0, 0) + dot(a_far[...], dx_come[...], 0, 0)
    out_ref[0, 0:rows, :] = value.astype(BF)
    out_ref[0, rows:, :] = (small_ref[...] + small_come[...].astype(F32)).astype(BF)


def grad_p(a, a_far, dx, dx_come, small, small_come, n_dp):
    rows = a.shape[1] // n_dp
    part = small.shape[0] // n_dp
    half = dx.shape[1]
    col = pl.BlockSpec((a.shape[0], rows), lambda i: (0, i))
    whole = pl.BlockSpec(dx.shape, lambda i: (0, 0))
    block = pl.BlockSpec((part, half), lambda i: (i, 0))
    return call(
        grad_p_body,
        shape((n_dp, rows + part, half), BF),
        grid=(n_dp,),
        in_specs=[col, col, whole, whole, block, block],
        out_specs=pl.BlockSpec((1, rows + part, half), lambda i: (i, 0, 0)),
        cost_estimate=cost(5e9),
    )(a, a_far, dx, dx_come, small, small_come)


def grad_q_body(a_ref, a_far, dg_ref, dg_come, gated_ref, gated_come, db_ref, db_far, out_ref):
    rows = a_ref.shape[1]
    sub = gated_ref.shape[1]
    wide = db_ref.shape[1] // 4
    value = dot(a_ref[...], dg_ref[...], 0, 0) + dot(a_far[...], dg_come[...], 0, 0)
    out_ref[0, 0:rows, :] = value.astype(BF)
    value = dot(gated_ref[...], db_ref[...], 0, 0) + dot(gated_come[...], db_far[...], 0, 0)
    for c in range(4):
        out_ref[0, rows + c * sub : rows + (c + 1) * sub, :] = value[:, c * wide : (c + 1) * wide].astype(BF)


def grad_q(a, a_far, dg, dg_come, gated, gated_come, db, db_far, n_dp):
    rows = a.shape[1] // n_dp
    half = dg.shape[1]
    sub = half // n_dp
    col = pl.BlockSpec((a.shape[0], rows), lambda i: (0, i))
    sub_col = pl.BlockSpec((a.shape[0], sub), lambda i: (0, i))

    def whole(v):
        return pl.BlockSpec(v.shape, lambda i: (0, 0))

    return call(
        grad_q_body,
        shape((n_dp, rows + 4 * sub, half), BF),
        grid=(n_dp,),
        in_specs=[col, col, whole(dg), whole(dg), sub_col, sub_col, whole(db), whole(db)],
        out_specs=pl.BlockSpec((1, rows + 4 * sub, half), lambda i: (i, 0, 0)),
        cost_estimate=cost(8e9),
    )(a, a_far, dg, dg_come, gated, gated_come, db, db_far)


def small_grads_body(dsmall, ddt, dconv, dvec, near_ref, far_ref, scr):
    half = near_ref.shape[1]
    sub = half // 4
    part = SMALL // 4
    scr[DOWN:DT, :] = dsmall[0:DT, :]
    scr[DT:VEC, :] = ddt[...]
    rows = [dconv[0:5, :], dvec[0:2, :], jnp.zeros((1, 2 * half), F32)]
    scr[VEC : VEC + 8, :] = jnp.concatenate(rows, axis=0)
    scr[VEC + 8 :, :] = jnp.zeros((SMALL - VEC - 8, 2 * half), F32)
    for block in range(4):
        at = slice(block * part, (block + 1) * part)
        for i in range(4):
            rows = slice(i * part, (i + 1) * part)
            lanes = slice(i * sub, (i + 1) * sub)
            near_ref[at, lanes] = scr[rows, block * sub : (block + 1) * sub]
            far_ref[at, lanes] = scr[rows, half + block * sub : half + (block + 1) * sub].astype(BF)


def small_grads(dsmall, ddt, dconv, dvec):
    half = ddt.shape[1] // 2
    return call(
        small_grads_body,
        (shape((SMALL, half), F32), shape((SMALL, half), BF)),
        scratch_shapes=[pltpu.VMEM((SMALL, 2 * half), F32)],
        cost_estimate=cost(2e9),
    )(dsmall, ddt, dconv, dvec)


def join_values(n_grp, where_ref, parts):
    mine = where_ref[1] == 0
    for d in range(n_grp):
        for h in (0, 1):
            sub = parts[0].shape[2]
            at = pl.ds(pl.multiple_of(((where_ref[0] ^ d) * 2 + h) * sub, sub), sub)
            yield at, jnp.where(mine, parts[d][h], parts[n_grp + d][h]).astype(F32)


def join_p_body(n_grp, n_dp, where_ref, w_ref, gain_ref, *refs):
    parts = refs[: 2 * n_grp]
    out_ref, sum_ref, down_ref, kq_ref, dt_ref, conv_ref, cb_ref, db_ref, skip_ref, small = refs[2 * n_grp + 1 :]
    i = pl.program_id(0)
    rows, sub = w_ref.shape[0], parts[0].shape[2]
    part = parts[0].shape[1] - rows

    @pl.when(i == 0)
    def _():
        sum_ref[...] = jnp.zeros(sum_ref.shape, F32)

    for at, value in join_values(n_grp, where_ref, parts):
        out_ref[:, at] = value[:rows] * gain_ref[...]
        sum_ref[...] += value[:rows] * w_ref[:, at].astype(F32)
        small[pl.ds(pl.multiple_of(i * part, 16), part), at] = value[rows:]

    @pl.when(i == n_dp - 1)
    def _():
        for b in range(down_ref.shape[0] // LANES):
            at = slice(b * LANES, (b + 1) * LANES)
            down_ref[at, :] = small[DOWN:KQ, at].T
        kq_ref[...] = small[KQ:DT, :]
        dt_ref[...] = small[DT:VEC, :]
        conv_ref[...] = small[VEC : VEC + 4, :]
        cb_ref[...] = small[VEC + 4 : VEC + 5, :]
        db_ref[...] = small[VEC + 5 : VEC + 6, :]
        skip_ref[...] = small[VEC + 6 : VEC + 7, :]


def join_q_body(n_grp, n_dp, where_ref, w_ref, gain_ref, *refs):
    parts, out_ref, sum_ref, o_ref = refs[: 2 * n_grp], refs[-3], refs[-2], refs[-1]
    i = pl.program_id(0)
    rows, sub = w_ref.shape[0], parts[0].shape[2]
    wide = o_ref.shape[1] // 4

    @pl.when(i == 0)
    def _():
        sum_ref[...] = jnp.zeros(sum_ref.shape, F32)

    for at, value in join_values(n_grp, where_ref, parts):
        out_ref[:, at] = value[:rows] * gain_ref[...]
        sum_ref[...] += value[:rows] * w_ref[:, at].astype(F32)
        for c in range(4):
            lanes = pl.ds(pl.multiple_of(c * wide + i * sub, sub), sub)
            o_ref[at, lanes] = value[rows + c * sub : rows + (c + 1) * sub]


def join_packed(body, where, weight, gain, parts, before, side, n_dp, extras, scratch=()):
    rows = weight.shape[0]
    n_grp = len(parts) // 2
    sub = parts[0].shape[2] // n_dp
    wide = 2 * n_grp * sub
    dims = (2, parts[0].shape[1], sub)
    mine = pl.BlockSpec(dims, lambda i, w: (0, 0, i * (1 - w[1])))
    other = pl.BlockSpec(dims, lambda i, w: (0, 0, i * w[1]))
    last = [] if before is None else [before]
    return call(
        partial(body, n_grp, n_dp),
        (shape(weight.shape, F32), shape((rows, sub), F32), *extras),
        grid_spec=pltpu.PrefetchScalarGridSpec(
            num_scalar_prefetch=1,
            grid=(n_dp,),
            in_specs=[
                pl.BlockSpec((rows, wide), lambda i, w: (0, side * n_dp + i)),
                pl.BlockSpec((rows, 1), lambda i, w: (0, 0)),
            ]
            + [mine] * n_grp
            + [other] * n_grp
            + [pl.BlockSpec(memory_space=pl.ANY)] * len(last),
            out_specs=[
                pl.BlockSpec((rows, wide), lambda i, w: (0, side * n_dp + i)),
                pl.BlockSpec((rows, sub), lambda i, w: (0, 0)),
            ]
            + [pl.BlockSpec(v.shape, lambda i, w: (0, 0)) for v in extras],
            scratch_shapes=list(scratch),
        ),
        input_output_aliases={3 + len(parts): 0} if last else {},
        cost_estimate=cost(8e9),
    )(where, weight, gain, *parts, *last)


def rms_of(hidden):
    return lax.rsqrt(jnp.mean(hidden * hidden, axis=1, keepdims=True) + EPSILON)


def slot_masks(lengths, length):
    ends = jnp.cumsum(lengths, axis=1)
    position = jnp.arange(length, dtype=jnp.int32)
    segment = jnp.sum((position[None, :, None] >= ends[:, None, :]).astype(jnp.int32), axis=2)
    valid = (position[None, :] < ends[:, -1:]).astype(F32)
    same = []
    for lag in (1, 2, 3):
        before = jnp.concatenate([jnp.full((segment.shape[0], lag), -1, jnp.int32), segment[:, :-lag]], axis=1)
        same.append((before == segment).astype(F32))
    stack = jnp.stack([same[0]] + same, axis=2).reshape(-1, 4, 1)
    spread = jnp.broadcast_to(stack, stack.shape[:2] + (LANES,)).reshape(-1, 4 * LANES)
    return spread, valid


def everywhere(value, axis):
    return lax.all_gather(value, "dp", axis=axis, tiled=True)


def after(value, *others):
    return lax.optimization_barrier((value, *others))[0]


def on_any_line(boundary, doc_lengths, norm_gain, in_weight, conv_weight, conv_bias, down_weight, kq_weight,
              dt_weight, dt_bias, skip_weight, out_weight):
    s = lax.axis_index("section")
    g = lax.axis_index("grp")
    n_grp = lax.axis_size("grp")
    n_dp = lax.axis_size("dp")
    length, width = boundary.shape[3], boundary.shape[4]
    inner = in_weight.shape[2] // 2
    block = inner // n_dp
    sub = block // (2 * n_grp)
    half = sub * n_dp
    mine_first = s == 0
    gain = norm_gain[0].astype(F32)[:, None]

    def pick(first, second):
        return jnp.where(mine_first, first, second)

    rows = boundary[0, :, 0]
    traded = swap(pick(rows[1], rows[0]), "section", 1)
    hidden = pick(rows[0], traded)
    cotangent = pick(traded, rows[1])
    lengths = lax.dynamic_index_in_dim(doc_lengths[:, 0], s, 0, keepdims=True)
    all_lengths = jnp.concatenate([lengths] + peers(lengths), axis=0)
    masks, valid = slot_masks(all_lengths, length)
    valid = valid[0][:, None]

    def columns(array):
        blocks = array.shape[1] // block
        view = array.reshape(array.shape[0], blocks, n_grp, 2, sub)
        view = lax.dynamic_index_in_dim(view, g, 2, keepdims=False)
        halves = [view[:, :, h].reshape(array.shape[0], blocks * sub) for h in (0, 1)]
        return pick(*halves), pick(halves[1], halves[0])

    def side(which):
        part = in_weight[0, :, which * inner : (which + 1) * inner]
        return columns((part.astype(F32) * gain).astype(BF))

    def out_side():
        view = lax.dynamic_slice_in_dim(out_weight[0], g * 2 * sub, 2 * sub, 0)
        return pick(view[:sub], view[sub:]), pick(view[sub:], view[:sub])

    def small_side():
        def lanes(array):
            return lax.dynamic_slice_in_dim(array, g * 2 * sub, 2 * sub, 1)

        down = lax.dynamic_slice_in_dim(down_weight[0], g * 2 * sub, 2 * sub, 0).T
        view = jnp.concatenate(
            [down, lanes(kq_weight[0]), jnp.zeros((2 * LANES - RANK - 2 * STATE, 2 * sub), BF), lanes(dt_weight[0]),
             lanes(conv_weight[0]), lanes(conv_bias), lanes(dt_bias), lanes(skip_weight)], axis=0)
        return pick(view[:, :sub], view[:, sub:]), pick(view[:, sub:], view[:, :sub])

    def two_layers(keep, send):
        come = swap(send, "section", 1)
        return pick(keep, come), pick(come, keep)

    x_sides, s_sides = two_layers(*side(0)), two_layers(*small_side())
    g_sides, o_sides = two_layers(*side(1)), two_layers(*out_side())

    def with_far(near):
        return near, swap(near, "section", 1)

    layers = []
    for l in (0, 1):
        w_s = jnp.concatenate(with_far(everywhere(s_sides[l], 1)), axis=1)
        w_x = with_far(everywhere(x_sides[l], 0))
        w_g = with_far(everywhere(g_sides[l], 0))
        w_o = with_far(everywhere(o_sides[l], 0))
        cat = w_s[: 2 * LANES]
        wdt = w_s[2 * LANES : 2 * LANES + RANK]
        tail = w_s[2 * LANES + RANK :].astype(F32)
        vec = jnp.concatenate([tail, jnp.zeros((9, tail.shape[1]), F32)], axis=0)
        layers.append((w_x, w_g, w_o, cat, wdt, vec))

    def group(value):
        return jnp.concatenate([value] + peers(value), axis=0)

    def scatter(value):
        total = value[:length].astype(F32)
        for d in range(1, n_grp):
            total = total + swap(value[d * length : (d + 1) * length], "grp", d).astype(F32)
        return total

    def forward(h, layer):
        w_x, w_g, w_o, cat, wdt, vec = layer
        a = group((h * rms_of(h)).astype(BF))
        x, act, part = proj_conv(n_grp, a, *w_x, masks, vec, cat)
        gate = proj(a, *w_g, 0)
        return a, x, gate, act, [part] + peers(part)

    def gated_back(saved, layer, dgated, y, rec_out):
        gate = saved[2]
        if y is None:
            y = rec_out[5]
        return gate_back(n_grp, y, gate, dgated) + tuple(rec_out)

    def backward(h, dout, dbranch, layer, saved, rec_out):
        w_x, w_g, w_o, cat, wdt, vec = layer
        a, x, gate, act, parts = saved
        gated_near, gated_far, dgate_near, dgate_far, lr, dstate, dpart, ddt, dvec = rec_out[:9]
        dx_near, dx_far, dsmall, dconv = conv_bwd([dpart] + peers(dpart), x, act, dstate, masks, vec, cat)
        scaled = scatter(total_of([dx_near, dx_far, dgate_near, dgate_far], [*w_x, *w_g], 1))
        rms = rms_of(h)
        own = h * rms
        dh = dout + rms * (scaled - own * jnp.mean(scaled * own, axis=1, keepdims=True))

        a_far, dbranch_far = swap(a, "section", 1), swap(dbranch, "section", 1)
        dgate_come, gated_come = swap(dgate_far, "section", 1), swap(gated_far, "section", 1)
        dx_come = swap(dx_far, "section", 1)

        def both(left, right, left_come, right_come):
            return (dot(left, right, 0, 0) + dot(left_come, right_come, 0, 0)).astype(BF)

        grad_g = both(a, dgate_near, a_far, dgate_come)
        grad_o = both(gated_near, dbranch, gated_come, dbranch_far)
        grad_x = both(a, dx_near, a_far, dx_come)
        grad_s = jnp.concatenate([dsmall, ddt, dconv[:5], dvec[:2], jnp.zeros((1, ddt.shape[1]), F32)], axis=0)
        grad_s = grad_s[:, :half] + swap(grad_s[:, half:].astype(BF), "section", 1).astype(F32)
        grad_o = jnp.concatenate([grad_o, grad_s.T.astype(BF)], axis=1)
        return dh, (grad_g, grad_o, grad_x)

    h0 = hidden.astype(F32)
    saved0 = forward(h0, layers[0])
    y0 = rec(saved0[4], saved0[3], None, layers[0][4], layers[0][5], masks, True)
    gated0 = gate_values(y0, saved0[2])[0].astype(BF)
    branch0 = scatter(total_of([gated0[:, :half], gated0[:, half:]], layers[0][2], 0))
    h1 = (h0 + valid * branch0).astype(BF).astype(F32)
    saved1 = forward(h1, layers[1])
    dout1 = cotangent.astype(F32)
    dbranch1 = group((valid * dout1).astype(BF))
    dgated1 = proj(dbranch1, *layers[1][2], 1)
    dy1 = gate_values(dgated1, saved1[2])[0]
    rec1 = rec(saved1[4], saved1[3], dy1, layers[1][4], layers[1][5], masks, True)
    rec1 = gated_back(saved1, layers[1], dgated1, None, rec1)
    branch1 = scatter(total_of(rec1[:2], layers[1][2], 0))
    out1 = h1 + valid * branch1
    dh1, grads1 = backward(h1, dout1, dbranch1, layers[1], saved1, rec1)
    dout0 = dh1.astype(BF).astype(F32)
    dbranch0 = group((valid * dout0).astype(BF))
    dgated0 = proj(dbranch0, *layers[0][2], 1)
    dy0 = gate_values(dgated0, saved0[2])[0]
    rec0 = rec(saved0[4], saved0[3], dy0, layers[0][4], layers[0][5], masks, False)
    rec0 = gated_back(saved0, layers[0], dgated0, y0, rec0)
    dh0, grads0 = backward(h0, dout0, dbranch0, layers[0], saved0, rec0)

    far = swap(pick(out1, dh0), "section", 1)
    result = pick(jnp.stack([dh0, far]), jnp.stack([far, out1]))
    result = result.reshape(1, 2, 1, length, width)

    def collected(l, grad):
        near = lax.psum_scatter(grad, "dp", scatter_dimension=0, tiled=True)
        far = directed(near, "section", [(1 - l, l)])
        halves = jnp.stack([near, far] if l == 0 else [far, near])
        out = [halves]
        for d in range(1, n_grp):
            pairs = [(l * n_grp + i, l * n_grp + (i ^ d)) for i in range(n_grp)]
            out.append(directed(halves, ("section", "grp"), pairs))
        return out

    (g1, o1, x1), (g0, o0, x0) = [[collected(l, grad) for grad in grads] for l, grads in ((1, grads1), (0, grads0))]

    def in_order(firsts, seconds):
        return jnp.stack([pick(a, b) for a, b in zip(firsts, seconds)])[jnp.arange(n_grp) ^ g]

    smalls = in_order([v[:, :, width:] for v in o0], [v[:, :, width:] for v in o1]).astype(F32)
    grad_small = smalls.transpose(3, 0, 1, 2).reshape(smalls.shape[3], block)
    sides = []
    for first, second in ((x0, x1), (g0, g1)):
        value = in_order(first, second).reshape(n_grp, 2, -1, n_dp, sub)
        sides.append(value.transpose(2, 3, 0, 1, 4).reshape(value.shape[2], inner))
    product = jnp.concatenate(sides, axis=1).astype(F32)
    grad_in = product * gain
    grad_gain = jnp.sum(product * in_weight[0].astype(F32), axis=1)
    grad_out = in_order([v[:, :, :width] for v in o0], [v[:, :, :width] for v in o1]).astype(F32).reshape(block, width)
    base = 2 * LANES + RANK
    return (
        result,
        grad_gain[None],
        grad_in[None],
        grad_small[None, base : base + 4],
        grad_small[base + 4][None],
        grad_small[:RANK].T[None],
        grad_small[None, RANK : RANK + 2 * STATE],
        grad_small[None, 2 * LANES : base],
        grad_small[base + 5][None],
        grad_small[base + 6][None],
        grad_out[None],
    )


def on_device(boundary, doc_lengths, norm_gain, in_weight, conv_weight, conv_bias, down_weight, kq_weight,
              dt_weight, dt_bias, skip_weight, out_weight):
    s = lax.axis_index("section")
    g = lax.axis_index("grp")
    n_grp = lax.axis_size("grp")
    n_dp = lax.axis_size("dp")
    length, width = boundary.shape[3], boundary.shape[4]
    inner = in_weight.shape[2] // 2
    block = inner // n_dp
    sub = block // (2 * n_grp)
    n_rows = width // n_dp
    mine_first = s == 0
    where = jnp.stack([g, s]).astype(jnp.int32)
    gain = norm_gain[0].astype(F32)[:, None]

    def pick(first, second):
        return jnp.where(mine_first, first, second)

    def section(value):
        return swap(value, "section", 1)

    def two_layers(keep, send):
        come = section(send)
        return pick(keep, come), pick(come, keep)

    def group(value):
        return jnp.concatenate([value] + peers(value), axis=0)

    def scatter(value):
        total = value[:length].astype(F32)
        for d in range(1, n_grp):
            total = total + swap(value[d * length : (d + 1) * length], "grp", d).astype(F32)
        return total

    def line(value):
        return lax.all_gather(value, "dp", axis=0)

    p_sides = two_layers(*cut_small(where, in_weight[0], gain, down_weight[0], kq_weight[0], dt_weight[0],
                                    conv_weight[0], conv_bias, dt_bias, skip_weight, n_dp, n_grp, sub))
    p0 = line(p_sides[0])
    p0_far = section(p0)
    rows = boundary[0, :, 0]
    traded = section(pick(rows[1], rows[0]))
    hidden = pick(rows[0], traded)
    cotangent = pick(traded, rows[1])
    lengths = lax.dynamic_index_in_dim(doc_lengths[:, 0], s, 0, keepdims=True)
    all_lengths = jnp.concatenate([lengths] + peers(lengths), axis=0)
    masks, valid = slot_masks(all_lengths, length)
    valid = valid[0][:, None]
    h0 = hidden.astype(F32)
    a0_parts = peers((h0 * rms_of(h0)).astype(BF))
    a0 = jnp.concatenate([(h0 * rms_of(h0)).astype(BF)] + a0_parts, axis=0)
    q_sides = two_layers(*cut_out(where, in_weight[0], gain, out_weight[0], n_dp, n_grp, sub))
    q0 = line(after(q_sides[0], p0, a0))
    q0_far = section(q0)
    dout1 = cotangent.astype(F32)

    def input_gradient(h, dout, scaled):
        rms = rms_of(h)
        own = h * rms
        return dout + rms * (scaled - own * jnp.mean(scaled * own, axis=1, keepdims=True))

    def summed(grad):
        return lax.psum_scatter(grad, "dp", scatter_dimension=0, tiled=True)[0]

    def collected(l, near):
        far = directed(near, "section", [(1 - l, l)])
        halves = jnp.stack([near, far] if l == 0 else [far, near])
        out = [halves]
        for d in range(1, n_grp):
            pairs = [(l * n_grp + i, l * n_grp + (i ^ d)) for i in range(n_grp)]
            out.append(directed(halves, ("section", "grp"), pairs))
        return out

    def gradient_q(a, a_far, dbranch, dbranch_far, gated, gated_far, dgate, dgate_far):
        return grad_q(a, a_far, dgate, section(dgate_far), gated, section(gated_far), dbranch, dbranch_far, n_dp)

    def gradient_p(a, a_far, dx_near, dx_far, dsmall, ddt, dconv, dvec):
        small_near, small_far = small_grads(dsmall, ddt, dconv, dvec)
        return grad_p(a, a_far, dx_near, section(dx_far), small_near, section(small_far), n_dp)

    x0, act0, part0, cat0, wdt0, vec0 = first_products(n_grp, a0, masks, p0, p0_far, n_rows)
    parts0 = [part0] + peers(part0)
    dbranch1 = group(after((valid * dout1).astype(BF), *parts0))
    y0 = rec(parts0, act0, None, wdt0, vec0, masks, True)
    p1 = line(after(p_sides[1], q0, *parts0))
    p1_far = section(p1)
    a0_far = section(after(a0, y0))
    gate0, gated0_near, gated0_far = gate_product(a0, after(y0, dbranch1), q0, q0_far, n_rows)
    branch0 = scatter(branch_product(gated0_near, gated0_far, q0, q0_far, n_rows))
    h1 = (h0 + valid * branch0).astype(BF).astype(F32)

    q1 = line(after(q_sides[1], p1, h1))
    q1_far = section(q1)
    a1 = group((h1 * rms_of(h1)).astype(BF))
    dbranch1_far = section(after(dbranch1, h1))
    x1, act1, part1, cat1, wdt1, vec1 = first_products(n_grp, a1, masks, p1, p1_far, n_rows)
    parts1 = [part1] + peers(part1)
    a1_far = section(after(a1, part1))
    y1 = rec(parts1, act1, None, wdt1, vec1, masks, True)
    gate1, gated1_near, gated1_far = gate_product(a1, y1, q1, q1_far, n_rows)

    dy1, dgate1_near, dgate1_far = dgated_product(dbranch1, y1, gate1, q1, q1_far, n_rows)
    gq1 = gradient_q(a1, a1_far, dbranch1, dbranch1_far, gated1_near, gated1_far, dgate1_near, dgate1_far)
    sq1 = summed(gq1)
    branch1 = branch_product(gated1_near, gated1_far, q1, q1_far, n_rows)
    lr1, dstate1, dpart1, ddt1, dvec1 = rec(parts1, act1, after(dy1, gq1, branch1), wdt1, vec1, masks, False)
    out1 = h1 + valid * scatter(branch1)
    dparts1 = [dpart1] + peers(dpart1)
    dstate1 = after(dstate1, out1)
    dx1_near, dx1_far, dsmall1, dconv1 = conv_bwd(dparts1, x1, act1, dstate1, masks, vec1, cat1)
    dnormed1 = dnormed_product(
        [dx1_near, dx1_far, dgate1_near, dgate1_far], p1, p1_far, q1, q1_far, n_rows)
    dh1 = input_gradient(h1, dout1, scatter(dnormed1))
    gp1 = gradient_p(a1, a1_far, after(dx1_near, dnormed1), dx1_far, dsmall1, ddt1, dconv1, dvec1)
    sp1 = summed(after(gp1, sq1))
    dout0 = dh1.astype(BF).astype(F32)
    dbranch0 = group((valid * dout0).astype(BF))

    q_parts1 = collected(1, after(sq1, dbranch0))
    dbranch0_far = section(dbranch0)
    dy0, dgate0_near, dgate0_far = dgated_product(after(dbranch0, gp1), y0, gate0, q0, q0_far, n_rows)
    gq0 = gradient_q(a0, a0_far, dbranch0, dbranch0_far, gated0_near, gated0_far, dgate0_near, dgate0_far)
    lr0, dstate0, dpart0, ddt0, dvec0 = rec(parts0, act0, after(dy0, gq0, sp1), wdt0, vec0, masks, False)
    p_parts1 = collected(1, sp1)
    sq0 = summed(after(gq0, sp1))
    dparts0 = [dpart0] + peers(dpart0)
    dstate0 = after(dstate0, *q_parts1, *p_parts1)
    dx0_near, dx0_far, dsmall0, dconv0 = conv_bwd(dparts0, x0, act0, dstate0, masks, vec0, cat0)
    gp0 = gradient_p(a0, a0_far, dx0_near, dx0_far, dsmall0, ddt0, dconv0, dvec0)
    sp0 = summed(after(gp0, sq0))
    dnormed0 = dnormed_product(
        [after(dx0_near, gp0), dx0_far, dgate0_near, dgate0_far], p0, p0_far, q0, q0_far, n_rows)
    dh0 = input_gradient(h0, dout0, scatter(dnormed0))
    q_parts0, p_parts0 = collected(0, sq0), collected(0, sp0)

    out_far = directed(out1, "section", [(0, 1)])
    dh_far = directed(dh0, "section", [(1, 0)])
    result = jnp.stack([pick(dh0, out_far), pick(dh_far, out1)]).reshape(1, 2, 1, length, width)

    grad_in, sum_q, grad_out = join_packed(
        join_q_body, where, in_weight[0], gain, q_parts0 + q_parts1, None, 1, n_dp, [shape((block, width), F32)])
    smalls = [shape(v, F32) for v in ((block, RANK), (2 * STATE, block), (RANK, block), (4, block))]
    smalls += [shape((1, block), F32)] * 3
    grad_in, sum_p, grad_down, grad_kq, grad_dt, grad_conv, grad_cb, grad_db, grad_skip = join_packed(
        join_p_body, where, in_weight[0], gain, p_parts0 + p_parts1, grad_in, 0, n_dp, smalls,
        [pltpu.VMEM((SMALL, block), F32)])
    grad_gain = jnp.sum(sum_q + sum_p, axis=1)
    return (
        result,
        grad_gain[None],
        grad_in[None],
        grad_conv[None],
        grad_cb,
        grad_down[None],
        grad_kq[None],
        grad_dt[None],
        grad_db,
        grad_skip,
        grad_out[None],
    )


def solution(mesh):
    packed = mesh.shape["dp"] == 4 and mesh.shape["grp"] == 4
    return jax.shard_map(
        on_device if packed else on_any_line,
        mesh=mesh,
        in_specs=(
            P("section", None, ("grp", "dp"), None, None),
            P(None, ("grp", "dp"), None),
            P("section", "dp"),
            P("section", "dp", None),
            P("section", None, "dp"),
            P("section", "dp"),
            P("section", "dp", None),
            P("section", None, "dp"),
            P("section", None, "dp"),
            P("section", "dp"),
            P("section", "dp"),
            P("section", "dp", None),
        ),
        out_specs=(
            P("section", None, ("grp", "dp"), None, None),
            P("section", "dp"),
            P("section", "dp", None),
            P("section", None, "dp"),
            P("section", "dp"),
            P("section", "dp", None),
            P("section", None, "dp"),
            P("section", None, "dp"),
            P("section", "dp"),
            P("section", "dp"),
            P("section", "dp", None),
        ),
        check_vma=False,
    )
```

```python
from functools import partial

import jax
import jax.numpy as jnp
from jax import lax
from jax.experimental import pallas as pl
from jax.experimental.pallas import tpu as pltpu
from jax.sharding import PartitionSpec as P

EPSILON = 1e-05
BF = jnp.bfloat16
F32 = jnp.float32
STATE = 16
RANK = 128
LANES = 128
ROWS = 8
MIB = 1024 * 1024


def dot(left, right, left_axis, right_axis, kind=F32):
    return lax.dot_general(
        left, right, (((left_axis,), (right_axis,)), ((), ())), preferred_element_type=kind
    )


def sig(value):
    return 1.0 / (1.0 + jnp.exp(-value))


def swap(value, axis, shift):
    return lax.ppermute(value, axis, [(i, i ^ shift) for i in range(lax.axis_size(axis))])


def directed(value, axis, pairs):
    return lax.ppermute(value, axis, pairs)


def peers(value):
    return [swap(value, "grp", d) for d in range(1, lax.axis_size("grp"))]


def call(body, out_shape, **kwargs):
    limit = kwargs.pop("vmem", 48)
    return pl.pallas_call(
        body,
        out_shape=out_shape,
        compiler_params=pltpu.CompilerParams(vmem_limit_bytes=limit * MIB),
        **kwargs,
    )


def cost(flops):
    return pl.CostEstimate(flops=int(1 * flops), bytes_accessed=0, transcendentals=0)


def shape(dims, kind):
    return jax.ShapeDtypeStruct(dims, kind)


def proj_body(a_ref, near_ref, far_ref, out_ref, *, w_axis):
    @pl.when(pl.program_id(0) == 0)
    def _():
        out_ref[...] = dot(a_ref[...], near_ref[...], 1, w_axis)

    @pl.when(pl.program_id(0) == 1)
    def _():
        out_ref[...] = dot(a_ref[...], far_ref[...], 1, w_axis)


def proj(a, near, far, w_axis):
    rows = a.shape[0]
    half = near.shape[1 - w_axis]

    def whole(v):
        return pl.BlockSpec(v.shape, lambda i: (0,) * v.ndim)

    return call(
        partial(proj_body, w_axis=w_axis),
        shape((rows, 2 * half), F32),
        grid=(2,),
        in_specs=[whole(a), whole(near), whole(far)],
        out_specs=pl.BlockSpec((rows, half), lambda i: (0, i)),
        cost_estimate=cost(4 * rows * half * a.shape[1]),
    )(a, near, far)


def total_body(n, w_axis, *refs):
    lefts, rights, out_ref = refs[:n], refs[n : 2 * n], refs[2 * n]
    total = dot(lefts[0][...], rights[0][...], 1, w_axis)
    for left, right in zip(lefts[1:], rights[1:]):
        total = total + dot(left[...], right[...], 1, w_axis)
    out_ref[...] = total.astype(BF)


def total_of(lefts, rights, w_axis):
    rows = lefts[0].shape[0]
    width = rights[0].shape[1 - w_axis]
    step = 512

    def left_spec(v):
        return pl.BlockSpec(v.shape, lambda i: (0, 0))

    def right_spec(v):
        if w_axis == 0:
            return pl.BlockSpec((v.shape[0], step), lambda i: (0, i))
        return pl.BlockSpec((step, v.shape[1]), lambda i: (i, 0))

    return call(
        partial(total_body, len(lefts), w_axis),
        shape((rows, width), BF),
        grid=(width // step,),
        in_specs=[left_spec(v) for v in lefts] + [right_spec(v) for v in rights],
        out_specs=pl.BlockSpec((rows, step), lambda i: (0, i)),
        cost_estimate=cost(2 * rows * width * sum(v.shape[1] for v in lefts)),
    )(*lefts, *rights)


def conv_of(x_ref, rows, pad_ref, mask_ref, vec_ref, cols):
    length = pad_ref.shape[0] - ROWS
    x = x_ref[rows, cols]
    pad_ref[0:ROWS, :] = jnp.zeros((ROWS, LANES), F32)
    pad_ref[ROWS : ROWS + length, :] = x
    total = vec_ref[4:5, cols] + vec_ref[0:1, cols] * x
    shifted = []
    for j in (1, 2, 3):
        earlier = pad_ref[ROWS - j : ROWS - j + length, :] * mask_ref[rows, j * LANES : (j + 1) * LANES]
        shifted.append(earlier)
        total = total + vec_ref[j : j + 1, cols] * earlier
    return total, shifted


def proj_conv_body(n_slots, a_ref, near_ref, far_ref, mask_ref, vec_ref, cat_ref, x_ref, inner_ref, part_ref,
                   pad_ref, sum_ref):
    i = pl.program_id(0)
    rows_all, half = x_ref.shape
    length = rows_all // n_slots

    @pl.when(i == 0)
    def _():
        x_ref[...] = dot(a_ref[...], near_ref[...], 1, 0)

    @pl.when(i == 1)
    def _():
        x_ref[...] = dot(a_ref[...], far_ref[...], 1, 0)

    for j in range(n_slots):
        rows = slice(j * length, (j + 1) * length)
        for b in range(half // LANES):
            cols = slice(b * LANES, (b + 1) * LANES)
            c, _ = conv_of(x_ref, rows, pad_ref, mask_ref, vec_ref, cols)
            inner_ref[rows, cols] = (c * sig(c)).astype(BF)
    both = dot(inner_ref[...], cat_ref[...], 1, 1)

    @pl.when(i == 0)
    def _():
        sum_ref[...] = both

    @pl.when(i == 1)
    def _():
        total = sum_ref[...] + both
        part_ref[...] = pack(total[:, :RANK], total[:, RANK:])


def proj_conv(n_slots, a, near, far, masks, vec, cat):
    rows = a.shape[0]
    half = near.shape[1]

    def whole(v):
        return pl.BlockSpec(v.shape, lambda i: (0,) * v.ndim)

    def block(n):
        return pl.BlockSpec((n, half), lambda i: (0, i))

    part_like = shape((rows, 2 * LANES), BF)
    return call(
        partial(proj_conv_body, n_slots),
        (shape((rows, 2 * half), F32), shape((rows, 2 * half), BF), part_like),
        grid=(2,),
        in_specs=[whole(a), whole(near), whole(far), whole(masks), block(vec.shape[0]), block(cat.shape[0])],
        out_specs=(block(rows), block(rows), whole(part_like)),
        scratch_shapes=[pltpu.VMEM((ROWS + rows // n_slots, LANES), F32), pltpu.VMEM((rows, 2 * LANES), F32)],
        cost_estimate=cost(4 * rows * half * a.shape[1]),
    )(a, near, far, masks, vec, cat)


def pack(low_rank, kq):
    high = kq.astype(BF).astype(F32)
    rest = pltpu.roll(kq - high, 64, axis=1)
    return jnp.concatenate([low_rank, high + rest], axis=1).astype(BF)


def summed_parts(parts, j, length):
    low_rank = jnp.zeros((length, RANK), F32)
    kq = jnp.zeros((length, LANES), F32)
    for d, part in enumerate(parts):
        rows = slice((j ^ d) * length, ((j ^ d) + 1) * length)
        low_rank = low_rank + part[rows, :RANK].astype(F32)
        kq = kq + part[rows, RANK:].astype(F32)
    kq = kq + pltpu.roll(kq, 64, axis=1)
    lane = lax.broadcasted_iota(jnp.int32, (1, LANES), 1)
    return low_rank, jnp.where(lane < 2 * STATE, kq, 0.0)


def rec_body(backward, keep_y, n_slots, length, width, *refs):
    parts, refs = refs[:n_slots], refs[n_slots:]
    y_out = None
    if backward:
        (inner, dy_ref, wdt, vec, mask, lr_out, dstate_out, dpart_out, ddt_out, dvec_out), refs = refs[:10], refs[10:]
        if keep_y:
            y_out, refs = refs[0], refs[1:]
        (kq_n, kq_i, c_i, lr_n, step_i, p_i, y_i, kb, str_n, hist, dy_i, a_i, h_scr, dkq_i,
         dlr_n, corr_n, prod, drate_n) = refs
    else:
        (inner, wdt, vec, mask, y_out, kq_n, kq_i, c_i, lr_n, step_i, p_i, y_i, kb, state) = refs
    nb = width // (2 * LANES)
    first = pl.program_id(0) == 0
    last = pl.program_id(0) == pl.num_programs(0) - 1
    lane = lax.broadcasted_iota(jnp.int32, (1, LANES), 1)
    pieces = [(hh, b, slice((hh * nb + b) * LANES, (hh * nb + b + 1) * LANES)) for hh in (0, 1) for b in range(nb)]

    def rows_of(j):
        return slice(j * length, (j + 1) * length)

    def spread(j, hh):
        return pl.ds(hh * n_slots + j, length, stride=ROWS)

    @pl.when(first)
    def _():
        for j in range(n_slots):
            low_rank, kq = summed_parts(parts, j, length)
            lr_n[rows_of(j), :] = low_rank.astype(BF)
            if backward:
                lr_out[rows_of(j), :] = low_rank.astype(BF)
            kq_n[rows_of(j), :] = kq
            for hh in (0, 1):
                kq_i[spread(j, hh), :] = kq
                c_i[spread(j, hh), :] = mask[rows_of(j), 0:LANES]
        kq = kq_i[...]
        high = kq.astype(BF).astype(F32)
        split = (high + pltpu.roll(kq - high, 64, axis=1)).astype(BF)
        source = lax.broadcasted_iota(jnp.int32, (LANES, 2 * LANES), 0) % 64
        column = lax.broadcasted_iota(jnp.int32, (LANES, 2 * LANES), 1) // LANES
        for n in range(0, 2 * STATE, 2):
            copied = dot(split, jnp.where(source == n + column, 1.0, 0.0).astype(BF), 1, 0)
            kb[n] = copied[:, :LANES]
            kb[n + 1] = copied[:, LANES:]
        if backward:
            dkq_i[...] = jnp.zeros(dkq_i.shape, F32)
            dlr_n[...] = jnp.zeros(dlr_n.shape, F32)
            corr_n[...] = jnp.zeros(corr_n.shape, F32)

    for j in range(n_slots):
        rows = rows_of(j)
        rate = dot(lr_n[rows, :], wdt[...], 1, 0)
        kq = kq_n[rows, :]
        ks = jnp.sum(jnp.where(lane < STATE, kq * kq, 0.0), axis=1, keepdims=True)
        for hh, b, cols in pieces:
            strength = sig(rate[:, cols] + vec[5:6, cols])
            step = strength / (1.0 + strength * ks)
            step_i[b, spread(j, hh), :] = step
            p_i[b, spread(j, hh), :] = step * inner[rows, cols].astype(F32)
            if backward:
                str_n[rows, cols] = strength
                dy_i[b, spread(j, hh), :] = dy_ref[rows, cols]

    if backward:
        hist[0] = jnp.zeros(hist.shape[1:], F32)
    else:
        state[...] = jnp.zeros(state.shape, F32)

    def forward_step(t, carry):
        now = pl.ds(pl.multiple_of(t * ROWS, ROWS), ROWS)
        c = c_i[now, :]
        steps = [step_i[b, now, :] for b in range(nb)]
        ps = [p_i[b, now, :] for b in range(nb)]
        ys = [jnp.zeros((ROWS, LANES), F32) for _ in range(nb)]
        for n in range(STATE):
            k = kb[n, now, :]
            ck2 = c * k * k
            if y_out is not None:
                q = kb[STATE + n, now, :]
            for b in range(nb):
                before = hist[t, n * nb + b] if backward else state[n * nb + b]
                after = (c - ck2 * steps[b]) * before + k * ps[b]
                if backward:
                    hist[t + 1, n * nb + b] = after
                else:
                    state[n * nb + b] = after
                if y_out is not None:
                    ys[b] = ys[b] + q * after
        if y_out is not None:
            for b in range(nb):
                y_i[b, now, :] = ys[b]
        return carry

    lax.fori_loop(0, length, forward_step, 0, unroll=2)

    if y_out is not None:
        for j in range(n_slots):
            rows = rows_of(j)
            for hh, b, cols in pieces:
                y_out[rows, cols] = y_i[b, spread(j, hh), :] + vec[6:7, cols] * inner[rows, cols].astype(F32)
    if not backward:
        return

    h_scr[...] = jnp.zeros(h_scr.shape, F32)

    def backward_step(i, carry):
        t = length - 1 - i
        at = pl.ds(pl.multiple_of(t * 2 * ROWS, 2 * ROWS), 2 * ROWS)
        now = pl.ds(pl.multiple_of(t * ROWS, ROWS), ROWS)
        c = c_i[now, :]
        steps = [step_i[b, now, :] for b in range(nb)]
        ps = [p_i[b, now, :] for b in range(nb)]
        dys = [dy_i[b, now, :] for b in range(nb)]
        a_sum = [jnp.zeros((ROWS, LANES), F32) for _ in range(nb)]
        b_sum = [jnp.zeros((ROWS, LANES), F32) for _ in range(nb)]
        for n in range(STATE):
            k, q = kb[n, now, :], kb[STATE + n, now, :]
            ck = c * k
            ck2 = ck * k
            dk1 = dk2 = dq = None
            for b in range(nb):
                before, after = hist[t, n * nb + b], hist[t + 1, n * nb + b]
                grad = dys[b] * q + h_scr[n * nb + b]
                a_sum[b] = a_sum[b] + grad * k
                both = grad * before
                b_sum[b] = b_sum[b] + ck2 * both
                h_scr[n * nb + b] = (c - ck2 * steps[b]) * grad
                one, two, three = ps[b] * grad, steps[b] * both, dys[b] * after
                dk1 = one if dk1 is None else dk1 + one
                dk2 = two if dk2 is None else dk2 + two
                dq = three if dq is None else dq + three
            dk = dk1 - (2.0 * ck) * dk2
            prod[at, n * LANES : (n + 1) * LANES] = jnp.concatenate([dk, dq], axis=0).astype(BF)
        for b in range(nb):
            a_i[b, now, :] = a_sum[b]
            p_i[b, now, :] = b_sum[b]
        return carry

    lax.fori_loop(0, length, backward_step, 0, unroll=2)

    source = lax.broadcasted_iota(jnp.int32, (STATE * LANES, LANES), 0) // LANES
    sums = jnp.where(source == lax.broadcasted_iota(jnp.int32, (STATE * LANES, LANES), 1), 1.0, 0.0).astype(BF)
    dkq_i[...] = dkq_i[...] + dot(prod[...], sums, 1, 0)

    ddt = [jnp.zeros((1, LANES), F32) for _ in pieces]
    dskip = [jnp.zeros((1, LANES), F32) for _ in pieces]
    for j in range(n_slots):
        rows = rows_of(j)
        kq = kq_n[rows, :]
        ks = jnp.sum(jnp.where(lane < STATE, kq * kq, 0.0), axis=1, keepdims=True)
        corr = jnp.zeros((length, 1), F32)
        for i, (hh, b, cols) in enumerate(pieces):
            at = spread(j, hh)
            inn = inner[rows, cols].astype(F32)
            a, step, dy = a_i[b, at, :], step_i[b, at, :], dy_ref[rows, cols]
            dstep = inn * a - p_i[b, at, :]
            strength = str_n[rows, cols]
            inv = 1.0 / (1.0 + strength * ks)
            drate = (dstep * (inv * inv) * (strength * (1.0 - strength))).astype(BF)
            drate_n[rows, cols] = drate
            dstate_out[rows, cols] = step * a + vec[6:7, cols] * dy
            corr = corr + jnp.sum(dstep * (step * step), axis=1, keepdims=True)
            ddt[i] = ddt[i] + jnp.sum(drate.astype(F32), axis=0, keepdims=True)
            dskip[i] = dskip[i] + jnp.sum(dy * inn, axis=0, keepdims=True)
        corr_n[rows, :] = corr_n[rows, :] + corr
        dlr_n[rows, :] = dlr_n[rows, :] + dot(drate_n[rows, :], wdt[...], 1, 1)
    ddt_out[...] = dot(lr_n[...], drate_n[...], 0, 0)
    dvec_out[...] = jnp.concatenate(
        [jnp.concatenate(ddt, axis=1), jnp.concatenate(dskip, axis=1), jnp.zeros((6, width), F32)], axis=0
    )

    @pl.when(last)
    def _():
        for j in range(n_slots):
            rows = rows_of(j)
            dk, dq = [
                dkq_i[pl.ds(m * ROWS + j, length, stride=2 * ROWS), :]
                + dkq_i[pl.ds(m * ROWS + n_slots + j, length, stride=2 * ROWS), :]
                for m in (0, 1)
            ]
            dkq = dk + pltpu.roll(dq, STATE, axis=1)
            dkq = dkq - jnp.where(lane < STATE, 2.0 * kq_n[rows, :] * corr_n[rows, :], 0.0)
            dpart_out[rows, :] = pack(dlr_n[rows, :], dkq)


def rec(parts, inner, dy, wdt, vec, masks, keep_y):
    rows, channels = inner.shape
    n_slots = len(parts)
    length = rows // n_slots
    width = channels // 2
    nb = width // (2 * LANES)

    def whole(a):
        return pl.BlockSpec(a.shape, lambda i: (0,) * a.ndim)

    def block(n):
        return pl.BlockSpec((n, width), lambda i: (0, i))

    wide = pltpu.VMEM((nb, ROWS * length, LANES), F32)
    row = pltpu.VMEM((rows, LANES), F32)
    spread = pltpu.VMEM((ROWS * length, LANES), F32)
    y_like = shape((rows, channels), F32)
    y_scratch = wide if dy is None or keep_y else pltpu.VMEM((ROWS, LANES), F32)
    scratch = [row, spread, spread, pltpu.VMEM((rows, RANK), BF), wide, wide, y_scratch]
    scratch += [pltpu.VMEM((2 * STATE, ROWS * length, LANES), F32)]
    if dy is None:
        scratch += [pltpu.VMEM((STATE * nb, ROWS, LANES), F32)]
        return call(
            partial(rec_body, False, True, n_slots, length, width),
            y_like,
            grid=(2,),
            in_specs=[whole(p) for p in parts] + [block(rows), block(RANK), block(vec.shape[0]), pl.BlockSpec((rows, LANES), lambda i: (0, 0))],
            out_specs=block(rows),
            scratch_shapes=scratch,
            cost_estimate=cost(20e9),
        )(*parts, inner, wdt, vec, masks)
    scratch += [
        pltpu.VMEM((rows, width), F32),
        pltpu.VMEM((length + 1, STATE * nb, ROWS, LANES), F32),
        wide,
        wide,
        pltpu.VMEM((STATE * nb, ROWS, LANES), F32),
        pltpu.VMEM((2 * ROWS * length, LANES), F32),
        pltpu.VMEM((rows, RANK), F32),
        row,
        pltpu.VMEM((2 * ROWS * length, STATE * LANES), BF),
        pltpu.VMEM((rows, width), BF),
    ]
    lr_like = shape((rows, RANK), BF)
    part_like = shape((rows, 2 * LANES), BF)
    outs = [lr_like, y_like, part_like, shape((RANK, channels), F32), shape((ROWS, channels), F32)]
    specs = [whole(lr_like), block(rows), whole(part_like), block(RANK), block(ROWS)]
    if keep_y:
        outs, specs = outs + [y_like], specs + [block(rows)]
    return call(
        partial(rec_body, True, keep_y, n_slots, length, width),
        tuple(outs),
        grid=(2,),
        in_specs=[whole(p) for p in parts] + [block(rows), block(rows), block(RANK), block(vec.shape[0]), pl.BlockSpec((rows, LANES), lambda i: (0, 0))],
        out_specs=tuple(specs),
        scratch_shapes=scratch,
        cost_estimate=cost(55e9),
        vmem=62,
    )(*parts, inner, dy, wdt, vec, masks)


def gate_values(y, gate):
    s = sig(gate)
    return y * (gate * s), y * (s * (1.0 + gate * (1.0 - s)))


def gate_back_body(y_ref, gate_ref, dgated_ref, gated_near, gated_far, dgate_near, dgate_far):
    half = gated_near.shape[1]
    for h, (gated, dgate) in enumerate([(gated_near, dgate_near), (gated_far, dgate_far)]):
        for b in range(half // LANES):
            cols = slice(b * LANES, (b + 1) * LANES)
            at = slice(h * half + b * LANES, h * half + (b + 1) * LANES)
            one, two = gate_values(y_ref[:, at], gate_ref[:, at])
            gated[:, cols] = one.astype(BF)
            dgate[:, cols] = (dgated_ref[:, at] * two).astype(BF)


def gate_back(n_slots, y, gate, dgated):
    rows, channels = y.shape
    length = rows // n_slots
    side = shape((rows, channels // 2), BF)
    return call(
        gate_back_body,
        (side,) * 4,
        grid=(n_slots,),
        in_specs=[pl.BlockSpec((length, channels), lambda j: (j, 0))] * 3,
        out_specs=[pl.BlockSpec((length, channels // 2), lambda j: (j, 0))] * 4,
        cost_estimate=cost(3e9),
    )(y, gate, dgated)


def conv_bwd_body(n_slots, p0, p1, p2, p3, x_ref, inner, dstate, mask_ref, vec_ref, wdk_ref,
                  dx_near, dx_far, dsmall_out, dvec_out, pad_ref, late_ref, dcat):
    j = pl.program_id(0)
    length, channels = x_ref.shape
    lane = lax.broadcasted_iota(jnp.int32, (1, LANES), 1)

    @pl.when(j == 0)
    def _():
        dsmall_out[...] = jnp.zeros(dsmall_out.shape, F32)
        dvec_out[...] = jnp.zeros(dvec_out.shape, F32)

    low_rank = jnp.zeros((length, RANK), F32)
    kq = jnp.zeros((length, LANES), F32)
    for d, part in enumerate((p0, p1, p2, p3)):
        rows = pl.ds(pl.multiple_of((j ^ d) * length, length), length)
        low_rank = low_rank + part[rows, :RANK].astype(F32)
        kq = kq + part[rows, RANK:].astype(F32)
    kq = kq + pltpu.roll(kq, 64, axis=1)
    dcat[:, :RANK] = low_rank.astype(BF)
    dcat[:, RANK:] = jnp.where(lane < 2 * STATE, kq, 0.0).astype(BF)
    dsmall_out[...] += dot(dcat[...], inner[...], 0, 0)
    late_ref[length : length + ROWS, :] = jnp.zeros((ROWS, LANES), F32)
    for b in range(channels // LANES):
        cols = slice(b * LANES, (b + 1) * LANES)
        c, earlier = conv_of(x_ref, slice(0, length), pad_ref, mask_ref, vec_ref, cols)
        dinner = dstate[:, cols] + dot(dcat[...], wdk_ref[:, cols], 1, 0)
        s = sig(c)
        dc = dinner * (s * (1.0 + c * (1.0 - s)))
        dx = vec_ref[0:1, cols] * dc
        sums = [jnp.sum(dc * x_ref[:, cols], axis=0, keepdims=True)]
        for lag in (1, 2, 3):
            sums.append(jnp.sum(dc * earlier[lag - 1], axis=0, keepdims=True))
            late_ref[0:length, :] = dc * mask_ref[:, lag * LANES : (lag + 1) * LANES]
            dx = dx + vec_ref[lag : lag + 1, cols] * late_ref[lag : lag + length, :]
        sums.append(jnp.sum(dc, axis=0, keepdims=True))
        half = channels // 2
        dx_out = dx_near if b * LANES < half else dx_far
        dx_out[:, (b * LANES) % half : (b * LANES) % half + LANES] = dx.astype(BF)
        for i, value in enumerate(sums):
            dvec_out[i : i + 1, cols] += value


def conv_bwd(parts, x, inner, dstate, masks, vec, wdk):
    rows, channels = x.shape
    n_slots = len(parts)
    length = rows // n_slots

    def whole(a):
        return pl.BlockSpec(a.shape, lambda i: (0,) * a.ndim)

    slot = pl.BlockSpec((length, channels), lambda j: (j, 0))
    slot_half = pl.BlockSpec((length, channels // 2), lambda j: (j, 0))
    side = shape((rows, channels // 2), BF)
    small = shape((2 * LANES, channels), F32)
    vecs = shape((ROWS, channels), F32)
    return call(
        partial(conv_bwd_body, n_slots),
        (side, side, small, vecs),
        grid=(n_slots,),
        in_specs=[whole(p) for p in parts]
        + [slot, slot, slot, pl.BlockSpec((length, 4 * LANES), lambda j: (j, 0)), whole(vec), whole(wdk)],
        out_specs=(slot_half, slot_half, whole(small), whole(vecs)),
        scratch_shapes=[
            pltpu.VMEM((ROWS + length, LANES), F32),
            pltpu.VMEM((ROWS + length, LANES), F32),
            pltpu.VMEM((length, 2 * LANES), BF),
        ],
    )(*parts, x, inner, dstate, masks, vec, wdk)


SMALL = 448
DOWN, KQ, DT, VEC = 0, 128, 160, 288


def cut_small_body(where_ref, w_ref, gain_ref, *refs):
    sources, (keep_ref, send_ref, small), fetched, sems = refs[:7], refs[7:10], refs[10:17], refs[17]
    i = pl.program_id(0)
    rows, sub = w_ref.shape[0], keep_ref.shape[1]
    part = keep_ref.shape[0] - rows
    copies = [pltpu.make_async_copy(v, f, sems.at[n]) for n, (v, f) in enumerate(zip(sources, fetched))]

    @pl.when(i == 0)
    def _():
        for copy in copies:
            copy.start()

    mine = where_ref[1] == 0
    scaled = w_ref[...].astype(F32) * gain_ref[...]
    first, second = scaled[:, :sub].astype(BF), scaled[:, sub:].astype(BF)
    keep_ref[0:rows, :] = jnp.where(mine, first, second)
    send_ref[0:rows, :] = jnp.where(mine, second, first)

    @pl.when(i == 0)
    def _():
        for copy in copies:
            copy.wait()
        down, kq, dt, conv, conv_bias, dt_bias, skip = fetched
        at = pl.ds(pl.multiple_of(where_ref[0] * 2 * sub, 2 * sub), 2 * sub)
        small[DOWN:KQ, :] = down[at, :].astype(F32).T.astype(BF)
        small[KQ:DT, :] = kq[:, at]
        small[DT:VEC, :] = dt[:, at]
        last = [v[:, at].astype(F32) for v in (conv, conv_bias, dt_bias, skip)] + [jnp.zeros((9, 2 * sub), F32)]
        small[VEC : VEC + 16, :] = jnp.concatenate(last, axis=0).astype(BF)
        small[VEC + 16 :, :] = jnp.zeros((SMALL - VEC - 16, 2 * sub), BF)

    piece = small[pl.ds(pl.multiple_of(i * part, 16), part), :]
    first, second = piece[:, :sub], piece[:, sub:]
    keep_ref[rows:, :] = jnp.where(mine, first, second)
    send_ref[rows:, :] = jnp.where(mine, second, first)


def cut_small(where, weight, gain, down, kq, dt, conv, conv_bias, dt_bias, skip, n_dp, n_grp, sub):
    rows = weight.shape[0]
    part = SMALL // n_dp
    out = shape((rows + part, n_dp * sub), BF)
    smalls = [down, kq, dt, conv, conv_bias, dt_bias, skip]
    return call(
        cut_small_body,
        (out, out),
        grid_spec=pltpu.PrefetchScalarGridSpec(
            num_scalar_prefetch=1,
            grid=(n_dp,),
            in_specs=[
                pl.BlockSpec((rows, 2 * sub), lambda i, w: (0, i * n_grp + w[0])),
                pl.BlockSpec((rows, 1), lambda i, w: (0, 0)),
            ]
            + [pl.BlockSpec(memory_space=pltpu.HBM)] * 7,
            out_specs=[pl.BlockSpec((rows + part, sub), lambda i, w: (0, i))] * 2,
            scratch_shapes=[pltpu.VMEM((SMALL, 2 * sub), BF)]
            + [pltpu.VMEM(v.shape, BF) for v in smalls]
            + [pltpu.SemaphoreType.DMA((7,))],
        ),
        cost_estimate=cost(3e9),
    )(where, weight, gain, *smalls)


def cut_out_body(where_ref, w_ref, gain_ref, o_ref, keep_ref, send_ref):
    i = pl.program_id(0)
    rows, sub = w_ref.shape[0], keep_ref.shape[1]
    mine = where_ref[1] == 0
    scaled = w_ref[...].astype(F32) * gain_ref[...]
    first, second = scaled[:, :sub].astype(BF), scaled[:, sub:].astype(BF)
    keep_ref[0:rows, :] = jnp.where(mine, first, second)
    send_ref[0:rows, :] = jnp.where(mine, second, first)
    n = pl.num_programs(0)
    wide = o_ref.shape[1] // 4
    for c in range(4):
        lanes = pl.ds(pl.multiple_of(c * wide + i * sub, sub), sub)
        first, second = o_ref[0:sub, lanes], o_ref[sub:, lanes]
        at = slice(rows + c * sub, rows + (c + 1) * sub)
        keep_ref[at, :] = jnp.where(mine, first, second)
        send_ref[at, :] = jnp.where(mine, second, first)


def cut_out(where, weight, gain, out_weight, n_dp, n_grp, sub):
    rows = weight.shape[0]
    out = shape((rows + 4 * sub, n_dp * sub), BF)
    return call(
        cut_out_body,
        (out, out),
        grid_spec=pltpu.PrefetchScalarGridSpec(
            num_scalar_prefetch=1,
            grid=(n_dp,),
            in_specs=[
                pl.BlockSpec((rows, 2 * sub), lambda i, w: (0, (n_dp + i) * n_grp + w[0])),
                pl.BlockSpec((rows, 1), lambda i, w: (0, 0)),
                pl.BlockSpec((2 * sub, out_weight.shape[1]), lambda i, w: (w[0], 0)),
            ],
            out_specs=[pl.BlockSpec((rows + 4 * sub, sub), lambda i, w: (0, i))] * 2,
        ),
        cost_estimate=cost(3e9),
    )(where, weight, gain, out_weight)


def flat_call(body, out_shape, arrays, specs=None, scratch=(), flops=0, vmem=48):
    def whole(v):
        return pl.BlockSpec(v.shape, lambda i: (0,) * len(v.shape))

    outs = out_shape if isinstance(out_shape, tuple) else (out_shape,)
    out_specs = tuple(whole(v) for v in outs)
    return call(
        body,
        out_shape,
        grid=(1,),
        in_specs=[(specs or {}).get(n, whole(v)) for n, v in enumerate(arrays)],
        out_specs=out_specs if isinstance(out_shape, tuple) else out_specs[0],
        scratch_shapes=list(scratch),
        cost_estimate=cost(flops),
        vmem=vmem,
    )(*arrays)


def q_block(q, which, rows):
    return pl.BlockSpec((q.shape[0], rows, q.shape[2]), lambda i: (0, which, 0))


def blocks_sum(a_ref, w_ref, rows):
    total = None
    for p in range(w_ref.shape[0]):
        term = dot(a_ref[:, p * rows : (p + 1) * rows], w_ref[p, 0:rows, :], 1, 0)
        total = term if total is None else total + term
    return total


def first_body(n_slots, rows, a_ref, mask_ref, near_ref, far_ref, *refs):
    x_ref, inner_ref, part_ref, cat_ref, wdt_ref, vec_ref, pad_ref, small = refs
    half = x_ref.shape[1] // 2
    n_dp = near_ref.shape[0]
    sub = half // n_dp
    length = x_ref.shape[0] // n_slots
    part = SMALL // n_dp
    for h, w_ref in enumerate((near_ref, far_ref)):
        for p in range(n_dp):
            lanes = slice(h * half + p * sub, h * half + (p + 1) * sub)
            for i in range(n_dp):
                small[i * part : (i + 1) * part, lanes] = w_ref[p, rows:, i * sub : (i + 1) * sub]
    cat_ref[0:DT, :] = small[0:DT, :]
    cat_ref[DT:, :] = jnp.zeros((cat_ref.shape[0] - DT, 2 * half), BF)
    wdt_ref[...] = small[DT:VEC, :]
    vec_ref[...] = small[VEC : VEC + 16, :].astype(F32)
    both = jnp.zeros((x_ref.shape[0], 2 * LANES), F32)
    for h, w_ref in enumerate((near_ref, far_ref)):
        lanes = slice(h * half, (h + 1) * half)
        x_ref[:, lanes] = blocks_sum(a_ref, w_ref, rows)
        for j in range(n_slots):
            at = slice(j * length, (j + 1) * length)
            for b in range(half // LANES):
                cols = slice(h * half + b * LANES, h * half + (b + 1) * LANES)
                c, _ = conv_of(x_ref, at, pad_ref, mask_ref, vec_ref, cols)
                inner_ref[at, cols] = (c * sig(c)).astype(BF)
        both = both + dot(inner_ref[:, lanes], cat_ref[:, lanes], 1, 1)
    part_ref[...] = pack(both[:, :RANK], both[:, RANK:])


def first_products(n_slots, a, masks, near, far, rows):
    n, half = a.shape[0], near.shape[2]
    return flat_call(
        partial(first_body, n_slots, rows),
        (
            shape((n, 2 * half), F32),
            shape((n, 2 * half), BF),
            shape((n, 2 * LANES), BF),
            shape((2 * LANES, 2 * half), BF),
            shape((RANK, 2 * half), BF),
            shape((16, 2 * half), F32),
        ),
        [a, masks, near, far],
        scratch=[pltpu.VMEM((ROWS + n // n_slots, LANES), F32), pltpu.VMEM((SMALL, 2 * half), BF)],
        flops=8e9,
    )


def gate_body(rows, a_ref, y_ref, near_ref, far_ref, gate_ref, gated_near, gated_far):
    half = gated_near.shape[1]
    for h, (w_ref, gated) in enumerate([(near_ref, gated_near), (far_ref, gated_far)]):
        at = slice(h * half, (h + 1) * half)
        gate = blocks_sum(a_ref, w_ref, rows)
        gate_ref[:, at] = gate
        gated[...] = (y_ref[:, at] * (gate * sig(gate))).astype(BF)


def gate_product(a, y, near, far, rows):
    half = near.shape[2]
    side = shape((a.shape[0], half), BF)
    return flat_call(
        partial(gate_body, rows),
        (shape(y.shape, F32), side, side),
        [a, y, near, far],
        specs={2: q_block(near, 0, rows), 3: q_block(far, 0, rows)},
        flops=6e9,
    )


def out_weight_of(near_ref, far_ref, w_scr):
    half = w_scr.shape[0] // 2
    n_dp = near_ref.shape[0]
    sub = half // n_dp
    wide = w_scr.shape[1] // 4
    for h, w_ref in enumerate((near_ref, far_ref)):
        for p in range(n_dp):
            for c in range(4):
                block = w_ref[p, c * sub : (c + 1) * sub, :]
                w_scr[h * half + p * sub : h * half + (p + 1) * sub, c * wide : (c + 1) * wide] = block


def branch_body(left_near, left_far, near_ref, far_ref, out_ref, w_scr):
    out_weight_of(near_ref, far_ref, w_scr)
    half = left_near.shape[1]
    wide = w_scr.shape[1] // 4
    for c in range(4):
        lanes = slice(c * wide, (c + 1) * wide)
        total = dot(left_near[...], w_scr[:half, lanes], 1, 0) + dot(left_far[...], w_scr[half:, lanes], 1, 0)
        out_ref[:, lanes] = total.astype(BF)


def branch_product(left_near, left_far, near, far, rows):
    half = near.shape[2]
    return flat_call(
        branch_body,
        shape((left_near.shape[0], 4 * half), BF),
        [left_near, left_far, near, far],
        specs={2: q_block(near, 1, rows), 3: q_block(far, 1, rows)},
        scratch=[pltpu.VMEM((2 * half, 4 * half), BF)],
        flops=5e9,
    )


def dgated_body(d_ref, y_ref, gate_ref, near_ref, far_ref, dy_ref, dgate_near, dgate_far, w_scr):
    out_weight_of(near_ref, far_ref, w_scr)
    half = dgate_near.shape[1]
    for h, dgate in enumerate((dgate_near, dgate_far)):
        at = slice(h * half, (h + 1) * half)
        dgated = dot(d_ref[...], w_scr[at, :], 1, 1)
        gate = gate_ref[:, at]
        dy_ref[:, at] = dgated * (gate * sig(gate))
        dgate[...] = (dgated * gate_values(y_ref[:, at], gate)[1]).astype(BF)


def dgated_product(dbranch, y, gate, near, far, rows):
    half = near.shape[2]
    side = shape((dbranch.shape[0], half), BF)
    return flat_call(
        dgated_body,
        (shape(y.shape, F32), side, side),
        [dbranch, y, gate, near, far],
        specs={3: q_block(near, 1, rows), 4: q_block(far, 1, rows)},
        scratch=[pltpu.VMEM((2 * half, dbranch.shape[1]), BF)],
        flops=6e9,
    )


def dnormed_body(rows, dx_near, dx_far, dg_near, dg_far, p_near, p_far, q_near, q_far, out_ref):
    for p in range(p_near.shape[0]):
        total = dot(dx_near[...], p_near[p, 0:rows, :], 1, 1) + dot(dx_far[...], p_far[p, 0:rows, :], 1, 1)
        total = total + dot(dg_near[...], q_near[p], 1, 1) + dot(dg_far[...], q_far[p], 1, 1)
        out_ref[:, p * rows : (p + 1) * rows] = total.astype(BF)


def dnormed_product(lefts, p_near, p_far, q_near, q_far, rows):
    n_dp = p_near.shape[0]
    return flat_call(
        partial(dnormed_body, rows),
        shape((lefts[0].shape[0], n_dp * rows), BF),
        [*lefts, p_near, p_far, q_near, q_far],
        specs={6: q_block(q_near, 0, rows), 7: q_block(q_far, 0, rows)},
        flops=8e9,
    )


def grad_p_body(a_ref, a_far, dx_ref, dx_come, small_ref, small_come, out_ref):
    rows = a_ref.shape[1]
    value = dot(a_ref[...], dx_ref[...], 0, 0) + dot(a_far[...], dx_come[...], 0, 0)
    out_ref[0, 0:rows, :] = value.astype(BF)
    out_ref[0, rows:, :] = (small_ref[...] + small_come[...].astype(F32)).astype(BF)


def grad_p(a, a_far, dx, dx_come, small, small_come, n_dp):
    rows = a.shape[1] // n_dp
    part = small.shape[0] // n_dp
    half = dx.shape[1]
    col = pl.BlockSpec((a.shape[0], rows), lambda i: (0, i))
    whole = pl.BlockSpec(dx.shape, lambda i: (0, 0))
    block = pl.BlockSpec((part, half), lambda i: (i, 0))
    return call(
        grad_p_body,
        shape((n_dp, rows + part, half), BF),
        grid=(n_dp,),
        in_specs=[col, col, whole, whole, block, block],
        out_specs=pl.BlockSpec((1, rows + part, half), lambda i: (i, 0, 0)),
        cost_estimate=cost(5e9),
    )(a, a_far, dx, dx_come, small, small_come)


def grad_q_body(a_ref, a_far, dg_ref, dg_come, gated_ref, gated_come, db_ref, db_far, out_ref):
    rows = a_ref.shape[1]
    sub = gated_ref.shape[1]
    wide = db_ref.shape[1] // 4
    value = dot(a_ref[...], dg_ref[...], 0, 0) + dot(a_far[...], dg_come[...], 0, 0)
    out_ref[0, 0:rows, :] = value.astype(BF)
    value = dot(gated_ref[...], db_ref[...], 0, 0) + dot(gated_come[...], db_far[...], 0, 0)
    for c in range(4):
        out_ref[0, rows + c * sub : rows + (c + 1) * sub, :] = value[:, c * wide : (c + 1) * wide].astype(BF)


def grad_q(a, a_far, dg, dg_come, gated, gated_come, db, db_far, n_dp):
    rows = a.shape[1] // n_dp
    half = dg.shape[1]
    sub = half // n_dp
    col = pl.BlockSpec((a.shape[0], rows), lambda i: (0, i))
    sub_col = pl.BlockSpec((a.shape[0], sub), lambda i: (0, i))

    def whole(v):
        return pl.BlockSpec(v.shape, lambda i: (0, 0))

    return call(
        grad_q_body,
        shape((n_dp, rows + 4 * sub, half), BF),
        grid=(n_dp,),
        in_specs=[col, col, whole(dg), whole(dg), sub_col, sub_col, whole(db), whole(db)],
        out_specs=pl.BlockSpec((1, rows + 4 * sub, half), lambda i: (i, 0, 0)),
        cost_estimate=cost(8e9),
    )(a, a_far, dg, dg_come, gated, gated_come, db, db_far)


def small_grads_body(dsmall, ddt, dconv, dvec, near_ref, far_ref, scr):
    half = near_ref.shape[1]
    sub = half // 4
    part = SMALL // 4
    scr[DOWN:DT, :] = dsmall[0:DT, :]
    scr[DT:VEC, :] = ddt[...]
    rows = [dconv[0:5, :], dvec[0:2, :], jnp.zeros((1, 2 * half), F32)]
    scr[VEC : VEC + 8, :] = jnp.concatenate(rows, axis=0)
    scr[VEC + 8 :, :] = jnp.zeros((SMALL - VEC - 8, 2 * half), F32)
    for block in range(4):
        at = slice(block * part, (block + 1) * part)
        for i in range(4):
            rows = slice(i * part, (i + 1) * part)
            lanes = slice(i * sub, (i + 1) * sub)
            near_ref[at, lanes] = scr[rows, block * sub : (block + 1) * sub]
            far_ref[at, lanes] = scr[rows, half + block * sub : half + (block + 1) * sub].astype(BF)


def small_grads(dsmall, ddt, dconv, dvec):
    half = ddt.shape[1] // 2
    return call(
        small_grads_body,
        (shape((SMALL, half), F32), shape((SMALL, half), BF)),
        scratch_shapes=[pltpu.VMEM((SMALL, 2 * half), F32)],
        cost_estimate=cost(2e9),
    )(dsmall, ddt, dconv, dvec)


def join_values(n_grp, where_ref, parts):
    mine = where_ref[1] == 0
    for d in range(n_grp):
        for h in (0, 1):
            sub = parts[0].shape[2]
            at = pl.ds(pl.multiple_of(((where_ref[0] ^ d) * 2 + h) * sub, sub), sub)
            yield at, jnp.where(mine, parts[d][h], parts[n_grp + d][h]).astype(F32)


def join_p_body(n_grp, n_dp, where_ref, w_ref, gain_ref, *refs):
    parts = refs[: 2 * n_grp]
    out_ref, sum_ref, down_ref, kq_ref, dt_ref, conv_ref, cb_ref, db_ref, skip_ref, small = refs[2 * n_grp + 1 :]
    i = pl.program_id(0)
    rows, sub = w_ref.shape[0], parts[0].shape[2]
    part = parts[0].shape[1] - rows

    @pl.when(i == 0)
    def _():
        sum_ref[...] = jnp.zeros(sum_ref.shape, F32)

    for at, value in join_values(n_grp, where_ref, parts):
        out_ref[:, at] = value[:rows] * gain_ref[...]
        sum_ref[...] += value[:rows] * w_ref[:, at].astype(F32)
        small[pl.ds(pl.multiple_of(i * part, 16), part), at] = value[rows:]

    @pl.when(i == n_dp - 1)
    def _():
        for b in range(down_ref.shape[0] // LANES):
            at = slice(b * LANES, (b + 1) * LANES)
            down_ref[at, :] = small[DOWN:KQ, at].T
        kq_ref[...] = small[KQ:DT, :]
        dt_ref[...] = small[DT:VEC, :]
        conv_ref[...] = small[VEC : VEC + 4, :]
        cb_ref[...] = small[VEC + 4 : VEC + 5, :]
        db_ref[...] = small[VEC + 5 : VEC + 6, :]
        skip_ref[...] = small[VEC + 6 : VEC + 7, :]


def join_q_body(n_grp, n_dp, where_ref, w_ref, gain_ref, *refs):
    parts, out_ref, sum_ref, o_ref = refs[: 2 * n_grp], refs[-3], refs[-2], refs[-1]
    i = pl.program_id(0)
    rows, sub = w_ref.shape[0], parts[0].shape[2]
    wide = o_ref.shape[1] // 4

    @pl.when(i == 0)
    def _():
        sum_ref[...] = jnp.zeros(sum_ref.shape, F32)

    for at, value in join_values(n_grp, where_ref, parts):
        out_ref[:, at] = value[:rows] * gain_ref[...]
        sum_ref[...] += value[:rows] * w_ref[:, at].astype(F32)
        for c in range(4):
            lanes = pl.ds(pl.multiple_of(c * wide + i * sub, sub), sub)
            o_ref[at, lanes] = value[rows + c * sub : rows + (c + 1) * sub]


def join_packed(body, where, weight, gain, parts, before, side, n_dp, extras, scratch=()):
    rows = weight.shape[0]
    n_grp = len(parts) // 2
    sub = parts[0].shape[2] // n_dp
    wide = 2 * n_grp * sub
    dims = (2, parts[0].shape[1], sub)
    mine = pl.BlockSpec(dims, lambda i, w: (0, 0, i * (1 - w[1])))
    other = pl.BlockSpec(dims, lambda i, w: (0, 0, i * w[1]))
    last = [] if before is None else [before]
    return call(
        partial(body, n_grp, n_dp),
        (shape(weight.shape, F32), shape((rows, sub), F32), *extras),
        grid_spec=pltpu.PrefetchScalarGridSpec(
            num_scalar_prefetch=1,
            grid=(n_dp,),
            in_specs=[
                pl.BlockSpec((rows, wide), lambda i, w: (0, side * n_dp + i)),
                pl.BlockSpec((rows, 1), lambda i, w: (0, 0)),
            ]
            + [mine] * n_grp
            + [other] * n_grp
            + [pl.BlockSpec(memory_space=pl.ANY)] * len(last),
            out_specs=[
                pl.BlockSpec((rows, wide), lambda i, w: (0, side * n_dp + i)),
                pl.BlockSpec((rows, sub), lambda i, w: (0, 0)),
            ]
            + [pl.BlockSpec(v.shape, lambda i, w: (0, 0)) for v in extras],
            scratch_shapes=list(scratch),
        ),
        input_output_aliases={3 + len(parts): 0} if last else {},
        cost_estimate=cost(8e9),
    )(where, weight, gain, *parts, *last)


def rms_of(hidden):
    return lax.rsqrt(jnp.mean(hidden * hidden, axis=1, keepdims=True) + EPSILON)


def slot_masks(lengths, length):
    ends = jnp.cumsum(lengths, axis=1)
    position = jnp.arange(length, dtype=jnp.int32)
    segment = jnp.sum((position[None, :, None] >= ends[:, None, :]).astype(jnp.int32), axis=2)
    valid = (position[None, :] < ends[:, -1:]).astype(F32)
    same = []
    for lag in (1, 2, 3):
        before = jnp.concatenate([jnp.full((segment.shape[0], lag), -1, jnp.int32), segment[:, :-lag]], axis=1)
        same.append((before == segment).astype(F32))
    stack = jnp.stack([same[0]] + same, axis=2).reshape(-1, 4, 1)
    spread = jnp.broadcast_to(stack, stack.shape[:2] + (LANES,)).reshape(-1, 4 * LANES)
    return spread, valid


def everywhere(value, axis):
    return lax.all_gather(value, "dp", axis=axis, tiled=True)


def after(value, *others):
    return lax.optimization_barrier((value, *others))[0]


def on_any_line(boundary, doc_lengths, norm_gain, in_weight, conv_weight, conv_bias, down_weight, kq_weight,
              dt_weight, dt_bias, skip_weight, out_weight):
    s = lax.axis_index("section")
    g = lax.axis_index("grp")
    n_grp = lax.axis_size("grp")
    n_dp = lax.axis_size("dp")
    length, width = boundary.shape[3], boundary.shape[4]
    inner = in_weight.shape[2] // 2
    block = inner // n_dp
    sub = block // (2 * n_grp)
    half = sub * n_dp
    mine_first = s == 0
    gain = norm_gain[0].astype(F32)[:, None]

    def pick(first, second):
        return jnp.where(mine_first, first, second)

    rows = boundary[0, :, 0]
    traded = swap(pick(rows[1], rows[0]), "section", 1)
    hidden = pick(rows[0], traded)
    cotangent = pick(traded, rows[1])
    lengths = lax.dynamic_index_in_dim(doc_lengths[:, 0], s, 0, keepdims=True)
    all_lengths = jnp.concatenate([lengths] + peers(lengths), axis=0)
    masks, valid = slot_masks(all_lengths, length)
    valid = valid[0][:, None]

    def columns(array):
        blocks = array.shape[1] // block
        view = array.reshape(array.shape[0], blocks, n_grp, 2, sub)
        view = lax.dynamic_index_in_dim(view, g, 2, keepdims=False)
        halves = [view[:, :, h].reshape(array.shape[0], blocks * sub) for h in (0, 1)]
        return pick(*halves), pick(halves[1], halves[0])

    def side(which):
        part = in_weight[0, :, which * inner : (which + 1) * inner]
        return columns((part.astype(F32) * gain).astype(BF))

    def out_side():
        view = lax.dynamic_slice_in_dim(out_weight[0], g * 2 * sub, 2 * sub, 0)
        return pick(view[:sub], view[sub:]), pick(view[sub:], view[:sub])

    def small_side():
        def lanes(array):
            return lax.dynamic_slice_in_dim(array, g * 2 * sub, 2 * sub, 1)

        down = lax.dynamic_slice_in_dim(down_weight[0], g * 2 * sub, 2 * sub, 0).T
        view = jnp.concatenate(
            [down, lanes(kq_weight[0]), jnp.zeros((2 * LANES - RANK - 2 * STATE, 2 * sub), BF), lanes(dt_weight[0]),
             lanes(conv_weight[0]), lanes(conv_bias), lanes(dt_bias), lanes(skip_weight)], axis=0)
        return pick(view[:, :sub], view[:, sub:]), pick(view[:, sub:], view[:, :sub])

    def two_layers(keep, send):
        come = swap(send, "section", 1)
        return pick(keep, come), pick(come, keep)

    x_sides, s_sides = two_layers(*side(0)), two_layers(*small_side())
    g_sides, o_sides = two_layers(*side(1)), two_layers(*out_side())

    def with_far(near):
        return near, swap(near, "section", 1)

    layers = []
    for l in (0, 1):
        w_s = jnp.concatenate(with_far(everywhere(s_sides[l], 1)), axis=1)
        w_x = with_far(everywhere(x_sides[l], 0))
        w_g = with_far(everywhere(g_sides[l], 0))
        w_o = with_far(everywhere(o_sides[l], 0))
        cat = w_s[: 2 * LANES]
        wdt = w_s[2 * LANES : 2 * LANES + RANK]
        tail = w_s[2 * LANES + RANK :].astype(F32)
        vec = jnp.concatenate([tail, jnp.zeros((9, tail.shape[1]), F32)], axis=0)
        layers.append((w_x, w_g, w_o, cat, wdt, vec))

    def group(value):
        return jnp.concatenate([value] + peers(value), axis=0)

    def scatter(value):
        total = value[:length].astype(F32)
        for d in range(1, n_grp):
            total = total + swap(value[d * length : (d + 1) * length], "grp", d).astype(F32)
        return total

    def forward(h, layer):
        w_x, w_g, w_o, cat, wdt, vec = layer
        a = group((h * rms_of(h)).astype(BF))
        x, act, part = proj_conv(n_grp, a, *w_x, masks, vec, cat)
        gate = proj(a, *w_g, 0)
        return a, x, gate, act, [part] + peers(part)

    def gated_back(saved, layer, dgated, y, rec_out):
        gate = saved[2]
        if y is None:
            y = rec_out[5]
        return gate_back(n_grp, y, gate, dgated) + tuple(rec_out)

    def backward(h, dout, dbranch, layer, saved, rec_out):
        w_x, w_g, w_o, cat, wdt, vec = layer
        a, x, gate, act, parts = saved
        gated_near, gated_far, dgate_near, dgate_far, lr, dstate, dpart, ddt, dvec = rec_out[:9]
        dx_near, dx_far, dsmall, dconv = conv_bwd([dpart] + peers(dpart), x, act, dstate, masks, vec, cat)
        scaled = scatter(total_of([dx_near, dx_far, dgate_near, dgate_far], [*w_x, *w_g], 1))
        rms = rms_of(h)
        own = h * rms
        dh = dout + rms * (scaled - own * jnp.mean(scaled * own, axis=1, keepdims=True))

        a_far, dbranch_far = swap(a, "section", 1), swap(dbranch, "section", 1)
        dgate_come, gated_come = swap(dgate_far, "section", 1), swap(gated_far, "section", 1)
        dx_come = swap(dx_far, "section", 1)

        def both(left, right, left_come, right_come):
            return (dot(left, right, 0, 0) + dot(left_come, right_come, 0, 0)).astype(BF)

        grad_g = both(a, dgate_near, a_far, dgate_come)
        grad_o = both(gated_near, dbranch, gated_come, dbranch_far)
        grad_x = both(a, dx_near, a_far, dx_come)
        grad_s = jnp.concatenate([dsmall, ddt, dconv[:5], dvec[:2], jnp.zeros((1, ddt.shape[1]), F32)], axis=0)
        grad_s = grad_s[:, :half] + swap(grad_s[:, half:].astype(BF), "section", 1).astype(F32)
        grad_o = jnp.concatenate([grad_o, grad_s.T.astype(BF)], axis=1)
        return dh, (grad_g, grad_o, grad_x)

    h0 = hidden.astype(F32)
    saved0 = forward(h0, layers[0])
    y0 = rec(saved0[4], saved0[3], None, layers[0][4], layers[0][5], masks, True)
    gated0 = gate_values(y0, saved0[2])[0].astype(BF)
    branch0 = scatter(total_of([gated0[:, :half], gated0[:, half:]], layers[0][2], 0))
    h1 = (h0 + valid * branch0).astype(BF).astype(F32)
    saved1 = forward(h1, layers[1])
    dout1 = cotangent.astype(F32)
    dbranch1 = group((valid * dout1).astype(BF))
    dgated1 = proj(dbranch1, *layers[1][2], 1)
    dy1 = gate_values(dgated1, saved1[2])[0]
    rec1 = rec(saved1[4], saved1[3], dy1, layers[1][4], layers[1][5], masks, True)
    rec1 = gated_back(saved1, layers[1], dgated1, None, rec1)
    branch1 = scatter(total_of(rec1[:2], layers[1][2], 0))
    out1 = h1 + valid * branch1
    dh1, grads1 = backward(h1, dout1, dbranch1, layers[1], saved1, rec1)
    dout0 = dh1.astype(BF).astype(F32)
    dbranch0 = group((valid * dout0).astype(BF))
    dgated0 = proj(dbranch0, *layers[0][2], 1)
    dy0 = gate_values(dgated0, saved0[2])[0]
    rec0 = rec(saved0[4], saved0[3], dy0, layers[0][4], layers[0][5], masks, False)
    rec0 = gated_back(saved0, layers[0], dgated0, y0, rec0)
    dh0, grads0 = backward(h0, dout0, dbranch0, layers[0], saved0, rec0)

    far = swap(pick(out1, dh0), "section", 1)
    result = pick(jnp.stack([dh0, far]), jnp.stack([far, out1]))
    result = result.reshape(1, 2, 1, length, width)

    def collected(l, grad):
        near = lax.psum_scatter(grad, "dp", scatter_dimension=0, tiled=True)
        far = directed(near, "section", [(1 - l, l)])
        halves = jnp.stack([near, far] if l == 0 else [far, near])
        out = [halves]
        for d in range(1, n_grp):
            pairs = [(l * n_grp + i, l * n_grp + (i ^ d)) for i in range(n_grp)]
            out.append(directed(halves, ("section", "grp"), pairs))
        return out

    (g1, o1, x1), (g0, o0, x0) = [[collected(l, grad) for grad in grads] for l, grads in ((1, grads1), (0, grads0))]

    def in_order(firsts, seconds):
        return jnp.stack([pick(a, b) for a, b in zip(firsts, seconds)])[jnp.arange(n_grp) ^ g]

    smalls = in_order([v[:, :, width:] for v in o0], [v[:, :, width:] for v in o1]).astype(F32)
    grad_small = smalls.transpose(3, 0, 1, 2).reshape(smalls.shape[3], block)
    sides = []
    for first, second in ((x0, x1), (g0, g1)):
        value = in_order(first, second).reshape(n_grp, 2, -1, n_dp, sub)
        sides.append(value.transpose(2, 3, 0, 1, 4).reshape(value.shape[2], inner))
    product = jnp.concatenate(sides, axis=1).astype(F32)
    grad_in = product * gain
    grad_gain = jnp.sum(product * in_weight[0].astype(F32), axis=1)
    grad_out = in_order([v[:, :, :width] for v in o0], [v[:, :, :width] for v in o1]).astype(F32).reshape(block, width)
    base = 2 * LANES + RANK
    return (
        result,
        grad_gain[None],
        grad_in[None],
        grad_small[None, base : base + 4],
        grad_small[base + 4][None],
        grad_small[:RANK].T[None],
        grad_small[None, RANK : RANK + 2 * STATE],
        grad_small[None, 2 * LANES : base],
        grad_small[base + 5][None],
        grad_small[base + 6][None],
        grad_out[None],
    )


def on_device(boundary, doc_lengths, norm_gain, in_weight, conv_weight, conv_bias, down_weight, kq_weight,
              dt_weight, dt_bias, skip_weight, out_weight):
    s = lax.axis_index("section")
    g = lax.axis_index("grp")
    n_grp = lax.axis_size("grp")
    n_dp = lax.axis_size("dp")
    length, width = boundary.shape[3], boundary.shape[4]
    inner = in_weight.shape[2] // 2
    block = inner // n_dp
    sub = block // (2 * n_grp)
    n_rows = width // n_dp
    mine_first = s == 0
    where = jnp.stack([g, s]).astype(jnp.int32)
    gain = norm_gain[0].astype(F32)[:, None]

    def pick(first, second):
        return jnp.where(mine_first, first, second)

    def section(value):
        return swap(value, "section", 1)

    def two_layers(keep, send):
        come = section(send)
        return pick(keep, come), pick(come, keep)

    def group(value):
        return jnp.concatenate([value] + peers(value), axis=0)

    def scatter(value):
        total = value[:length].astype(F32)
        come = [swap(value[d * length : (d + 1) * length], "grp", d) for d in range(1, n_grp)]
        for piece in come:
            total = total + piece.astype(F32)
        return total, come

    def line(value):
        return lax.all_gather(value, "dp", axis=0)

    p_sides = two_layers(*cut_small(where, in_weight[0], gain, down_weight[0], kq_weight[0], dt_weight[0],
                                    conv_weight[0], conv_bias, dt_bias, skip_weight, n_dp, n_grp, sub))
    p0 = line(p_sides[0])
    rows = boundary[0, :, 0]
    traded = section(pick(rows[1], rows[0]))
    hidden = pick(rows[0], traded)
    cotangent = pick(traded, rows[1])
    lengths = lax.dynamic_index_in_dim(doc_lengths[:, 0], s, 0, keepdims=True)
    all_lengths = jnp.concatenate([lengths] + peers(lengths), axis=0)
    masks, valid = slot_masks(all_lengths, length)
    valid = valid[0][:, None]
    h0 = hidden.astype(F32)
    a0_parts = peers((h0 * rms_of(h0)).astype(BF))
    a0 = jnp.concatenate([(h0 * rms_of(h0)).astype(BF)] + a0_parts, axis=0)
    q_sides = two_layers(*cut_out(where, in_weight[0], gain, out_weight[0], n_dp, n_grp, sub))
    p0_far = section(after(p0, q_sides[0], *a0_parts))
    q0 = line(after(q_sides[0], p0, a0))
    dout1 = cotangent.astype(F32)

    def input_gradient(h, dout, scaled):
        rms = rms_of(h)
        own = h * rms
        return dout + rms * (scaled - own * jnp.mean(scaled * own, axis=1, keepdims=True))

    def summed(grad):
        return lax.psum_scatter(grad, "dp", scatter_dimension=0, tiled=True)[0]

    def collected(l, near):
        far = directed(near, "section", [(1 - l, l)])
        halves = jnp.stack([near, far] if l == 0 else [far, near])
        out = [halves]
        for d in range(1, n_grp):
            pairs = [(l * n_grp + i, l * n_grp + (i ^ d)) for i in range(n_grp)]
            out.append(directed(halves, ("section", "grp"), pairs))
        return out

    def gradient_q(a, a_far, dbranch, dbranch_far, gated, gated_far, dgate, dgate_far):
        return grad_q(a, a_far, dgate, section(dgate_far), gated, section(gated_far), dbranch, dbranch_far, n_dp)

    def gradient_p(a, a_far, dx_near, dx_far, dsmall, ddt, dconv, dvec):
        small_near, small_far = small_grads(dsmall, ddt, dconv, dvec)
        return grad_p(a, a_far, dx_near, section(dx_far), small_near, section(small_far), n_dp)

    x0, act0, part0, cat0, wdt0, vec0 = first_products(n_grp, a0, masks, p0, p0_far, n_rows)
    parts0 = [part0] + peers(part0)
    y0 = rec(parts0, act0, None, wdt0, vec0, masks, True)
    dbranch1 = group(after((valid * dout1).astype(BF), y0))
    q0_far = section(after(q0, dbranch1))
    p1 = line(after(p_sides[1], q0, dbranch1))
    a0_far = section(after(a0, y0))
    gate0, gated0_near, gated0_far = gate_product(a0, y0, q0, q0_far, n_rows)
    branch0 = scatter(branch_product(gated0_near, gated0_far, q0, q0_far, n_rows))[0]
    h1 = (h0 + valid * branch0).astype(BF).astype(F32)

    p1_far = section(after(p1, h1))
    q1 = line(after(q_sides[1], p1, h1))
    a1 = group((h1 * rms_of(h1)).astype(BF))
    x1, act1, part1, cat1, wdt1, vec1 = first_products(n_grp, a1, masks, p1, p1_far, n_rows)
    parts1 = [part1] + peers(part1)
    a1_far = section(after(a1, part1))
    y1 = rec(parts1, act1, None, wdt1, vec1, masks, True)
    q1_far = section(after(q1, y1))
    dbranch1_far = section(after(dbranch1, y1))
    gate1, gated1_near, gated1_far = gate_product(a1, y1, q1, q1_far, n_rows)

    dy1, dgate1_near, dgate1_far = dgated_product(dbranch1, y1, gate1, q1, q1_far, n_rows)
    gq1 = gradient_q(a1, a1_far, dbranch1, dbranch1_far, gated1_near, gated1_far, dgate1_near, dgate1_far)
    sq1 = summed(gq1)
    branch1 = branch_product(gated1_near, gated1_far, q1, q1_far, n_rows)
    lr1, dstate1, dpart1, ddt1, dvec1 = rec(parts1, act1, after(dy1, gq1, branch1), wdt1, vec1, masks, False)
    out1 = h1 + valid * scatter(branch1)[0]
    dparts1 = [dpart1] + peers(dpart1)
    dstate1 = after(dstate1, out1)
    dx1_near, dx1_far, dsmall1, dconv1 = conv_bwd(dparts1, x1, act1, dstate1, masks, vec1, cat1)
    dnormed1 = dnormed_product(
        [dx1_near, dx1_far, dgate1_near, dgate1_far], p1, p1_far, q1, q1_far, n_rows)
    scaled1, come1 = scatter(dnormed1)
    dh1 = input_gradient(h1, dout1, scaled1)
    gp1 = gradient_p(a1, a1_far, after(dx1_near, come1[0]), dx1_far, dsmall1, ddt1, dconv1, dvec1)
    sp1 = summed(after(gp1, sq1))
    dout0 = dh1.astype(BF).astype(F32)
    dbranch0 = group((valid * dout0).astype(BF))

    q_parts1 = collected(1, after(sq1, dbranch0))
    dbranch0_far = section(dbranch0)
    dy0, dgate0_near, dgate0_far = dgated_product(after(dbranch0, gp1), y0, gate0, q0, q0_far, n_rows)
    gq0 = gradient_q(a0, a0_far, dbranch0, dbranch0_far, gated0_near, gated0_far, dgate0_near, dgate0_far)
    lr0, dstate0, dpart0, ddt0, dvec0 = rec(parts0, act0, after(dy0, gq0, sp1), wdt0, vec0, masks, False)
    p_parts1 = collected(1, sp1)
    sq0 = summed(after(gq0, sp1))
    dparts0 = [dpart0] + peers(dpart0)
    dstate0 = after(dstate0, *q_parts1, *p_parts1)
    dx0_near, dx0_far, dsmall0, dconv0 = conv_bwd(dparts0, x0, act0, dstate0, masks, vec0, cat0)
    gp0 = gradient_p(a0, a0_far, dx0_near, dx0_far, dsmall0, ddt0, dconv0, dvec0)
    sp0 = summed(after(gp0, sq0))
    q_parts0 = collected(0, sq0)
    dnormed0 = dnormed_product(
        [after(dx0_near, gp0), dx0_far, dgate0_near, dgate0_far], p0, p0_far, q0, q0_far, n_rows)
    p_parts0 = collected(0, after(sp0, dnormed0, *q_parts0))
    dh0 = input_gradient(h0, dout0, after(scatter(dnormed0)[0], p_parts0[0]))

    out_far = directed(out1, "section", [(0, 1)])
    dh_far = directed(dh0, "section", [(1, 0)])
    result = jnp.stack([pick(dh0, out_far), pick(dh_far, out1)]).reshape(1, 2, 1, length, width)

    grad_in, sum_q, grad_out = join_packed(
        join_q_body, where, in_weight[0], gain, q_parts0 + q_parts1, None, 1, n_dp, [shape((block, width), F32)])
    smalls = [shape(v, F32) for v in ((block, RANK), (2 * STATE, block), (RANK, block), (4, block))]
    smalls += [shape((1, block), F32)] * 3
    grad_in, sum_p, grad_down, grad_kq, grad_dt, grad_conv, grad_cb, grad_db, grad_skip = join_packed(
        join_p_body, where, in_weight[0], gain, p_parts0 + p_parts1, grad_in, 0, n_dp, smalls,
        [pltpu.VMEM((SMALL, block), F32)])
    grad_gain = jnp.sum(sum_q + sum_p, axis=1)
    return (
        result,
        grad_gain[None],
        grad_in[None],
        grad_conv[None],
        grad_cb,
        grad_down[None],
        grad_kq[None],
        grad_dt[None],
        grad_db,
        grad_skip,
        grad_out[None],
    )


def solution(mesh):
    packed = mesh.shape["dp"] == 4 and mesh.shape["grp"] == 4
    return jax.shard_map(
        on_device if packed else on_any_line,
        mesh=mesh,
        in_specs=(
            P("section", None, ("grp", "dp"), None, None),
            P(None, ("grp", "dp"), None),
            P("section", "dp"),
            P("section", "dp", None),
            P("section", None, "dp"),
            P("section", "dp"),
            P("section", "dp", None),
            P("section", None, "dp"),
            P("section", None, "dp"),
            P("section", "dp"),
            P("section", "dp"),
            P("section", "dp", None),
        ),
        out_specs=(
            P("section", None, ("grp", "dp"), None, None),
            P("section", "dp"),
            P("section", "dp", None),
            P("section", None, "dp"),
            P("section", "dp"),
            P("section", "dp", None),
            P("section", None, "dp"),
            P("section", None, "dp"),
            P("section", "dp"),
            P("section", "dp"),
            P("section", "dp", None),
        ),
        check_vma=False,
    )
```

```python
from functools import partial

import jax
import jax.numpy as jnp
from jax import lax
from jax.experimental import pallas as pl
from jax.experimental.pallas import tpu as pltpu
from jax.sharding import PartitionSpec as P

EPSILON = 1e-05
BF = jnp.bfloat16
F32 = jnp.float32
STATE = 16
RANK = 128
LANES = 128
ROWS = 8
MIB = 1024 * 1024


def dot(left, right, left_axis, right_axis, kind=F32):
    return lax.dot_general(
        left, right, (((left_axis,), (right_axis,)), ((), ())), preferred_element_type=kind
    )


def sig(value):
    return 1.0 / (1.0 + jnp.exp(-value))


def swap(value, axis, shift):
    return lax.ppermute(value, axis, [(i, i ^ shift) for i in range(lax.axis_size(axis))])


def directed(value, axis, pairs):
    return lax.ppermute(value, axis, pairs)


def peers(value):
    return [swap(value, "grp", d) for d in range(1, lax.axis_size("grp"))]


def call(body, out_shape, **kwargs):
    limit = kwargs.pop("vmem", 48)
    return pl.pallas_call(
        body,
        out_shape=out_shape,
        compiler_params=pltpu.CompilerParams(vmem_limit_bytes=limit * MIB),
        **kwargs,
    )


def cost(flops):
    return pl.CostEstimate(flops=int(1 * flops), bytes_accessed=0, transcendentals=0)


def shape(dims, kind):
    return jax.ShapeDtypeStruct(dims, kind)


def proj_body(a_ref, near_ref, far_ref, out_ref, *, w_axis):
    @pl.when(pl.program_id(0) == 0)
    def _():
        out_ref[...] = dot(a_ref[...], near_ref[...], 1, w_axis)

    @pl.when(pl.program_id(0) == 1)
    def _():
        out_ref[...] = dot(a_ref[...], far_ref[...], 1, w_axis)


def proj(a, near, far, w_axis):
    rows = a.shape[0]
    half = near.shape[1 - w_axis]

    def whole(v):
        return pl.BlockSpec(v.shape, lambda i: (0,) * v.ndim)

    return call(
        partial(proj_body, w_axis=w_axis),
        shape((rows, 2 * half), F32),
        grid=(2,),
        in_specs=[whole(a), whole(near), whole(far)],
        out_specs=pl.BlockSpec((rows, half), lambda i: (0, i)),
        cost_estimate=cost(4 * rows * half * a.shape[1]),
    )(a, near, far)


def total_body(n, w_axis, *refs):
    lefts, rights, out_ref = refs[:n], refs[n : 2 * n], refs[2 * n]
    total = dot(lefts[0][...], rights[0][...], 1, w_axis)
    for left, right in zip(lefts[1:], rights[1:]):
        total = total + dot(left[...], right[...], 1, w_axis)
    out_ref[...] = total.astype(BF)


def total_of(lefts, rights, w_axis):
    rows = lefts[0].shape[0]
    width = rights[0].shape[1 - w_axis]
    step = 512

    def left_spec(v):
        return pl.BlockSpec(v.shape, lambda i: (0, 0))

    def right_spec(v):
        if w_axis == 0:
            return pl.BlockSpec((v.shape[0], step), lambda i: (0, i))
        return pl.BlockSpec((step, v.shape[1]), lambda i: (i, 0))

    return call(
        partial(total_body, len(lefts), w_axis),
        shape((rows, width), BF),
        grid=(width // step,),
        in_specs=[left_spec(v) for v in lefts] + [right_spec(v) for v in rights],
        out_specs=pl.BlockSpec((rows, step), lambda i: (0, i)),
        cost_estimate=cost(2 * rows * width * sum(v.shape[1] for v in lefts)),
    )(*lefts, *rights)


def conv_of(x_ref, rows, pad_ref, mask_ref, vec_ref, cols):
    length = pad_ref.shape[0] - ROWS
    x = x_ref[rows, cols]
    pad_ref[0:ROWS, :] = jnp.zeros((ROWS, LANES), F32)
    pad_ref[ROWS : ROWS + length, :] = x
    total = vec_ref[4:5, cols] + vec_ref[0:1, cols] * x
    shifted = []
    for j in (1, 2, 3):
        earlier = pad_ref[ROWS - j : ROWS - j + length, :] * mask_ref[rows, j * LANES : (j + 1) * LANES]
        shifted.append(earlier)
        total = total + vec_ref[j : j + 1, cols] * earlier
    return total, shifted


def proj_conv_body(n_slots, a_ref, near_ref, far_ref, mask_ref, vec_ref, cat_ref, x_ref, inner_ref, part_ref,
                   pad_ref, sum_ref):
    i = pl.program_id(0)
    rows_all, half = x_ref.shape
    length = rows_all // n_slots

    @pl.when(i == 0)
    def _():
        x_ref[...] = dot(a_ref[...], near_ref[...], 1, 0)

    @pl.when(i == 1)
    def _():
        x_ref[...] = dot(a_ref[...], far_ref[...], 1, 0)

    for j in range(n_slots):
        rows = slice(j * length, (j + 1) * length)
        for b in range(half // LANES):
            cols = slice(b * LANES, (b + 1) * LANES)
            c, _ = conv_of(x_ref, rows, pad_ref, mask_ref, vec_ref, cols)
            inner_ref[rows, cols] = (c * sig(c)).astype(BF)
    both = dot(inner_ref[...], cat_ref[...], 1, 1)

    @pl.when(i == 0)
    def _():
        sum_ref[...] = both

    @pl.when(i == 1)
    def _():
        total = sum_ref[...] + both
        part_ref[...] = pack(total[:, :RANK], total[:, RANK:])


def proj_conv(n_slots, a, near, far, masks, vec, cat):
    rows = a.shape[0]
    half = near.shape[1]

    def whole(v):
        return pl.BlockSpec(v.shape, lambda i: (0,) * v.ndim)

    def block(n):
        return pl.BlockSpec((n, half), lambda i: (0, i))

    part_like = shape((rows, 2 * LANES), BF)
    return call(
        partial(proj_conv_body, n_slots),
        (shape((rows, 2 * half), F32), shape((rows, 2 * half), BF), part_like),
        grid=(2,),
        in_specs=[whole(a), whole(near), whole(far), whole(masks), block(vec.shape[0]), block(cat.shape[0])],
        out_specs=(block(rows), block(rows), whole(part_like)),
        scratch_shapes=[pltpu.VMEM((ROWS + rows // n_slots, LANES), F32), pltpu.VMEM((rows, 2 * LANES), F32)],
        cost_estimate=cost(4 * rows * half * a.shape[1]),
    )(a, near, far, masks, vec, cat)


def pack(low_rank, kq):
    high = kq.astype(BF).astype(F32)
    rest = pltpu.roll(kq - high, 64, axis=1)
    return jnp.concatenate([low_rank, high + rest], axis=1).astype(BF)


def summed_parts(parts, j, length):
    low_rank = jnp.zeros((length, RANK), F32)
    kq = jnp.zeros((length, LANES), F32)
    for d, part in enumerate(parts):
        rows = slice((j ^ d) * length, ((j ^ d) + 1) * length)
        low_rank = low_rank + part[rows, :RANK].astype(F32)
        kq = kq + part[rows, RANK:].astype(F32)
    kq = kq + pltpu.roll(kq, 64, axis=1)
    lane = lax.broadcasted_iota(jnp.int32, (1, LANES), 1)
    return low_rank, jnp.where(lane < 2 * STATE, kq, 0.0)


def rec_body(backward, keep_y, n_slots, length, width, *refs):
    parts, refs = refs[:n_slots], refs[n_slots:]
    y_out = None
    if backward:
        (inner, dy_ref, wdt, vec, mask, lr_out, dstate_out, dpart_out, ddt_out, dvec_out), refs = refs[:10], refs[10:]
        if keep_y:
            y_out, refs = refs[0], refs[1:]
        (kq_n, kq_i, c_i, lr_n, step_i, p_i, y_i, kb, str_n, hist, dy_i, a_i, h_scr, dkq_i,
         dlr_n, corr_n, prod, drate_n) = refs
    else:
        (inner, wdt, vec, mask, y_out, kq_n, kq_i, c_i, lr_n, step_i, p_i, y_i, kb, state) = refs
    nb = width // (2 * LANES)
    first = pl.program_id(0) == 0
    last = pl.program_id(0) == pl.num_programs(0) - 1
    lane = lax.broadcasted_iota(jnp.int32, (1, LANES), 1)
    pieces = [(hh, b, slice((hh * nb + b) * LANES, (hh * nb + b + 1) * LANES)) for hh in (0, 1) for b in range(nb)]

    def rows_of(j):
        return slice(j * length, (j + 1) * length)

    def spread(j, hh):
        return pl.ds(hh * n_slots + j, length, stride=ROWS)

    @pl.when(first)
    def _():
        for j in range(n_slots):
            low_rank, kq = summed_parts(parts, j, length)
            lr_n[rows_of(j), :] = low_rank.astype(BF)
            if backward:
                lr_out[rows_of(j), :] = low_rank.astype(BF)
            kq_n[rows_of(j), :] = kq
            for hh in (0, 1):
                kq_i[spread(j, hh), :] = kq
                c_i[spread(j, hh), :] = mask[rows_of(j), 0:LANES]
        kq = kq_i[...]
        high = kq.astype(BF).astype(F32)
        split = (high + pltpu.roll(kq - high, 64, axis=1)).astype(BF)
        source = lax.broadcasted_iota(jnp.int32, (LANES, 2 * LANES), 0) % 64
        column = lax.broadcasted_iota(jnp.int32, (LANES, 2 * LANES), 1) // LANES
        for n in range(0, 2 * STATE, 2):
            copied = dot(split, jnp.where(source == n + column, 1.0, 0.0).astype(BF), 1, 0)
            kb[n] = copied[:, :LANES]
            kb[n + 1] = copied[:, LANES:]
        if backward:
            dkq_i[...] = jnp.zeros(dkq_i.shape, F32)
            dlr_n[...] = jnp.zeros(dlr_n.shape, F32)
            corr_n[...] = jnp.zeros(corr_n.shape, F32)

    for j in range(n_slots):
        rows = rows_of(j)
        rate = dot(lr_n[rows, :], wdt[...], 1, 0)
        kq = kq_n[rows, :]
        ks = jnp.sum(jnp.where(lane < STATE, kq * kq, 0.0), axis=1, keepdims=True)
        for hh, b, cols in pieces:
            strength = sig(rate[:, cols] + vec[5:6, cols])
            step = strength / (1.0 + strength * ks)
            step_i[b, spread(j, hh), :] = step
            p_i[b, spread(j, hh), :] = step * inner[rows, cols].astype(F32)
            if backward:
                str_n[rows, cols] = strength
                dy_i[b, spread(j, hh), :] = dy_ref[rows, cols]

    if backward:
        hist[0] = jnp.zeros(hist.shape[1:], F32)
    else:
        state[...] = jnp.zeros(state.shape, F32)

    def forward_step(t, carry):
        now = pl.ds(pl.multiple_of(t * ROWS, ROWS), ROWS)
        c = c_i[now, :]
        steps = [step_i[b, now, :] for b in range(nb)]
        ps = [p_i[b, now, :] for b in range(nb)]
        ys = [jnp.zeros((ROWS, LANES), F32) for _ in range(nb)]
        for n in range(STATE):
            k = kb[n, now, :]
            ck2 = c * k * k
            if y_out is not None:
                q = kb[STATE + n, now, :]
            for b in range(nb):
                before = hist[t, n * nb + b] if backward else state[n * nb + b]
                after = (c - ck2 * steps[b]) * before + k * ps[b]
                if backward:
                    hist[t + 1, n * nb + b] = after
                else:
                    state[n * nb + b] = after
                if y_out is not None:
                    ys[b] = ys[b] + q * after
        if y_out is not None:
            for b in range(nb):
                y_i[b, now, :] = ys[b]
        return carry

    lax.fori_loop(0, length, forward_step, 0, unroll=2)

    if y_out is not None:
        for j in range(n_slots):
            rows = rows_of(j)
            for hh, b, cols in pieces:
                y_out[rows, cols] = y_i[b, spread(j, hh), :] + vec[6:7, cols] * inner[rows, cols].astype(F32)
    if not backward:
        return

    h_scr[...] = jnp.zeros(h_scr.shape, F32)

    def backward_step(i, carry):
        t = length - 1 - i
        at = pl.ds(pl.multiple_of(t * 2 * ROWS, 2 * ROWS), 2 * ROWS)
        now = pl.ds(pl.multiple_of(t * ROWS, ROWS), ROWS)
        c = c_i[now, :]
        steps = [step_i[b, now, :] for b in range(nb)]
        ps = [p_i[b, now, :] for b in range(nb)]
        dys = [dy_i[b, now, :] for b in range(nb)]
        a_sum = [jnp.zeros((ROWS, LANES), F32) for _ in range(nb)]
        b_sum = [jnp.zeros((ROWS, LANES), F32) for _ in range(nb)]
        for n in range(STATE):
            k, q = kb[n, now, :], kb[STATE + n, now, :]
            ck = c * k
            ck2 = ck * k
            dk1 = dk2 = dq = None
            for b in range(nb):
                before, after = hist[t, n * nb + b], hist[t + 1, n * nb + b]
                grad = dys[b] * q + h_scr[n * nb + b]
                a_sum[b] = a_sum[b] + grad * k
                both = grad * before
                b_sum[b] = b_sum[b] + ck2 * both
                h_scr[n * nb + b] = (c - ck2 * steps[b]) * grad
                one, two, three = ps[b] * grad, steps[b] * both, dys[b] * after
                dk1 = one if dk1 is None else dk1 + one
                dk2 = two if dk2 is None else dk2 + two
                dq = three if dq is None else dq + three
            dk = dk1 - (2.0 * ck) * dk2
            prod[at, n * LANES : (n + 1) * LANES] = jnp.concatenate([dk, dq], axis=0).astype(BF)
        for b in range(nb):
            a_i[b, now, :] = a_sum[b]
            p_i[b, now, :] = b_sum[b]
        return carry

    lax.fori_loop(0, length, backward_step, 0, unroll=2)

    source = lax.broadcasted_iota(jnp.int32, (STATE * LANES, LANES), 0) // LANES
    sums = jnp.where(source == lax.broadcasted_iota(jnp.int32, (STATE * LANES, LANES), 1), 1.0, 0.0).astype(BF)
    dkq_i[...] = dkq_i[...] + dot(prod[...], sums, 1, 0)

    ddt = [jnp.zeros((1, LANES), F32) for _ in pieces]
    dskip = [jnp.zeros((1, LANES), F32) for _ in pieces]
    for j in range(n_slots):
        rows = rows_of(j)
        kq = kq_n[rows, :]
        ks = jnp.sum(jnp.where(lane < STATE, kq * kq, 0.0), axis=1, keepdims=True)
        corr = jnp.zeros((length, 1), F32)
        for i, (hh, b, cols) in enumerate(pieces):
            at = spread(j, hh)
            inn = inner[rows, cols].astype(F32)
            a, step, dy = a_i[b, at, :], step_i[b, at, :], dy_ref[rows, cols]
            dstep = inn * a - p_i[b, at, :]
            strength = str_n[rows, cols]
            inv = 1.0 / (1.0 + strength * ks)
            drate = (dstep * (inv * inv) * (strength * (1.0 - strength))).astype(BF)
            drate_n[rows, cols] = drate
            dstate_out[rows, cols] = step * a + vec[6:7, cols] * dy
            corr = corr + jnp.sum(dstep * (step * step), axis=1, keepdims=True)
            ddt[i] = ddt[i] + jnp.sum(drate.astype(F32), axis=0, keepdims=True)
            dskip[i] = dskip[i] + jnp.sum(dy * inn, axis=0, keepdims=True)
        corr_n[rows, :] = corr_n[rows, :] + corr
        dlr_n[rows, :] = dlr_n[rows, :] + dot(drate_n[rows, :], wdt[...], 1, 1)
    ddt_out[...] = dot(lr_n[...], drate_n[...], 0, 0)
    dvec_out[...] = jnp.concatenate(
        [jnp.concatenate(ddt, axis=1), jnp.concatenate(dskip, axis=1), jnp.zeros((6, width), F32)], axis=0
    )

    @pl.when(last)
    def _():
        for j in range(n_slots):
            rows = rows_of(j)
            dk, dq = [
                dkq_i[pl.ds(m * ROWS + j, length, stride=2 * ROWS), :]
                + dkq_i[pl.ds(m * ROWS + n_slots + j, length, stride=2 * ROWS), :]
                for m in (0, 1)
            ]
            dkq = dk + pltpu.roll(dq, STATE, axis=1)
            dkq = dkq - jnp.where(lane < STATE, 2.0 * kq_n[rows, :] * corr_n[rows, :], 0.0)
            dpart_out[rows, :] = dlr_n[rows, :].astype(BF)
            dkq = jnp.where(lane < 2 * STATE, dkq, 0.0)
            packed = dkq if j == 0 else packed + pltpu.roll(dkq, 2 * STATE * j, axis=1)
        dpart_out[n_slots * length :, :] = packed.astype(BF)


def rec(parts, inner, dy, wdt, vec, masks, keep_y):
    rows, channels = inner.shape
    n_slots = len(parts)
    length = rows // n_slots
    width = channels // 2
    nb = width // (2 * LANES)

    def whole(a):
        return pl.BlockSpec(a.shape, lambda i: (0,) * a.ndim)

    def block(n):
        return pl.BlockSpec((n, width), lambda i: (0, i))

    wide = pltpu.VMEM((nb, ROWS * length, LANES), F32)
    row = pltpu.VMEM((rows, LANES), F32)
    spread = pltpu.VMEM((ROWS * length, LANES), F32)
    y_like = shape((rows, channels), F32)
    y_scratch = wide if dy is None or keep_y else pltpu.VMEM((ROWS, LANES), F32)
    scratch = [row, spread, spread, pltpu.VMEM((rows, RANK), BF), wide, wide, y_scratch]
    scratch += [pltpu.VMEM((2 * STATE, ROWS * length, LANES), F32)]
    if dy is None:
        scratch += [pltpu.VMEM((STATE * nb, ROWS, LANES), F32)]
        return call(
            partial(rec_body, False, True, n_slots, length, width),
            y_like,
            grid=(2,),
            in_specs=[whole(p) for p in parts] + [block(rows), block(RANK), block(vec.shape[0]), pl.BlockSpec((rows, LANES), lambda i: (0, 0))],
            out_specs=block(rows),
            scratch_shapes=scratch,
            cost_estimate=cost(20e9),
        )(*parts, inner, wdt, vec, masks)
    scratch += [
        pltpu.VMEM((rows, width), F32),
        pltpu.VMEM((length + 1, STATE * nb, ROWS, LANES), F32),
        wide,
        wide,
        pltpu.VMEM((STATE * nb, ROWS, LANES), F32),
        pltpu.VMEM((2 * ROWS * length, LANES), F32),
        pltpu.VMEM((rows, RANK), F32),
        row,
        pltpu.VMEM((2 * ROWS * length, STATE * LANES), BF),
        pltpu.VMEM((rows, width), BF),
    ]
    lr_like = shape((rows, RANK), BF)
    part_like = shape((rows + length, LANES), BF)
    outs = [lr_like, y_like, part_like, shape((RANK, channels), F32), shape((ROWS, channels), F32)]
    specs = [whole(lr_like), block(rows), whole(part_like), block(RANK), block(ROWS)]
    if keep_y:
        outs, specs = outs + [y_like], specs + [block(rows)]
    return call(
        partial(rec_body, True, keep_y, n_slots, length, width),
        tuple(outs),
        grid=(2,),
        in_specs=[whole(p) for p in parts] + [block(rows), block(rows), block(RANK), block(vec.shape[0]), pl.BlockSpec((rows, LANES), lambda i: (0, 0))],
        out_specs=tuple(specs),
        scratch_shapes=scratch,
        cost_estimate=cost(55e9),
        vmem=62,
    )(*parts, inner, dy, wdt, vec, masks)


def gate_values(y, gate):
    s = sig(gate)
    return y * (gate * s), y * (s * (1.0 + gate * (1.0 - s)))


def gate_back_body(y_ref, gate_ref, dgated_ref, gated_near, gated_far, dgate_near, dgate_far):
    half = gated_near.shape[1]
    for h, (gated, dgate) in enumerate([(gated_near, dgate_near), (gated_far, dgate_far)]):
        for b in range(half // LANES):
            cols = slice(b * LANES, (b + 1) * LANES)
            at = slice(h * half + b * LANES, h * half + (b + 1) * LANES)
            one, two = gate_values(y_ref[:, at], gate_ref[:, at])
            gated[:, cols] = one.astype(BF)
            dgate[:, cols] = (dgated_ref[:, at] * two).astype(BF)


def gate_back(n_slots, y, gate, dgated):
    rows, channels = y.shape
    length = rows // n_slots
    side = shape((rows, channels // 2), BF)
    return call(
        gate_back_body,
        (side,) * 4,
        grid=(n_slots,),
        in_specs=[pl.BlockSpec((length, channels), lambda j: (j, 0))] * 3,
        out_specs=[pl.BlockSpec((length, channels // 2), lambda j: (j, 0))] * 4,
        cost_estimate=cost(3e9),
    )(y, gate, dgated)


def conv_bwd_body(n_slots, p0, p1, p2, p3, x_ref, inner, dstate, mask_ref, vec_ref, wdk_ref,
                  dx_near, dx_far, dsmall_out, dvec_out, pad_ref, late_ref, dcat):
    j = pl.program_id(0)
    length, channels = x_ref.shape
    lane = lax.broadcasted_iota(jnp.int32, (1, LANES), 1)

    @pl.when(j == 0)
    def _():
        dsmall_out[...] = jnp.zeros(dsmall_out.shape, F32)
        dvec_out[...] = jnp.zeros(dvec_out.shape, F32)

    low_rank = jnp.zeros((length, RANK), F32)
    kq = jnp.zeros((length, LANES), F32)
    for d, part in enumerate((p0, p1, p2, p3)):
        rows = pl.ds(pl.multiple_of((j ^ d) * length, length), length)
        low_rank = low_rank + part[rows, :].astype(F32)
        packed = part[n_slots * length :, :].astype(F32)
        mine = packed
        for n in range(1, n_slots):
            mine = jnp.where((j ^ d) == n, pltpu.roll(packed, LANES - 2 * STATE * n, axis=1), mine)
        kq = kq + mine
    dcat[:, :RANK] = low_rank.astype(BF)
    dcat[:, RANK:] = jnp.where(lane < 2 * STATE, kq, 0.0).astype(BF)
    dsmall_out[...] += dot(dcat[...], inner[...], 0, 0)
    late_ref[length : length + ROWS, :] = jnp.zeros((ROWS, LANES), F32)
    for b in range(channels // LANES):
        cols = slice(b * LANES, (b + 1) * LANES)
        c, earlier = conv_of(x_ref, slice(0, length), pad_ref, mask_ref, vec_ref, cols)
        dinner = dstate[:, cols] + dot(dcat[...], wdk_ref[:, cols], 1, 0)
        s = sig(c)
        dc = dinner * (s * (1.0 + c * (1.0 - s)))
        dx = vec_ref[0:1, cols] * dc
        sums = [jnp.sum(dc * x_ref[:, cols], axis=0, keepdims=True)]
        for lag in (1, 2, 3):
            sums.append(jnp.sum(dc * earlier[lag - 1], axis=0, keepdims=True))
            late_ref[0:length, :] = dc * mask_ref[:, lag * LANES : (lag + 1) * LANES]
            dx = dx + vec_ref[lag : lag + 1, cols] * late_ref[lag : lag + length, :]
        sums.append(jnp.sum(dc, axis=0, keepdims=True))
        half = channels // 2
        dx_out = dx_near if b * LANES < half else dx_far
        dx_out[:, (b * LANES) % half : (b * LANES) % half + LANES] = dx.astype(BF)
        for i, value in enumerate(sums):
            dvec_out[i : i + 1, cols] += value


def conv_bwd(parts, x, inner, dstate, masks, vec, wdk):
    rows, channels = x.shape
    n_slots = len(parts)
    length = rows // n_slots

    def whole(a):
        return pl.BlockSpec(a.shape, lambda i: (0,) * a.ndim)

    slot = pl.BlockSpec((length, channels), lambda j: (j, 0))
    slot_half = pl.BlockSpec((length, channels // 2), lambda j: (j, 0))
    side = shape((rows, channels // 2), BF)
    small = shape((2 * LANES, channels), F32)
    vecs = shape((ROWS, channels), F32)
    return call(
        partial(conv_bwd_body, n_slots),
        (side, side, small, vecs),
        grid=(n_slots,),
        in_specs=[whole(p) for p in parts]
        + [slot, slot, slot, pl.BlockSpec((length, 4 * LANES), lambda j: (j, 0)), whole(vec), whole(wdk)],
        out_specs=(slot_half, slot_half, whole(small), whole(vecs)),
        scratch_shapes=[
            pltpu.VMEM((ROWS + length, LANES), F32),
            pltpu.VMEM((ROWS + length, LANES), F32),
            pltpu.VMEM((length, 2 * LANES), BF),
        ],
    )(*parts, x, inner, dstate, masks, vec, wdk)


SMALL = 448
DOWN, KQ, DT, VEC = 0, 128, 160, 288


def cut_small_body(where_ref, w_ref, gain_ref, *refs):
    sources, (keep_ref, send_ref, small), fetched, sems = refs[:7], refs[7:10], refs[10:17], refs[17]
    i = pl.program_id(0)
    rows, sub = w_ref.shape[0], keep_ref.shape[1]
    part = keep_ref.shape[0] - rows
    copies = [pltpu.make_async_copy(v, f, sems.at[n]) for n, (v, f) in enumerate(zip(sources, fetched))]

    @pl.when(i == 0)
    def _():
        for copy in copies:
            copy.start()

    mine = where_ref[1] == 0
    scaled = w_ref[...].astype(F32) * gain_ref[...]
    first, second = scaled[:, :sub].astype(BF), scaled[:, sub:].astype(BF)
    keep_ref[0:rows, :] = jnp.where(mine, first, second)
    send_ref[0:rows, :] = jnp.where(mine, second, first)

    @pl.when(i == 0)
    def _():
        for copy in copies:
            copy.wait()
        down, kq, dt, conv, conv_bias, dt_bias, skip = fetched
        at = pl.ds(pl.multiple_of(where_ref[0] * 2 * sub, 2 * sub), 2 * sub)
        small[DOWN:KQ, :] = down[at, :].astype(F32).T.astype(BF)
        small[KQ:DT, :] = kq[:, at]
        small[DT:VEC, :] = dt[:, at]
        last = [v[:, at].astype(F32) for v in (conv, conv_bias, dt_bias, skip)] + [jnp.zeros((9, 2 * sub), F32)]
        small[VEC : VEC + 16, :] = jnp.concatenate(last, axis=0).astype(BF)
        small[VEC + 16 :, :] = jnp.zeros((SMALL - VEC - 16, 2 * sub), BF)

    piece = small[pl.ds(pl.multiple_of(i * part, 16), part), :]
    first, second = piece[:, :sub], piece[:, sub:]
    keep_ref[rows:, :] = jnp.where(mine, first, second)
    send_ref[rows:, :] = jnp.where(mine, second, first)


def cut_small(where, weight, gain, down, kq, dt, conv, conv_bias, dt_bias, skip, n_dp, n_grp, sub):
    rows = weight.shape[0]
    part = SMALL // n_dp
    out = shape((rows + part, n_dp * sub), BF)
    smalls = [down, kq, dt, conv, conv_bias, dt_bias, skip]
    return call(
        cut_small_body,
        (out, out),
        grid_spec=pltpu.PrefetchScalarGridSpec(
            num_scalar_prefetch=1,
            grid=(n_dp,),
            in_specs=[
                pl.BlockSpec((rows, 2 * sub), lambda i, w: (0, i * n_grp + w[0])),
                pl.BlockSpec((rows, 1), lambda i, w: (0, 0)),
            ]
            + [pl.BlockSpec(memory_space=pltpu.HBM)] * 7,
            out_specs=[pl.BlockSpec((rows + part, sub), lambda i, w: (0, i))] * 2,
            scratch_shapes=[pltpu.VMEM((SMALL, 2 * sub), BF)]
            + [pltpu.VMEM(v.shape, BF) for v in smalls]
            + [pltpu.SemaphoreType.DMA((7,))],
        ),
        cost_estimate=cost(3e9),
        vmem=62,
    )(where, weight, gain, *smalls)


def cut_out_body(where_ref, w_ref, gain_ref, o_ref, keep_ref, send_ref):
    i = pl.program_id(0)
    rows, sub = w_ref.shape[0], keep_ref.shape[1]
    mine = where_ref[1] == 0
    scaled = w_ref[...].astype(F32) * gain_ref[...]
    first, second = scaled[:, :sub].astype(BF), scaled[:, sub:].astype(BF)
    keep_ref[0:rows, :] = jnp.where(mine, first, second)
    send_ref[0:rows, :] = jnp.where(mine, second, first)
    n = pl.num_programs(0)
    wide = o_ref.shape[1] // 4
    for c in range(4):
        lanes = pl.ds(pl.multiple_of(c * wide + i * sub, sub), sub)
        first, second = o_ref[0:sub, lanes], o_ref[sub:, lanes]
        at = slice(rows + c * sub, rows + (c + 1) * sub)
        keep_ref[at, :] = jnp.where(mine, first, second)
        send_ref[at, :] = jnp.where(mine, second, first)


def cut_out(where, weight, gain, out_weight, n_dp, n_grp, sub):
    rows = weight.shape[0]
    out = shape((rows + 4 * sub, n_dp * sub), BF)
    return call(
        cut_out_body,
        (out, out),
        grid_spec=pltpu.PrefetchScalarGridSpec(
            num_scalar_prefetch=1,
            grid=(n_dp,),
            in_specs=[
                pl.BlockSpec((rows, 2 * sub), lambda i, w: (0, (n_dp + i) * n_grp + w[0])),
                pl.BlockSpec((rows, 1), lambda i, w: (0, 0)),
                pl.BlockSpec((2 * sub, out_weight.shape[1]), lambda i, w: (w[0], 0)),
            ],
            out_specs=[pl.BlockSpec((rows + 4 * sub, sub), lambda i, w: (0, i))] * 2,
        ),
        cost_estimate=cost(3e9),
    )(where, weight, gain, out_weight)


def flat_call(body, out_shape, arrays, specs=None, scratch=(), flops=0, vmem=48):
    def whole(v):
        return pl.BlockSpec(v.shape, lambda i: (0,) * len(v.shape))

    outs = out_shape if isinstance(out_shape, tuple) else (out_shape,)
    out_specs = tuple(whole(v) for v in outs)
    return call(
        body,
        out_shape,
        grid=(1,),
        in_specs=[(specs or {}).get(n, whole(v)) for n, v in enumerate(arrays)],
        out_specs=out_specs if isinstance(out_shape, tuple) else out_specs[0],
        scratch_shapes=list(scratch),
        cost_estimate=cost(flops),
        vmem=vmem,
    )(*arrays)


def q_block(q, which, rows):
    return pl.BlockSpec((q.shape[0], rows, q.shape[2]), lambda i: (0, which, 0))


def blocks_sum(a_ref, w_ref, rows):
    total = None
    for p in range(w_ref.shape[0]):
        term = dot(a_ref[:, p * rows : (p + 1) * rows], w_ref[p, 0:rows, :], 1, 0)
        total = term if total is None else total + term
    return total


def first_body(n_slots, rows, a_ref, mask_ref, near_ref, far_ref, *refs):
    x_ref, inner_ref, part_ref, cat_ref, wdt_ref, vec_ref, pad_ref, small = refs
    half = x_ref.shape[1] // 2
    n_dp = near_ref.shape[0]
    sub = half // n_dp
    length = x_ref.shape[0] // n_slots
    part = SMALL // n_dp
    for h, w_ref in enumerate((near_ref, far_ref)):
        for p in range(n_dp):
            lanes = slice(h * half + p * sub, h * half + (p + 1) * sub)
            for i in range(n_dp):
                small[i * part : (i + 1) * part, lanes] = w_ref[p, rows:, i * sub : (i + 1) * sub]
    cat_ref[0:DT, :] = small[0:DT, :]
    cat_ref[DT:, :] = jnp.zeros((cat_ref.shape[0] - DT, 2 * half), BF)
    wdt_ref[...] = small[DT:VEC, :]
    vec_ref[...] = small[VEC : VEC + 16, :].astype(F32)
    both = jnp.zeros((x_ref.shape[0], 2 * LANES), F32)
    for h, w_ref in enumerate((near_ref, far_ref)):
        lanes = slice(h * half, (h + 1) * half)
        x_ref[:, lanes] = blocks_sum(a_ref, w_ref, rows)
        for j in range(n_slots):
            at = slice(j * length, (j + 1) * length)
            for b in range(half // LANES):
                cols = slice(h * half + b * LANES, h * half + (b + 1) * LANES)
                c, _ = conv_of(x_ref, at, pad_ref, mask_ref, vec_ref, cols)
                inner_ref[at, cols] = (c * sig(c)).astype(BF)
        both = both + dot(inner_ref[:, lanes], cat_ref[:, lanes], 1, 1)
    part_ref[...] = pack(both[:, :RANK], both[:, RANK:])


def first_products(n_slots, a, masks, near, far, rows):
    n, half = a.shape[0], near.shape[2]
    return flat_call(
        partial(first_body, n_slots, rows),
        (
            shape((n, 2 * half), F32),
            shape((n, 2 * half), BF),
            shape((n, 2 * LANES), BF),
            shape((2 * LANES, 2 * half), BF),
            shape((RANK, 2 * half), BF),
            shape((16, 2 * half), F32),
        ),
        [a, masks, near, far],
        scratch=[pltpu.VMEM((ROWS + n // n_slots, LANES), F32), pltpu.VMEM((SMALL, 2 * half), BF)],
        flops=8e9,
    )


def gate_body(rows, a_ref, y_ref, near_ref, far_ref, gate_ref, gated_near, gated_far):
    half = gated_near.shape[1]
    for h, (w_ref, gated) in enumerate([(near_ref, gated_near), (far_ref, gated_far)]):
        at = slice(h * half, (h + 1) * half)
        gate = blocks_sum(a_ref, w_ref, rows)
        gate_ref[:, at] = gate
        gated[...] = (y_ref[:, at] * (gate * sig(gate))).astype(BF)


def gate_product(a, y, near, far, rows):
    half = near.shape[2]
    side = shape((a.shape[0], half), BF)
    return flat_call(
        partial(gate_body, rows),
        (shape(y.shape, F32), side, side),
        [a, y, near, far],
        specs={2: q_block(near, 0, rows), 3: q_block(far, 0, rows)},
        flops=6e9,
    )


def out_weight_of(near_ref, far_ref, w_scr):
    half = w_scr.shape[0] // 2
    n_dp = near_ref.shape[0]
    sub = half // n_dp
    wide = w_scr.shape[1] // 4
    for h, w_ref in enumerate((near_ref, far_ref)):
        for p in range(n_dp):
            for c in range(4):
                block = w_ref[p, c * sub : (c + 1) * sub, :]
                w_scr[h * half + p * sub : h * half + (p + 1) * sub, c * wide : (c + 1) * wide] = block


def branch_body(left_near, left_far, near_ref, far_ref, out_ref, w_scr):
    out_weight_of(near_ref, far_ref, w_scr)
    half = left_near.shape[1]
    wide = w_scr.shape[1] // 4
    for c in range(4):
        lanes = slice(c * wide, (c + 1) * wide)
        total = dot(left_near[...], w_scr[:half, lanes], 1, 0) + dot(left_far[...], w_scr[half:, lanes], 1, 0)
        out_ref[:, lanes] = total.astype(BF)


def branch_product(left_near, left_far, near, far, rows):
    half = near.shape[2]
    return flat_call(
        branch_body,
        shape((left_near.shape[0], 4 * half), BF),
        [left_near, left_far, near, far],
        specs={2: q_block(near, 1, rows), 3: q_block(far, 1, rows)},
        scratch=[pltpu.VMEM((2 * half, 4 * half), BF)],
        flops=5e9,
    )


def dgated_body(d_ref, y_ref, gate_ref, near_ref, far_ref, dy_ref, dgate_near, dgate_far, w_scr):
    out_weight_of(near_ref, far_ref, w_scr)
    half = dgate_near.shape[1]
    for h, dgate in enumerate((dgate_near, dgate_far)):
        at = slice(h * half, (h + 1) * half)
        dgated = dot(d_ref[...], w_scr[at, :], 1, 1)
        gate = gate_ref[:, at]
        dy_ref[:, at] = dgated * (gate * sig(gate))
        dgate[...] = (dgated * gate_values(y_ref[:, at], gate)[1]).astype(BF)


def dgated_product(dbranch, y, gate, near, far, rows):
    half = near.shape[2]
    side = shape((dbranch.shape[0], half), BF)
    return flat_call(
        dgated_body,
        (shape(y.shape, F32), side, side),
        [dbranch, y, gate, near, far],
        specs={3: q_block(near, 1, rows), 4: q_block(far, 1, rows)},
        scratch=[pltpu.VMEM((2 * half, dbranch.shape[1]), BF)],
        flops=6e9,
    )


def dnormed_body(rows, dx_near, dx_far, dg_near, dg_far, p_near, p_far, q_near, q_far, out_ref):
    total = dot(dx_near[...], p_near[0, 0:rows, :], 1, 1) + dot(dx_far[...], p_far[0, 0:rows, :], 1, 1)
    total = total + dot(dg_near[...], q_near[0], 1, 1) + dot(dg_far[...], q_far[0], 1, 1)
    out_ref[...] = total.astype(BF)


def dnormed_product(lefts, p_near, p_far, q_near, q_far, rows):
    n_dp, _, half = p_near.shape
    n = lefts[0].shape[0]
    left = pl.BlockSpec((n, half), lambda i: (0, 0))
    p_spec = pl.BlockSpec((1, p_near.shape[1], half), lambda i: (i, 0, 0))
    q_spec = pl.BlockSpec((1, rows, half), lambda i: (i, 0, 0))
    return call(
        partial(dnormed_body, rows),
        shape((n, n_dp * rows), BF),
        grid=(n_dp,),
        in_specs=[left] * 4 + [p_spec] * 2 + [q_spec] * 2,
        out_specs=pl.BlockSpec((n, rows), lambda i: (0, i)),
        cost_estimate=cost(8e9),
    )(*lefts, p_near, p_far, q_near, q_far)


def grad_p_body(a_ref, a_far, dx_ref, dx_come, small_ref, small_come, out_ref):
    rows = a_ref.shape[1]
    value = dot(a_ref[...], dx_ref[...], 0, 0) + dot(a_far[...], dx_come[...], 0, 0)
    out_ref[0, 0:rows, :] = value.astype(BF)
    out_ref[0, rows:, :] = (small_ref[...] + small_come[...].astype(F32)).astype(BF)


def grad_p(a, a_far, dx, dx_come, small, small_come, n_dp):
    rows = a.shape[1] // n_dp
    part = small.shape[0] // n_dp
    half = dx.shape[1]
    col = pl.BlockSpec((a.shape[0], rows), lambda i: (0, i))
    whole = pl.BlockSpec(dx.shape, lambda i: (0, 0))
    block = pl.BlockSpec((part, half), lambda i: (i, 0))
    return call(
        grad_p_body,
        shape((n_dp, rows + part, half), BF),
        grid=(n_dp,),
        in_specs=[col, col, whole, whole, block, block],
        out_specs=pl.BlockSpec((1, rows + part, half), lambda i: (i, 0, 0)),
        cost_estimate=cost(5e9),
    )(a, a_far, dx, dx_come, small, small_come)


def grad_q_body(a_ref, a_far, dg_ref, dg_come, gated_ref, gated_come, db_ref, db_far, out_ref):
    rows = a_ref.shape[1]
    sub = gated_ref.shape[1]
    wide = db_ref.shape[1] // 4
    value = dot(a_ref[...], dg_ref[...], 0, 0) + dot(a_far[...], dg_come[...], 0, 0)
    out_ref[0, 0:rows, :] = value.astype(BF)
    value = dot(gated_ref[...], db_ref[...], 0, 0) + dot(gated_come[...], db_far[...], 0, 0)
    for c in range(4):
        out_ref[0, rows + c * sub : rows + (c + 1) * sub, :] = value[:, c * wide : (c + 1) * wide].astype(BF)


def grad_q(a, a_far, dg, dg_come, gated, gated_come, db, db_far, n_dp):
    rows = a.shape[1] // n_dp
    half = dg.shape[1]
    sub = half // n_dp
    col = pl.BlockSpec((a.shape[0], rows), lambda i: (0, i))
    sub_col = pl.BlockSpec((a.shape[0], sub), lambda i: (0, i))

    def whole(v):
        return pl.BlockSpec(v.shape, lambda i: (0, 0))

    return call(
        grad_q_body,
        shape((n_dp, rows + 4 * sub, half), BF),
        grid=(n_dp,),
        in_specs=[col, col, whole(dg), whole(dg), sub_col, sub_col, whole(db), whole(db)],
        out_specs=pl.BlockSpec((1, rows + 4 * sub, half), lambda i: (i, 0, 0)),
        cost_estimate=cost(8e9),
    )(a, a_far, dg, dg_come, gated, gated_come, db, db_far)


def small_grads_body(dsmall, ddt, dconv, dvec, near_ref, far_ref, scr):
    half = near_ref.shape[1]
    sub = half // 4
    part = SMALL // 4
    scr[DOWN:DT, :] = dsmall[0:DT, :]
    scr[DT:VEC, :] = ddt[...]
    rows = [dconv[0:5, :], dvec[0:2, :], jnp.zeros((1, 2 * half), F32)]
    scr[VEC : VEC + 8, :] = jnp.concatenate(rows, axis=0)
    scr[VEC + 8 :, :] = jnp.zeros((SMALL - VEC - 8, 2 * half), F32)
    for block in range(4):
        at = slice(block * part, (block + 1) * part)
        for i in range(4):
            rows = slice(i * part, (i + 1) * part)
            lanes = slice(i * sub, (i + 1) * sub)
            near_ref[at, lanes] = scr[rows, block * sub : (block + 1) * sub]
            far_ref[at, lanes] = scr[rows, half + block * sub : half + (block + 1) * sub].astype(BF)


def small_grads(dsmall, ddt, dconv, dvec):
    half = ddt.shape[1] // 2
    return call(
        small_grads_body,
        (shape((SMALL, half), F32), shape((SMALL, half), BF)),
        scratch_shapes=[pltpu.VMEM((SMALL, 2 * half), F32)],
        cost_estimate=cost(2e9),
    )(dsmall, ddt, dconv, dvec)


def join_values(n_grp, where_ref, parts):
    mine = where_ref[1] == 0
    for d in range(n_grp):
        for h in (0, 1):
            sub = parts[0].shape[2]
            at = pl.ds(pl.multiple_of(((where_ref[0] ^ d) * 2 + h) * sub, sub), sub)
            yield at, jnp.where(mine, parts[d][h], parts[n_grp + d][h]).astype(F32)


def join_p_body(n_grp, n_dp, where_ref, w_ref, gain_ref, *refs):
    parts = refs[: 2 * n_grp]
    out_ref, sum_ref, down_ref, kq_ref, dt_ref, conv_ref, cb_ref, db_ref, skip_ref, small = refs[2 * n_grp + 1 :]
    i = pl.program_id(0)
    rows, sub = w_ref.shape[0], parts[0].shape[2]
    part = parts[0].shape[1] - rows

    @pl.when(i == 0)
    def _():
        sum_ref[...] = jnp.zeros(sum_ref.shape, F32)

    for at, value in join_values(n_grp, where_ref, parts):
        out_ref[:, at] = value[:rows] * gain_ref[...]
        sum_ref[...] += value[:rows] * w_ref[:, at].astype(F32)
        small[pl.ds(pl.multiple_of(i * part, 16), part), at] = value[rows:]

    @pl.when(i == n_dp - 1)
    def _():
        for b in range(down_ref.shape[0] // LANES):
            at = slice(b * LANES, (b + 1) * LANES)
            down_ref[at, :] = small[DOWN:KQ, at].T
        kq_ref[...] = small[KQ:DT, :]
        dt_ref[...] = small[DT:VEC, :]
        conv_ref[...] = small[VEC : VEC + 4, :]
        cb_ref[...] = small[VEC + 4 : VEC + 5, :]
        db_ref[...] = small[VEC + 5 : VEC + 6, :]
        skip_ref[...] = small[VEC + 6 : VEC + 7, :]


def join_q_body(n_grp, n_dp, where_ref, w_ref, gain_ref, *refs):
    parts, out_ref, sum_ref, o_ref = refs[: 2 * n_grp], refs[-3], refs[-2], refs[-1]
    i = pl.program_id(0)
    rows, sub = w_ref.shape[0], parts[0].shape[2]
    wide = o_ref.shape[1] // 4

    @pl.when(i == 0)
    def _():
        sum_ref[...] = jnp.zeros(sum_ref.shape, F32)

    for at, value in join_values(n_grp, where_ref, parts):
        out_ref[:, at] = value[:rows] * gain_ref[...]
        sum_ref[...] += value[:rows] * w_ref[:, at].astype(F32)
        for c in range(4):
            lanes = pl.ds(pl.multiple_of(c * wide + i * sub, sub), sub)
            o_ref[at, lanes] = value[rows + c * sub : rows + (c + 1) * sub]


def join_packed(body, where, weight, gain, parts, before, side, n_dp, extras, scratch=()):
    rows = weight.shape[0]
    n_grp = len(parts) // 2
    sub = parts[0].shape[2] // n_dp
    wide = 2 * n_grp * sub
    dims = (2, parts[0].shape[1], sub)
    mine = pl.BlockSpec(dims, lambda i, w: (0, 0, i * (1 - w[1])))
    other = pl.BlockSpec(dims, lambda i, w: (0, 0, i * w[1]))
    last = [] if before is None else [before]
    return call(
        partial(body, n_grp, n_dp),
        (shape(weight.shape, F32), shape((rows, sub), F32), *extras),
        grid_spec=pltpu.PrefetchScalarGridSpec(
            num_scalar_prefetch=1,
            grid=(n_dp,),
            in_specs=[
                pl.BlockSpec((rows, wide), lambda i, w: (0, side * n_dp + i)),
                pl.BlockSpec((rows, 1), lambda i, w: (0, 0)),
            ]
            + [mine] * n_grp
            + [other] * n_grp
            + [pl.BlockSpec(memory_space=pl.ANY)] * len(last),
            out_specs=[
                pl.BlockSpec((rows, wide), lambda i, w: (0, side * n_dp + i)),
                pl.BlockSpec((rows, sub), lambda i, w: (0, 0)),
            ]
            + [pl.BlockSpec(v.shape, lambda i, w: (0, 0)) for v in extras],
            scratch_shapes=list(scratch),
        ),
        input_output_aliases={3 + len(parts): 0} if last else {},
        cost_estimate=cost(8e9),
    )(where, weight, gain, *parts, *last)


def rms_of(hidden):
    return lax.rsqrt(jnp.mean(hidden * hidden, axis=1, keepdims=True) + EPSILON)


def slot_masks(lengths, length):
    ends = jnp.cumsum(lengths, axis=1)
    position = jnp.arange(length, dtype=jnp.int32)
    segment = jnp.sum((position[None, :, None] >= ends[:, None, :]).astype(jnp.int32), axis=2)
    valid = (position[None, :] < ends[:, -1:]).astype(F32)
    same = []
    for lag in (1, 2, 3):
        before = jnp.concatenate([jnp.full((segment.shape[0], lag), -1, jnp.int32), segment[:, :-lag]], axis=1)
        same.append((before == segment).astype(F32))
    stack = jnp.stack([same[0]] + same, axis=2).reshape(-1, 4, 1)
    spread = jnp.broadcast_to(stack, stack.shape[:2] + (LANES,)).reshape(-1, 4 * LANES)
    return spread, valid


def everywhere(value, axis):
    return lax.all_gather(value, "dp", axis=axis, tiled=True)


def after(value, *others):
    return lax.optimization_barrier((value, *others))[0]


def on_any_line(boundary, doc_lengths, norm_gain, in_weight, conv_weight, conv_bias, down_weight, kq_weight,
              dt_weight, dt_bias, skip_weight, out_weight):
    s = lax.axis_index("section")
    g = lax.axis_index("grp")
    n_grp = lax.axis_size("grp")
    n_dp = lax.axis_size("dp")
    length, width = boundary.shape[3], boundary.shape[4]
    inner = in_weight.shape[2] // 2
    block = inner // n_dp
    sub = block // (2 * n_grp)
    half = sub * n_dp
    mine_first = s == 0
    gain = norm_gain[0].astype(F32)[:, None]

    def pick(first, second):
        return jnp.where(mine_first, first, second)

    rows = boundary[0, :, 0]
    traded = swap(pick(rows[1], rows[0]), "section", 1)
    hidden = pick(rows[0], traded)
    cotangent = pick(traded, rows[1])
    lengths = lax.dynamic_index_in_dim(doc_lengths[:, 0], s, 0, keepdims=True)
    all_lengths = jnp.concatenate([lengths] + peers(lengths), axis=0)
    masks, valid = slot_masks(all_lengths, length)
    valid = valid[0][:, None]

    def columns(array):
        blocks = array.shape[1] // block
        view = array.reshape(array.shape[0], blocks, n_grp, 2, sub)
        view = lax.dynamic_index_in_dim(view, g, 2, keepdims=False)
        halves = [view[:, :, h].reshape(array.shape[0], blocks * sub) for h in (0, 1)]
        return pick(*halves), pick(halves[1], halves[0])

    def side(which):
        part = in_weight[0, :, which * inner : (which + 1) * inner]
        return columns((part.astype(F32) * gain).astype(BF))

    def out_side():
        view = lax.dynamic_slice_in_dim(out_weight[0], g * 2 * sub, 2 * sub, 0)
        return pick(view[:sub], view[sub:]), pick(view[sub:], view[:sub])

    def small_side():
        def lanes(array):
            return lax.dynamic_slice_in_dim(array, g * 2 * sub, 2 * sub, 1)

        down = lax.dynamic_slice_in_dim(down_weight[0], g * 2 * sub, 2 * sub, 0).T
        view = jnp.concatenate(
            [down, lanes(kq_weight[0]), jnp.zeros((2 * LANES - RANK - 2 * STATE, 2 * sub), BF), lanes(dt_weight[0]),
             lanes(conv_weight[0]), lanes(conv_bias), lanes(dt_bias), lanes(skip_weight)], axis=0)
        return pick(view[:, :sub], view[:, sub:]), pick(view[:, sub:], view[:, :sub])

    def two_layers(keep, send):
        come = swap(send, "section", 1)
        return pick(keep, come), pick(come, keep)

    x_sides, s_sides = two_layers(*side(0)), two_layers(*small_side())
    g_sides, o_sides = two_layers(*side(1)), two_layers(*out_side())

    def with_far(near):
        return near, swap(near, "section", 1)

    layers = []
    for l in (0, 1):
        w_s = jnp.concatenate(with_far(everywhere(s_sides[l], 1)), axis=1)
        w_x = with_far(everywhere(x_sides[l], 0))
        w_g = with_far(everywhere(g_sides[l], 0))
        w_o = with_far(everywhere(o_sides[l], 0))
        cat = w_s[: 2 * LANES]
        wdt = w_s[2 * LANES : 2 * LANES + RANK]
        tail = w_s[2 * LANES + RANK :].astype(F32)
        vec = jnp.concatenate([tail, jnp.zeros((9, tail.shape[1]), F32)], axis=0)
        layers.append((w_x, w_g, w_o, cat, wdt, vec))

    def group(value):
        return jnp.concatenate([value] + peers(value), axis=0)

    def scatter(value):
        total = value[:length].astype(F32)
        for d in range(1, n_grp):
            total = total + swap(value[d * length : (d + 1) * length], "grp", d).astype(F32)
        return total

    def forward(h, layer):
        w_x, w_g, w_o, cat, wdt, vec = layer
        a = group((h * rms_of(h)).astype(BF))
        x, act, part = proj_conv(n_grp, a, *w_x, masks, vec, cat)
        gate = proj(a, *w_g, 0)
        return a, x, gate, act, [part] + peers(part)

    def gated_back(saved, layer, dgated, y, rec_out):
        gate = saved[2]
        if y is None:
            y = rec_out[5]
        return gate_back(n_grp, y, gate, dgated) + tuple(rec_out)

    def backward(h, dout, dbranch, layer, saved, rec_out):
        w_x, w_g, w_o, cat, wdt, vec = layer
        a, x, gate, act, parts = saved
        gated_near, gated_far, dgate_near, dgate_far, lr, dstate, dpart, ddt, dvec = rec_out[:9]
        dx_near, dx_far, dsmall, dconv = conv_bwd([dpart] + peers(dpart), x, act, dstate, masks, vec, cat)
        scaled = scatter(total_of([dx_near, dx_far, dgate_near, dgate_far], [*w_x, *w_g], 1))
        rms = rms_of(h)
        own = h * rms
        dh = dout + rms * (scaled - own * jnp.mean(scaled * own, axis=1, keepdims=True))

        a_far, dbranch_far = swap(a, "section", 1), swap(dbranch, "section", 1)
        dgate_come, gated_come = swap(dgate_far, "section", 1), swap(gated_far, "section", 1)
        dx_come = swap(dx_far, "section", 1)

        def both(left, right, left_come, right_come):
            return (dot(left, right, 0, 0) + dot(left_come, right_come, 0, 0)).astype(BF)

        grad_g = both(a, dgate_near, a_far, dgate_come)
        grad_o = both(gated_near, dbranch, gated_come, dbranch_far)
        grad_x = both(a, dx_near, a_far, dx_come)
        grad_s = jnp.concatenate([dsmall, ddt, dconv[:5], dvec[:2], jnp.zeros((1, ddt.shape[1]), F32)], axis=0)
        grad_s = grad_s[:, :half] + swap(grad_s[:, half:].astype(BF), "section", 1).astype(F32)
        grad_o = jnp.concatenate([grad_o, grad_s.T.astype(BF)], axis=1)
        return dh, (grad_g, grad_o, grad_x)

    h0 = hidden.astype(F32)
    saved0 = forward(h0, layers[0])
    y0 = rec(saved0[4], saved0[3], None, layers[0][4], layers[0][5], masks, True)
    gated0 = gate_values(y0, saved0[2])[0].astype(BF)
    branch0 = scatter(total_of([gated0[:, :half], gated0[:, half:]], layers[0][2], 0))
    h1 = (h0 + valid * branch0).astype(BF).astype(F32)
    saved1 = forward(h1, layers[1])
    dout1 = cotangent.astype(F32)
    dbranch1 = group((valid * dout1).astype(BF))
    dgated1 = proj(dbranch1, *layers[1][2], 1)
    dy1 = gate_values(dgated1, saved1[2])[0]
    rec1 = rec(saved1[4], saved1[3], dy1, layers[1][4], layers[1][5], masks, True)
    rec1 = gated_back(saved1, layers[1], dgated1, None, rec1)
    branch1 = scatter(total_of(rec1[:2], layers[1][2], 0))
    out1 = h1 + valid * branch1
    dh1, grads1 = backward(h1, dout1, dbranch1, layers[1], saved1, rec1)
    dout0 = dh1.astype(BF).astype(F32)
    dbranch0 = group((valid * dout0).astype(BF))
    dgated0 = proj(dbranch0, *layers[0][2], 1)
    dy0 = gate_values(dgated0, saved0[2])[0]
    rec0 = rec(saved0[4], saved0[3], dy0, layers[0][4], layers[0][5], masks, False)
    rec0 = gated_back(saved0, layers[0], dgated0, y0, rec0)
    dh0, grads0 = backward(h0, dout0, dbranch0, layers[0], saved0, rec0)

    far = swap(pick(out1, dh0), "section", 1)
    result = pick(jnp.stack([dh0, far]), jnp.stack([far, out1]))
    result = result.reshape(1, 2, 1, length, width)

    def collected(l, grad):
        near = lax.psum_scatter(grad, "dp", scatter_dimension=0, tiled=True)
        far = directed(near, "section", [(1 - l, l)])
        halves = jnp.stack([near, far] if l == 0 else [far, near])
        out = [halves]
        for d in range(1, n_grp):
            pairs = [(l * n_grp + i, l * n_grp + (i ^ d)) for i in range(n_grp)]
            out.append(directed(halves, ("section", "grp"), pairs))
        return out

    (g1, o1, x1), (g0, o0, x0) = [[collected(l, grad) for grad in grads] for l, grads in ((1, grads1), (0, grads0))]

    def in_order(firsts, seconds):
        return jnp.stack([pick(a, b) for a, b in zip(firsts, seconds)])[jnp.arange(n_grp) ^ g]

    smalls = in_order([v[:, :, width:] for v in o0], [v[:, :, width:] for v in o1]).astype(F32)
    grad_small = smalls.transpose(3, 0, 1, 2).reshape(smalls.shape[3], block)
    sides = []
    for first, second in ((x0, x1), (g0, g1)):
        value = in_order(first, second).reshape(n_grp, 2, -1, n_dp, sub)
        sides.append(value.transpose(2, 3, 0, 1, 4).reshape(value.shape[2], inner))
    product = jnp.concatenate(sides, axis=1).astype(F32)
    grad_in = product * gain
    grad_gain = jnp.sum(product * in_weight[0].astype(F32), axis=1)
    grad_out = in_order([v[:, :, :width] for v in o0], [v[:, :, :width] for v in o1]).astype(F32).reshape(block, width)
    base = 2 * LANES + RANK
    return (
        result,
        grad_gain[None],
        grad_in[None],
        grad_small[None, base : base + 4],
        grad_small[base + 4][None],
        grad_small[:RANK].T[None],
        grad_small[None, RANK : RANK + 2 * STATE],
        grad_small[None, 2 * LANES : base],
        grad_small[base + 5][None],
        grad_small[base + 6][None],
        grad_out[None],
    )


def on_device(boundary, doc_lengths, norm_gain, in_weight, conv_weight, conv_bias, down_weight, kq_weight,
              dt_weight, dt_bias, skip_weight, out_weight):
    s = lax.axis_index("section")
    g = lax.axis_index("grp")
    n_grp = lax.axis_size("grp")
    n_dp = lax.axis_size("dp")
    length, width = boundary.shape[3], boundary.shape[4]
    inner = in_weight.shape[2] // 2
    block = inner // n_dp
    sub = block // (2 * n_grp)
    n_rows = width // n_dp
    mine_first = s == 0
    where = jnp.stack([g, s]).astype(jnp.int32)
    gain = norm_gain[0].astype(F32)[:, None]

    def pick(first, second):
        return jnp.where(mine_first, first, second)

    def section(value):
        return swap(value, "section", 1)

    def two_layers(keep, send):
        come = section(send)
        return pick(keep, come), pick(come, keep)

    def group(value):
        return jnp.concatenate([value] + peers(value), axis=0)

    def scatter(value):
        total = value[:length].astype(F32)
        come = [swap(value[d * length : (d + 1) * length], "grp", d) for d in range(1, n_grp)]
        for piece in come:
            total = total + piece.astype(F32)
        return total, come

    def line(value):
        return lax.all_gather(value, "dp", axis=0)

    p_sides = two_layers(*cut_small(where, in_weight[0], gain, down_weight[0], kq_weight[0], dt_weight[0],
                                    conv_weight[0], conv_bias, dt_bias, skip_weight, n_dp, n_grp, sub))
    p0 = line(p_sides[0])
    rows = boundary[0, :, 0]
    traded = section(pick(rows[1], rows[0]))
    hidden = pick(rows[0], traded)
    cotangent = pick(traded, rows[1])
    lengths = lax.dynamic_index_in_dim(doc_lengths[:, 0], s, 0, keepdims=True)
    all_lengths = jnp.concatenate([lengths] + peers(lengths), axis=0)
    masks, valid = slot_masks(all_lengths, length)
    valid = valid[0][:, None]
    h0 = hidden.astype(F32)
    a0_parts = peers((h0 * rms_of(h0)).astype(BF))
    a0 = jnp.concatenate([(h0 * rms_of(h0)).astype(BF)] + a0_parts, axis=0)
    q_sides = two_layers(*cut_out(where, in_weight[0], gain, out_weight[0], n_dp, n_grp, sub))
    p0_far = section(after(p0, q_sides[0], *a0_parts))
    q0 = line(after(q_sides[0], p0, a0))
    dout1 = cotangent.astype(F32)

    def input_gradient(h, dout, scaled):
        rms = rms_of(h)
        own = h * rms
        return dout + rms * (scaled - own * jnp.mean(scaled * own, axis=1, keepdims=True))

    def summed(grad):
        return lax.psum_scatter(grad, "dp", scatter_dimension=0, tiled=True)[0]

    def collected(l, near):
        far = directed(near, "section", [(1 - l, l)])
        halves = jnp.stack([near, far] if l == 0 else [far, near])
        out = [halves]
        for d in range(1, n_grp):
            pairs = [(l * n_grp + i, l * n_grp + (i ^ d)) for i in range(n_grp)]
            out.append(directed(halves, ("section", "grp"), pairs))
        return out

    def gradient_q(a, a_far, dbranch, dbranch_far, gated, gated_far, dgate, dgate_far):
        return grad_q(a, a_far, dgate, section(dgate_far), gated, section(gated_far), dbranch, dbranch_far, n_dp)

    def gradient_p(a, a_far, dx_near, dx_far, dsmall, ddt, dconv, dvec):
        small_near, small_far = small_grads(dsmall, ddt, dconv, dvec)
        return grad_p(a, a_far, dx_near, section(dx_far), small_near, section(small_far), n_dp)

    x0, act0, part0, cat0, wdt0, vec0 = first_products(n_grp, a0, masks, p0, p0_far, n_rows)
    parts0 = [part0] + peers(part0)
    y0 = rec(parts0, act0, None, wdt0, vec0, masks, True)
    dbranch1 = group(after((valid * dout1).astype(BF), y0))
    q0_far = section(after(q0, dbranch1))
    p1 = line(after(p_sides[1], q0, dbranch1))
    a0_far = section(after(a0, y0))
    gate0, gated0_near, gated0_far = gate_product(a0, y0, q0, q0_far, n_rows)
    branch0 = scatter(branch_product(gated0_near, gated0_far, q0, q0_far, n_rows))[0]
    h1 = (h0 + valid * branch0).astype(BF).astype(F32)

    p1_far = section(after(p1, h1))
    q1 = line(after(q_sides[1], p1, h1))
    a1 = group((h1 * rms_of(h1)).astype(BF))
    x1, act1, part1, cat1, wdt1, vec1 = first_products(n_grp, a1, masks, p1, p1_far, n_rows)
    parts1 = [part1] + peers(part1)
    a1_far = section(after(a1, part1))
    y1 = rec(parts1, act1, None, wdt1, vec1, masks, True)
    q1_far = section(after(q1, y1))
    dbranch1_far = section(after(dbranch1, y1))
    gate1, gated1_near, gated1_far = gate_product(a1, y1, q1, q1_far, n_rows)

    dy1, dgate1_near, dgate1_far = dgated_product(dbranch1, y1, gate1, q1, q1_far, n_rows)
    gq1 = gradient_q(a1, a1_far, dbranch1, dbranch1_far, gated1_near, gated1_far, dgate1_near, dgate1_far)
    sq1 = summed(gq1)
    branch1 = branch_product(gated1_near, gated1_far, q1, q1_far, n_rows)
    lr1, dstate1, dpart1, ddt1, dvec1 = rec(parts1, act1, after(dy1, gq1, branch1), wdt1, vec1, masks, False)
    out1 = h1 + valid * scatter(branch1)[0]
    dparts1 = [dpart1] + peers(dpart1)
    dstate1 = after(dstate1, out1)
    dx1_near, dx1_far, dsmall1, dconv1 = conv_bwd(dparts1, x1, act1, dstate1, masks, vec1, cat1)
    dnormed1 = dnormed_product(
        [dx1_near, dx1_far, dgate1_near, dgate1_far], p1, p1_far, q1, q1_far, n_rows)
    scaled1, come1 = scatter(dnormed1)
    dh1 = input_gradient(h1, dout1, scaled1)
    gp1 = gradient_p(a1, a1_far, after(dx1_near, come1[0]), dx1_far, dsmall1, ddt1, dconv1, dvec1)
    sp1 = summed(after(gp1, sq1))
    dout0 = dh1.astype(BF).astype(F32)
    dbranch0 = group((valid * dout0).astype(BF))

    q_parts1 = collected(1, after(sq1, dbranch0))
    dbranch0_far = section(dbranch0)
    dy0, dgate0_near, dgate0_far = dgated_product(after(dbranch0, gp1), y0, gate0, q0, q0_far, n_rows)
    gq0 = gradient_q(a0, a0_far, dbranch0, dbranch0_far, gated0_near, gated0_far, dgate0_near, dgate0_far)
    lr0, dstate0, dpart0, ddt0, dvec0 = rec(parts0, act0, after(dy0, gq0, sp1), wdt0, vec0, masks, False)
    p_parts1 = collected(1, sp1)
    sq0 = summed(after(gq0, sp1))
    dparts0 = [dpart0] + peers(dpart0)
    dstate0 = after(dstate0, *q_parts1, *p_parts1)
    dx0_near, dx0_far, dsmall0, dconv0 = conv_bwd(dparts0, x0, act0, dstate0, masks, vec0, cat0)
    gp0 = gradient_p(a0, a0_far, dx0_near, dx0_far, dsmall0, ddt0, dconv0, dvec0)
    sp0 = summed(after(gp0, sq0))
    q_parts0 = collected(0, sq0)
    dnormed0 = dnormed_product(
        [after(dx0_near, gp0), dx0_far, dgate0_near, dgate0_far], p0, p0_far, q0, q0_far, n_rows)
    p_parts0 = collected(0, after(sp0, dnormed0, *q_parts0))
    dh0 = input_gradient(h0, dout0, after(scatter(dnormed0)[0], p_parts0[0]))

    out_far = directed(out1, "section", [(0, 1)])
    dh_far = directed(dh0, "section", [(1, 0)])
    result = jnp.stack([pick(dh0, out_far), pick(dh_far, out1)]).reshape(1, 2, 1, length, width)

    grad_in, sum_q, grad_out = join_packed(
        join_q_body, where, in_weight[0], gain, q_parts0 + q_parts1, None, 1, n_dp, [shape((block, width), F32)])
    smalls = [shape(v, F32) for v in ((block, RANK), (2 * STATE, block), (RANK, block), (4, block))]
    smalls += [shape((1, block), F32)] * 3
    grad_in, sum_p, grad_down, grad_kq, grad_dt, grad_conv, grad_cb, grad_db, grad_skip = join_packed(
        join_p_body, where, in_weight[0], gain, p_parts0 + p_parts1, grad_in, 0, n_dp, smalls,
        [pltpu.VMEM((SMALL, block), F32)])
    grad_gain = jnp.sum(sum_q + sum_p, axis=1)
    return (
        result,
        grad_gain[None],
        grad_in[None],
        grad_conv[None],
        grad_cb,
        grad_down[None],
        grad_kq[None],
        grad_dt[None],
        grad_db,
        grad_skip,
        grad_out[None],
    )


def solution(mesh):
    packed = mesh.shape["dp"] == 4 and mesh.shape["grp"] == 4
    return jax.shard_map(
        on_device if packed else on_any_line,
        mesh=mesh,
        in_specs=(
            P("section", None, ("grp", "dp"), None, None),
            P(None, ("grp", "dp"), None),
            P("section", "dp"),
            P("section", "dp", None),
            P("section", None, "dp"),
            P("section", "dp"),
            P("section", "dp", None),
            P("section", None, "dp"),
            P("section", None, "dp"),
            P("section", "dp"),
            P("section", "dp"),
            P("section", "dp", None),
        ),
        out_specs=(
            P("section", None, ("grp", "dp"), None, None),
            P("section", "dp"),
            P("section", "dp", None),
            P("section", None, "dp"),
            P("section", "dp"),
            P("section", "dp", None),
            P("section", None, "dp"),
            P("section", None, "dp"),
            P("section", "dp"),
            P("section", "dp"),
            P("section", "dp", None),
        ),
        check_vma=False,
    )
```

```python
from functools import partial

import jax
import jax.numpy as jnp
from jax import lax
from jax.experimental import pallas as pl
from jax.experimental.pallas import tpu as pltpu
from jax.sharding import PartitionSpec as P

EPSILON = 1e-05
BF = jnp.bfloat16
F32 = jnp.float32
STATE = 16
RANK = 128
LANES = 128
ROWS = 8
MIB = 1024 * 1024


def dot(left, right, left_axis, right_axis, kind=F32):
    return lax.dot_general(
        left, right, (((left_axis,), (right_axis,)), ((), ())), preferred_element_type=kind
    )


def sig(value):
    return 1.0 / (1.0 + jnp.exp(-value))


def swap(value, axis, shift):
    return lax.ppermute(value, axis, [(i, i ^ shift) for i in range(lax.axis_size(axis))])


def directed(value, axis, pairs):
    return lax.ppermute(value, axis, pairs)


def peers(value):
    return [swap(value, "grp", d) for d in range(1, lax.axis_size("grp"))]


def call(body, out_shape, **kwargs):
    limit = kwargs.pop("vmem", 48)
    return pl.pallas_call(
        body,
        out_shape=out_shape,
        compiler_params=pltpu.CompilerParams(vmem_limit_bytes=limit * MIB),
        **kwargs,
    )


def cost(flops):
    return pl.CostEstimate(flops=int(1 * flops), bytes_accessed=0, transcendentals=0)


def shape(dims, kind):
    return jax.ShapeDtypeStruct(dims, kind)


def proj_body(a_ref, near_ref, far_ref, out_ref, *, w_axis):
    @pl.when(pl.program_id(0) == 0)
    def _():
        out_ref[...] = dot(a_ref[...], near_ref[...], 1, w_axis)

    @pl.when(pl.program_id(0) == 1)
    def _():
        out_ref[...] = dot(a_ref[...], far_ref[...], 1, w_axis)


def proj(a, near, far, w_axis):
    rows = a.shape[0]
    half = near.shape[1 - w_axis]

    def whole(v):
        return pl.BlockSpec(v.shape, lambda i: (0,) * v.ndim)

    return call(
        partial(proj_body, w_axis=w_axis),
        shape((rows, 2 * half), F32),
        grid=(2,),
        in_specs=[whole(a), whole(near), whole(far)],
        out_specs=pl.BlockSpec((rows, half), lambda i: (0, i)),
        cost_estimate=cost(4 * rows * half * a.shape[1]),
    )(a, near, far)


def total_body(n, w_axis, *refs):
    lefts, rights, out_ref = refs[:n], refs[n : 2 * n], refs[2 * n]
    total = dot(lefts[0][...], rights[0][...], 1, w_axis)
    for left, right in zip(lefts[1:], rights[1:]):
        total = total + dot(left[...], right[...], 1, w_axis)
    out_ref[...] = total.astype(BF)


def total_of(lefts, rights, w_axis):
    rows = lefts[0].shape[0]
    width = rights[0].shape[1 - w_axis]
    step = 512

    def left_spec(v):
        return pl.BlockSpec(v.shape, lambda i: (0, 0))

    def right_spec(v):
        if w_axis == 0:
            return pl.BlockSpec((v.shape[0], step), lambda i: (0, i))
        return pl.BlockSpec((step, v.shape[1]), lambda i: (i, 0))

    return call(
        partial(total_body, len(lefts), w_axis),
        shape((rows, width), BF),
        grid=(width // step,),
        in_specs=[left_spec(v) for v in lefts] + [right_spec(v) for v in rights],
        out_specs=pl.BlockSpec((rows, step), lambda i: (0, i)),
        cost_estimate=cost(2 * rows * width * sum(v.shape[1] for v in lefts)),
    )(*lefts, *rights)


def conv_of(x_ref, rows, pad_ref, mask_ref, vec_ref, cols):
    length = pad_ref.shape[0] - ROWS
    x = x_ref[rows, cols]
    pad_ref[0:ROWS, :] = jnp.zeros((ROWS, LANES), F32)
    pad_ref[ROWS : ROWS + length, :] = x
    total = vec_ref[4:5, cols] + vec_ref[0:1, cols] * x
    shifted = []
    for j in (1, 2, 3):
        earlier = pad_ref[ROWS - j : ROWS - j + length, :] * mask_ref[rows, j * LANES : (j + 1) * LANES]
        shifted.append(earlier)
        total = total + vec_ref[j : j + 1, cols] * earlier
    return total, shifted


def proj_conv_body(n_slots, a_ref, near_ref, far_ref, mask_ref, vec_ref, cat_ref, x_ref, inner_ref, part_ref,
                   pad_ref, sum_ref):
    i = pl.program_id(0)
    rows_all, half = x_ref.shape
    length = rows_all // n_slots

    @pl.when(i == 0)
    def _():
        x_ref[...] = dot(a_ref[...], near_ref[...], 1, 0)

    @pl.when(i == 1)
    def _():
        x_ref[...] = dot(a_ref[...], far_ref[...], 1, 0)

    for j in range(n_slots):
        rows = slice(j * length, (j + 1) * length)
        for b in range(half // LANES):
            cols = slice(b * LANES, (b + 1) * LANES)
            c, _ = conv_of(x_ref, rows, pad_ref, mask_ref, vec_ref, cols)
            inner_ref[rows, cols] = (c * sig(c)).astype(BF)
    both = dot(inner_ref[...], cat_ref[...], 1, 1)

    @pl.when(i == 0)
    def _():
        sum_ref[...] = both

    @pl.when(i == 1)
    def _():
        total = sum_ref[...] + both
        part_ref[...] = pack(total[:, :RANK], total[:, RANK:])


def proj_conv(n_slots, a, near, far, masks, vec, cat):
    rows = a.shape[0]
    half = near.shape[1]

    def whole(v):
        return pl.BlockSpec(v.shape, lambda i: (0,) * v.ndim)

    def block(n):
        return pl.BlockSpec((n, half), lambda i: (0, i))

    part_like = shape((rows, 2 * LANES), BF)
    return call(
        partial(proj_conv_body, n_slots),
        (shape((rows, 2 * half), F32), shape((rows, 2 * half), BF), part_like),
        grid=(2,),
        in_specs=[whole(a), whole(near), whole(far), whole(masks), block(vec.shape[0]), block(cat.shape[0])],
        out_specs=(block(rows), block(rows), whole(part_like)),
        scratch_shapes=[pltpu.VMEM((ROWS + rows // n_slots, LANES), F32), pltpu.VMEM((rows, 2 * LANES), F32)],
        cost_estimate=cost(4 * rows * half * a.shape[1]),
    )(a, near, far, masks, vec, cat)


def pack(low_rank, kq):
    high = kq.astype(BF).astype(F32)
    rest = pltpu.roll(kq - high, 64, axis=1)
    return jnp.concatenate([low_rank, high + rest], axis=1).astype(BF)


def summed_parts(parts, j, length):
    low_rank = jnp.zeros((length, RANK), F32)
    kq = jnp.zeros((length, LANES), F32)
    for d, part in enumerate(parts):
        rows = slice((j ^ d) * length, ((j ^ d) + 1) * length)
        low_rank = low_rank + part[rows, :RANK].astype(F32)
        kq = kq + part[rows, RANK:].astype(F32)
    kq = kq + pltpu.roll(kq, 64, axis=1)
    lane = lax.broadcasted_iota(jnp.int32, (1, LANES), 1)
    return low_rank, jnp.where(lane < 2 * STATE, kq, 0.0)


def rec_body(backward, keep_y, n_slots, length, width, *refs):
    parts, refs = refs[:n_slots], refs[n_slots:]
    y_out = None
    if backward:
        (inner, dy_ref, wdt, vec, mask, lr_out, dstate_out, dpart_out, ddt_out, dvec_out), refs = refs[:10], refs[10:]
        if keep_y:
            y_out, refs = refs[0], refs[1:]
        (kq_n, kq_i, c_i, lr_n, step_i, p_i, y_i, kb, str_n, hist, dy_i, a_i, h_scr, dkq_i,
         dlr_n, corr_n, prod, drate_n) = refs
    else:
        (inner, wdt, vec, mask, y_out, kq_n, kq_i, c_i, lr_n, step_i, p_i, y_i, kb, state) = refs
    nb = width // (2 * LANES)
    first = pl.program_id(0) == 0
    last = pl.program_id(0) == pl.num_programs(0) - 1
    lane = lax.broadcasted_iota(jnp.int32, (1, LANES), 1)
    pieces = [(hh, b, slice((hh * nb + b) * LANES, (hh * nb + b + 1) * LANES)) for hh in (0, 1) for b in range(nb)]

    def rows_of(j):
        return slice(j * length, (j + 1) * length)

    def spread(j, hh):
        return pl.ds(hh * n_slots + j, length, stride=ROWS)

    @pl.when(first)
    def _():
        for j in range(n_slots):
            low_rank, kq = summed_parts(parts, j, length)
            lr_n[rows_of(j), :] = low_rank.astype(BF)
            if backward:
                lr_out[rows_of(j), :] = low_rank.astype(BF)
            kq_n[rows_of(j), :] = kq
            for hh in (0, 1):
                kq_i[spread(j, hh), :] = kq
                c_i[spread(j, hh), :] = mask[rows_of(j), 0:LANES]
        kq = kq_i[...]
        high = kq.astype(BF).astype(F32)
        split = (high + pltpu.roll(kq - high, 64, axis=1)).astype(BF)
        source = lax.broadcasted_iota(jnp.int32, (LANES, 2 * LANES), 0) % 64
        column = lax.broadcasted_iota(jnp.int32, (LANES, 2 * LANES), 1) // LANES
        for n in range(0, 2 * STATE, 2):
            copied = dot(split, jnp.where(source == n + column, 1.0, 0.0).astype(BF), 1, 0)
            kb[n] = copied[:, :LANES]
            kb[n + 1] = copied[:, LANES:]
        if backward:
            dkq_i[...] = jnp.zeros(dkq_i.shape, F32)
            dlr_n[...] = jnp.zeros(dlr_n.shape, F32)
            corr_n[...] = jnp.zeros(corr_n.shape, F32)

    for j in range(n_slots):
        rows = rows_of(j)
        rate = dot(lr_n[rows, :], wdt[...], 1, 0)
        kq = kq_n[rows, :]
        ks = jnp.sum(jnp.where(lane < STATE, kq * kq, 0.0), axis=1, keepdims=True)
        for hh, b, cols in pieces:
            strength = sig(rate[:, cols] + vec[5:6, cols])
            step = strength / (1.0 + strength * ks)
            step_i[b, spread(j, hh), :] = step
            p_i[b, spread(j, hh), :] = step * inner[rows, cols].astype(F32)
            if backward:
                str_n[rows, cols] = strength
                dy_i[b, spread(j, hh), :] = dy_ref[rows, cols]

    if backward:
        hist[0] = jnp.zeros(hist.shape[1:], F32)
    else:
        state[...] = jnp.zeros(state.shape, F32)

    def forward_step(t, carry):
        now = pl.ds(pl.multiple_of(t * ROWS, ROWS), ROWS)
        c = c_i[now, :]
        steps = [step_i[b, now, :] for b in range(nb)]
        ps = [p_i[b, now, :] for b in range(nb)]
        ys = [jnp.zeros((ROWS, LANES), F32) for _ in range(nb)]
        for n in range(STATE):
            k = kb[n, now, :]
            ck2 = c * k * k
            if y_out is not None:
                q = kb[STATE + n, now, :]
            for b in range(nb):
                before = hist[t, n * nb + b] if backward else state[n * nb + b]
                after = (c - ck2 * steps[b]) * before + k * ps[b]
                if backward:
                    hist[t + 1, n * nb + b] = after
                else:
                    state[n * nb + b] = after
                if y_out is not None:
                    ys[b] = ys[b] + q * after
        if y_out is not None:
            for b in range(nb):
                y_i[b, now, :] = ys[b]
        return carry

    lax.fori_loop(0, length, forward_step, 0, unroll=4)

    if y_out is not None:
        for j in range(n_slots):
            rows = rows_of(j)
            for hh, b, cols in pieces:
                y_out[rows, cols] = y_i[b, spread(j, hh), :] + vec[6:7, cols] * inner[rows, cols].astype(F32)
    if not backward:
        return

    h_scr[...] = jnp.zeros(h_scr.shape, F32)

    def backward_step(i, carry):
        t = length - 1 - i
        at = pl.ds(pl.multiple_of(t * 2 * ROWS, 2 * ROWS), 2 * ROWS)
        now = pl.ds(pl.multiple_of(t * ROWS, ROWS), ROWS)
        c = c_i[now, :]
        steps = [step_i[b, now, :] for b in range(nb)]
        ps = [p_i[b, now, :] for b in range(nb)]
        dys = [dy_i[b, now, :] for b in range(nb)]
        a_sum = [jnp.zeros((ROWS, LANES), F32) for _ in range(nb)]
        b_sum = [jnp.zeros((ROWS, LANES), F32) for _ in range(nb)]
        for n in range(STATE):
            k, q = kb[n, now, :], kb[STATE + n, now, :]
            ck = c * k
            ck2 = ck * k
            dk1 = dk2 = dq = None
            for b in range(nb):
                before, after = hist[t, n * nb + b], hist[t + 1, n * nb + b]
                grad = dys[b] * q + h_scr[n * nb + b]
                a_sum[b] = a_sum[b] + grad * k
                both = grad * before
                b_sum[b] = b_sum[b] + ck2 * both
                h_scr[n * nb + b] = (c - ck2 * steps[b]) * grad
                one, two, three = ps[b] * grad, steps[b] * both, dys[b] * after
                dk1 = one if dk1 is None else dk1 + one
                dk2 = two if dk2 is None else dk2 + two
                dq = three if dq is None else dq + three
            dk = dk1 - (2.0 * ck) * dk2
            prod[at, n * LANES : (n + 1) * LANES] = jnp.concatenate([dk, dq], axis=0).astype(BF)
        for b in range(nb):
            a_i[b, now, :] = a_sum[b]
            p_i[b, now, :] = b_sum[b]
        return carry

    lax.fori_loop(0, length, backward_step, 0, unroll=4)

    source = lax.broadcasted_iota(jnp.int32, (STATE * LANES, LANES), 0) // LANES
    sums = jnp.where(source == lax.broadcasted_iota(jnp.int32, (STATE * LANES, LANES), 1), 1.0, 0.0).astype(BF)
    dkq_i[...] = dkq_i[...] + dot(prod[...], sums, 1, 0)

    ddt = [jnp.zeros((1, LANES), F32) for _ in pieces]
    dskip = [jnp.zeros((1, LANES), F32) for _ in pieces]
    for j in range(n_slots):
        rows = rows_of(j)
        kq = kq_n[rows, :]
        ks = jnp.sum(jnp.where(lane < STATE, kq * kq, 0.0), axis=1, keepdims=True)
        corr = jnp.zeros((length, 1), F32)
        for i, (hh, b, cols) in enumerate(pieces):
            at = spread(j, hh)
            inn = inner[rows, cols].astype(F32)
            a, step, dy = a_i[b, at, :], step_i[b, at, :], dy_ref[rows, cols]
            dstep = inn * a - p_i[b, at, :]
            strength = str_n[rows, cols]
            inv = 1.0 / (1.0 + strength * ks)
            drate = (dstep * (inv * inv) * (strength * (1.0 - strength))).astype(BF)
            drate_n[rows, cols] = drate
            dstate_out[rows, cols] = step * a + vec[6:7, cols] * dy
            corr = corr + jnp.sum(dstep * (step * step), axis=1, keepdims=True)
            ddt[i] = ddt[i] + jnp.sum(drate.astype(F32), axis=0, keepdims=True)
            dskip[i] = dskip[i] + jnp.sum(dy * inn, axis=0, keepdims=True)
        corr_n[rows, :] = corr_n[rows, :] + corr
        dlr_n[rows, :] = dlr_n[rows, :] + dot(drate_n[rows, :], wdt[...], 1, 1)
    ddt_out[...] = dot(lr_n[...], drate_n[...], 0, 0)
    dvec_out[...] = jnp.concatenate(
        [jnp.concatenate(ddt, axis=1), jnp.concatenate(dskip, axis=1), jnp.zeros((6, width), F32)], axis=0
    )

    @pl.when(last)
    def _():
        for j in range(n_slots):
            rows = rows_of(j)
            dk, dq = [
                dkq_i[pl.ds(m * ROWS + j, length, stride=2 * ROWS), :]
                + dkq_i[pl.ds(m * ROWS + n_slots + j, length, stride=2 * ROWS), :]
                for m in (0, 1)
            ]
            dkq = dk + pltpu.roll(dq, STATE, axis=1)
            dkq = dkq - jnp.where(lane < STATE, 2.0 * kq_n[rows, :] * corr_n[rows, :], 0.0)
            dpart_out[rows, :] = dlr_n[rows, :].astype(BF)
            dkq = jnp.where(lane < 2 * STATE, dkq, 0.0)
            packed = dkq if j == 0 else packed + pltpu.roll(dkq, 2 * STATE * j, axis=1)
        dpart_out[n_slots * length :, :] = packed.astype(BF)


def rec(parts, inner, dy, wdt, vec, masks, keep_y):
    rows, channels = inner.shape
    n_slots = len(parts)
    length = rows // n_slots
    width = channels // 2
    nb = width // (2 * LANES)

    def whole(a):
        return pl.BlockSpec(a.shape, lambda i: (0,) * a.ndim)

    def block(n):
        return pl.BlockSpec((n, width), lambda i: (0, i))

    wide = pltpu.VMEM((nb, ROWS * length, LANES), F32)
    row = pltpu.VMEM((rows, LANES), F32)
    spread = pltpu.VMEM((ROWS * length, LANES), F32)
    y_like = shape((rows, channels), F32)
    y_scratch = wide if dy is None or keep_y else pltpu.VMEM((ROWS, LANES), F32)
    scratch = [row, spread, spread, pltpu.VMEM((rows, RANK), BF), wide, wide, y_scratch]
    scratch += [pltpu.VMEM((2 * STATE, ROWS * length, LANES), F32)]
    if dy is None:
        scratch += [pltpu.VMEM((STATE * nb, ROWS, LANES), F32)]
        return call(
            partial(rec_body, False, True, n_slots, length, width),
            y_like,
            grid=(2,),
            in_specs=[whole(p) for p in parts] + [block(rows), block(RANK), block(vec.shape[0]), pl.BlockSpec((rows, LANES), lambda i: (0, 0))],
            out_specs=block(rows),
            scratch_shapes=scratch,
            cost_estimate=cost(20e9),
        )(*parts, inner, wdt, vec, masks)
    scratch += [
        pltpu.VMEM((rows, width), F32),
        pltpu.VMEM((length + 1, STATE * nb, ROWS, LANES), F32),
        wide,
        wide,
        pltpu.VMEM((STATE * nb, ROWS, LANES), F32),
        pltpu.VMEM((2 * ROWS * length, LANES), F32),
        pltpu.VMEM((rows, RANK), F32),
        row,
        pltpu.VMEM((2 * ROWS * length, STATE * LANES), BF),
        pltpu.VMEM((rows, width), BF),
    ]
    lr_like = shape((rows, RANK), BF)
    part_like = shape((rows + length, LANES), BF)
    outs = [lr_like, y_like, part_like, shape((RANK, channels), F32), shape((ROWS, channels), F32)]
    specs = [whole(lr_like), block(rows), whole(part_like), block(RANK), block(ROWS)]
    if keep_y:
        outs, specs = outs + [y_like], specs + [block(rows)]
    return call(
        partial(rec_body, True, keep_y, n_slots, length, width),
        tuple(outs),
        grid=(2,),
        in_specs=[whole(p) for p in parts] + [block(rows), block(rows), block(RANK), block(vec.shape[0]), pl.BlockSpec((rows, LANES), lambda i: (0, 0))],
        out_specs=tuple(specs),
        scratch_shapes=scratch,
        cost_estimate=cost(55e9),
        vmem=62,
    )(*parts, inner, dy, wdt, vec, masks)


def gate_values(y, gate):
    s = sig(gate)
    return y * (gate * s), y * (s * (1.0 + gate * (1.0 - s)))


def gate_back_body(y_ref, gate_ref, dgated_ref, gated_near, gated_far, dgate_near, dgate_far):
    half = gated_near.shape[1]
    for h, (gated, dgate) in enumerate([(gated_near, dgate_near), (gated_far, dgate_far)]):
        for b in range(half // LANES):
            cols = slice(b * LANES, (b + 1) * LANES)
            at = slice(h * half + b * LANES, h * half + (b + 1) * LANES)
            one, two = gate_values(y_ref[:, at], gate_ref[:, at])
            gated[:, cols] = one.astype(BF)
            dgate[:, cols] = (dgated_ref[:, at] * two).astype(BF)


def gate_back(n_slots, y, gate, dgated):
    rows, channels = y.shape
    length = rows // n_slots
    side = shape((rows, channels // 2), BF)
    return call(
        gate_back_body,
        (side,) * 4,
        grid=(n_slots,),
        in_specs=[pl.BlockSpec((length, channels), lambda j: (j, 0))] * 3,
        out_specs=[pl.BlockSpec((length, channels // 2), lambda j: (j, 0))] * 4,
        cost_estimate=cost(3e9),
    )(y, gate, dgated)


def conv_bwd_body(n_slots, p0, p1, p2, p3, x_ref, inner, dstate, mask_ref, vec_ref, wdk_ref,
                  dx_near, dx_far, dsmall_out, dvec_out, pad_ref, late_ref, dcat):
    j = pl.program_id(0)
    length, channels = x_ref.shape
    lane = lax.broadcasted_iota(jnp.int32, (1, LANES), 1)

    @pl.when(j == 0)
    def _():
        dsmall_out[...] = jnp.zeros(dsmall_out.shape, F32)
        dvec_out[...] = jnp.zeros(dvec_out.shape, F32)

    low_rank = jnp.zeros((length, RANK), F32)
    kq = jnp.zeros((length, LANES), F32)
    for d, part in enumerate((p0, p1, p2, p3)):
        rows = pl.ds(pl.multiple_of((j ^ d) * length, length), length)
        low_rank = low_rank + part[rows, :].astype(F32)
        packed = part[n_slots * length :, :].astype(F32)
        mine = packed
        for n in range(1, n_slots):
            mine = jnp.where((j ^ d) == n, pltpu.roll(packed, LANES - 2 * STATE * n, axis=1), mine)
        kq = kq + mine
    dcat[:, :RANK] = low_rank.astype(BF)
    dcat[:, RANK:] = jnp.where(lane < 2 * STATE, kq, 0.0).astype(BF)
    dsmall_out[...] += dot(dcat[...], inner[...], 0, 0)
    late_ref[length : length + ROWS, :] = jnp.zeros((ROWS, LANES), F32)
    for b in range(channels // LANES):
        cols = slice(b * LANES, (b + 1) * LANES)
        c, earlier = conv_of(x_ref, slice(0, length), pad_ref, mask_ref, vec_ref, cols)
        dinner = dstate[:, cols] + dot(dcat[...], wdk_ref[:, cols], 1, 0)
        s = sig(c)
        dc = dinner * (s * (1.0 + c * (1.0 - s)))
        dx = vec_ref[0:1, cols] * dc
        sums = [jnp.sum(dc * x_ref[:, cols], axis=0, keepdims=True)]
        for lag in (1, 2, 3):
            sums.append(jnp.sum(dc * earlier[lag - 1], axis=0, keepdims=True))
            late_ref[0:length, :] = dc * mask_ref[:, lag * LANES : (lag + 1) * LANES]
            dx = dx + vec_ref[lag : lag + 1, cols] * late_ref[lag : lag + length, :]
        sums.append(jnp.sum(dc, axis=0, keepdims=True))
        half = channels // 2
        dx_out = dx_near if b * LANES < half else dx_far
        dx_out[:, (b * LANES) % half : (b * LANES) % half + LANES] = dx.astype(BF)
        for i, value in enumerate(sums):
            dvec_out[i : i + 1, cols] += value


def conv_bwd(parts, x, inner, dstate, masks, vec, wdk):
    rows, channels = x.shape
    n_slots = len(parts)
    length = rows // n_slots

    def whole(a):
        return pl.BlockSpec(a.shape, lambda i: (0,) * a.ndim)

    slot = pl.BlockSpec((length, channels), lambda j: (j, 0))
    slot_half = pl.BlockSpec((length, channels // 2), lambda j: (j, 0))
    side = shape((rows, channels // 2), BF)
    small = shape((2 * LANES, channels), F32)
    vecs = shape((ROWS, channels), F32)
    return call(
        partial(conv_bwd_body, n_slots),
        (side, side, small, vecs),
        grid=(n_slots,),
        in_specs=[whole(p) for p in parts]
        + [slot, slot, slot, pl.BlockSpec((length, 4 * LANES), lambda j: (j, 0)), whole(vec), whole(wdk)],
        out_specs=(slot_half, slot_half, whole(small), whole(vecs)),
        scratch_shapes=[
            pltpu.VMEM((ROWS + length, LANES), F32),
            pltpu.VMEM((ROWS + length, LANES), F32),
            pltpu.VMEM((length, 2 * LANES), BF),
        ],
    )(*parts, x, inner, dstate, masks, vec, wdk)


SMALL = 448
DOWN, KQ, DT, VEC = 0, 128, 160, 288


def cut_small_body(where_ref, w_ref, gain_ref, *refs):
    sources, (keep_ref, send_ref, small), fetched, sems = refs[:7], refs[7:10], refs[10:17], refs[17]
    i = pl.program_id(0)
    rows, sub = w_ref.shape[0], keep_ref.shape[1]
    part = keep_ref.shape[0] - rows
    copies = [pltpu.make_async_copy(v, f, sems.at[n]) for n, (v, f) in enumerate(zip(sources, fetched))]

    @pl.when(i == 0)
    def _():
        for copy in copies:
            copy.start()

    mine = where_ref[1] == 0
    scaled = w_ref[...].astype(F32) * gain_ref[...]
    first, second = scaled[:, :sub].astype(BF), scaled[:, sub:].astype(BF)
    keep_ref[0:rows, :] = jnp.where(mine, first, second)
    send_ref[0:rows, :] = jnp.where(mine, second, first)

    @pl.when(i == 0)
    def _():
        for copy in copies:
            copy.wait()
        down, kq, dt, conv, conv_bias, dt_bias, skip = fetched
        at = pl.ds(pl.multiple_of(where_ref[0] * 2 * sub, 2 * sub), 2 * sub)
        small[DOWN:KQ, :] = down[at, :].astype(F32).T.astype(BF)
        small[KQ:DT, :] = kq[:, at]
        small[DT:VEC, :] = dt[:, at]
        last = [v[:, at].astype(F32) for v in (conv, conv_bias, dt_bias, skip)] + [jnp.zeros((9, 2 * sub), F32)]
        small[VEC : VEC + 16, :] = jnp.concatenate(last, axis=0).astype(BF)
        small[VEC + 16 :, :] = jnp.zeros((SMALL - VEC - 16, 2 * sub), BF)

    piece = small[pl.ds(pl.multiple_of(i * part, 16), part), :]
    first, second = piece[:, :sub], piece[:, sub:]
    keep_ref[rows:, :] = jnp.where(mine, first, second)
    send_ref[rows:, :] = jnp.where(mine, second, first)


def cut_small(where, weight, gain, down, kq, dt, conv, conv_bias, dt_bias, skip, n_dp, n_grp, sub):
    rows = weight.shape[0]
    part = SMALL // n_dp
    out = shape((rows + part, n_dp * sub), BF)
    smalls = [down, kq, dt, conv, conv_bias, dt_bias, skip]
    return call(
        cut_small_body,
        (out, out),
        grid_spec=pltpu.PrefetchScalarGridSpec(
            num_scalar_prefetch=1,
            grid=(n_dp,),
            in_specs=[
                pl.BlockSpec((rows, 2 * sub), lambda i, w: (0, i * n_grp + w[0])),
                pl.BlockSpec((rows, 1), lambda i, w: (0, 0)),
            ]
            + [pl.BlockSpec(memory_space=pltpu.HBM)] * 7,
            out_specs=[pl.BlockSpec((rows + part, sub), lambda i, w: (0, i))] * 2,
            scratch_shapes=[pltpu.VMEM((SMALL, 2 * sub), BF)]
            + [pltpu.VMEM(v.shape, BF) for v in smalls]
            + [pltpu.SemaphoreType.DMA((7,))],
        ),
        cost_estimate=cost(3e9),
        vmem=62,
    )(where, weight, gain, *smalls)


def cut_out_body(where_ref, w_ref, gain_ref, o_ref, keep_ref, send_ref):
    i = pl.program_id(0)
    rows, sub = w_ref.shape[0], keep_ref.shape[1]
    mine = where_ref[1] == 0
    scaled = w_ref[...].astype(F32) * gain_ref[...]
    first, second = scaled[:, :sub].astype(BF), scaled[:, sub:].astype(BF)
    keep_ref[0:rows, :] = jnp.where(mine, first, second)
    send_ref[0:rows, :] = jnp.where(mine, second, first)
    n = pl.num_programs(0)
    wide = o_ref.shape[1] // 4
    for c in range(4):
        lanes = pl.ds(pl.multiple_of(c * wide + i * sub, sub), sub)
        first, second = o_ref[0:sub, lanes], o_ref[sub:, lanes]
        at = slice(rows + c * sub, rows + (c + 1) * sub)
        keep_ref[at, :] = jnp.where(mine, first, second)
        send_ref[at, :] = jnp.where(mine, second, first)


def cut_out(where, weight, gain, out_weight, n_dp, n_grp, sub):
    rows = weight.shape[0]
    out = shape((rows + 4 * sub, n_dp * sub), BF)
    return call(
        cut_out_body,
        (out, out),
        grid_spec=pltpu.PrefetchScalarGridSpec(
            num_scalar_prefetch=1,
            grid=(n_dp,),
            in_specs=[
                pl.BlockSpec((rows, 2 * sub), lambda i, w: (0, (n_dp + i) * n_grp + w[0])),
                pl.BlockSpec((rows, 1), lambda i, w: (0, 0)),
                pl.BlockSpec((2 * sub, out_weight.shape[1]), lambda i, w: (w[0], 0)),
            ],
            out_specs=[pl.BlockSpec((rows + 4 * sub, sub), lambda i, w: (0, i))] * 2,
        ),
        cost_estimate=cost(3e9),
    )(where, weight, gain, out_weight)


def flat_call(body, out_shape, arrays, specs=None, scratch=(), flops=0, vmem=48):
    def whole(v):
        return pl.BlockSpec(v.shape, lambda i: (0,) * len(v.shape))

    outs = out_shape if isinstance(out_shape, tuple) else (out_shape,)
    out_specs = tuple(whole(v) for v in outs)
    return call(
        body,
        out_shape,
        grid=(1,),
        in_specs=[(specs or {}).get(n, whole(v)) for n, v in enumerate(arrays)],
        out_specs=out_specs if isinstance(out_shape, tuple) else out_specs[0],
        scratch_shapes=list(scratch),
        cost_estimate=cost(flops),
        vmem=vmem,
    )(*arrays)


def q_block(q, which, rows):
    return pl.BlockSpec((q.shape[0], rows, q.shape[2]), lambda i: (0, which, 0))


def blocks_sum(a_ref, w_ref, rows):
    total = None
    for p in range(w_ref.shape[0]):
        term = dot(a_ref[:, p * rows : (p + 1) * rows], w_ref[p, 0:rows, :], 1, 0)
        total = term if total is None else total + term
    return total


def first_body(n_slots, rows, a_ref, mask_ref, near_ref, far_ref, *refs):
    x_ref, inner_ref, part_ref, cat_ref, wdt_ref, vec_ref, pad_ref, small = refs
    half = x_ref.shape[1] // 2
    n_dp = near_ref.shape[0]
    sub = half // n_dp
    length = x_ref.shape[0] // n_slots
    part = SMALL // n_dp
    for h, w_ref in enumerate((near_ref, far_ref)):
        for p in range(n_dp):
            lanes = slice(h * half + p * sub, h * half + (p + 1) * sub)
            for i in range(n_dp):
                small[i * part : (i + 1) * part, lanes] = w_ref[p, rows:, i * sub : (i + 1) * sub]
    cat_ref[0:DT, :] = small[0:DT, :]
    cat_ref[DT:, :] = jnp.zeros((cat_ref.shape[0] - DT, 2 * half), BF)
    wdt_ref[...] = small[DT:VEC, :]
    vec_ref[...] = small[VEC : VEC + 16, :].astype(F32)
    both = jnp.zeros((x_ref.shape[0], 2 * LANES), F32)
    for h, w_ref in enumerate((near_ref, far_ref)):
        lanes = slice(h * half, (h + 1) * half)
        x_ref[:, lanes] = blocks_sum(a_ref, w_ref, rows)
        for j in range(n_slots):
            at = slice(j * length, (j + 1) * length)
            for b in range(half // LANES):
                cols = slice(h * half + b * LANES, h * half + (b + 1) * LANES)
                c, _ = conv_of(x_ref, at, pad_ref, mask_ref, vec_ref, cols)
                inner_ref[at, cols] = (c * sig(c)).astype(BF)
        both = both + dot(inner_ref[:, lanes], cat_ref[:, lanes], 1, 1)
    part_ref[...] = pack(both[:, :RANK], both[:, RANK:])


def first_products(n_slots, a, masks, near, far, rows):
    n, half = a.shape[0], near.shape[2]
    return flat_call(
        partial(first_body, n_slots, rows),
        (
            shape((n, 2 * half), F32),
            shape((n, 2 * half), BF),
            shape((n, 2 * LANES), BF),
            shape((2 * LANES, 2 * half), BF),
            shape((RANK, 2 * half), BF),
            shape((16, 2 * half), F32),
        ),
        [a, masks, near, far],
        scratch=[pltpu.VMEM((ROWS + n // n_slots, LANES), F32), pltpu.VMEM((SMALL, 2 * half), BF)],
        flops=8e9,
    )


def gate_body(rows, a_ref, y_ref, near_ref, far_ref, gate_ref, gated_near, gated_far):
    half = gated_near.shape[1]
    for h, (w_ref, gated) in enumerate([(near_ref, gated_near), (far_ref, gated_far)]):
        at = slice(h * half, (h + 1) * half)
        gate = blocks_sum(a_ref, w_ref, rows)
        gate_ref[:, at] = gate
        gated[...] = (y_ref[:, at] * (gate * sig(gate))).astype(BF)


def gate_product(a, y, near, far, rows):
    half = near.shape[2]
    side = shape((a.shape[0], half), BF)
    return flat_call(
        partial(gate_body, rows),
        (shape(y.shape, F32), side, side),
        [a, y, near, far],
        specs={2: q_block(near, 0, rows), 3: q_block(far, 0, rows)},
        flops=6e9,
    )


def out_weight_of(near_ref, far_ref, w_scr):
    half = w_scr.shape[0] // 2
    n_dp = near_ref.shape[0]
    sub = half // n_dp
    wide = w_scr.shape[1] // 4
    for h, w_ref in enumerate((near_ref, far_ref)):
        for p in range(n_dp):
            for c in range(4):
                block = w_ref[p, c * sub : (c + 1) * sub, :]
                w_scr[h * half + p * sub : h * half + (p + 1) * sub, c * wide : (c + 1) * wide] = block


def branch_body(left_near, left_far, near_ref, far_ref, out_ref, w_scr):
    out_weight_of(near_ref, far_ref, w_scr)
    half = left_near.shape[1]
    wide = w_scr.shape[1] // 4
    for c in range(4):
        lanes = slice(c * wide, (c + 1) * wide)
        total = dot(left_near[...], w_scr[:half, lanes], 1, 0) + dot(left_far[...], w_scr[half:, lanes], 1, 0)
        out_ref[:, lanes] = total.astype(BF)


def branch_product(left_near, left_far, near, far, rows):
    half = near.shape[2]
    return flat_call(
        branch_body,
        shape((left_near.shape[0], 4 * half), BF),
        [left_near, left_far, near, far],
        specs={2: q_block(near, 1, rows), 3: q_block(far, 1, rows)},
        scratch=[pltpu.VMEM((2 * half, 4 * half), BF)],
        flops=5e9,
    )


def dgated_body(d_ref, y_ref, gate_ref, near_ref, far_ref, dy_ref, dgate_near, dgate_far, w_scr):
    out_weight_of(near_ref, far_ref, w_scr)
    half = dgate_near.shape[1]
    for h, dgate in enumerate((dgate_near, dgate_far)):
        at = slice(h * half, (h + 1) * half)
        dgated = dot(d_ref[...], w_scr[at, :], 1, 1)
        gate = gate_ref[:, at]
        dy_ref[:, at] = dgated * (gate * sig(gate))
        dgate[...] = (dgated * gate_values(y_ref[:, at], gate)[1]).astype(BF)


def dgated_product(dbranch, y, gate, near, far, rows):
    half = near.shape[2]
    side = shape((dbranch.shape[0], half), BF)
    return flat_call(
        dgated_body,
        (shape(y.shape, F32), side, side),
        [dbranch, y, gate, near, far],
        specs={3: q_block(near, 1, rows), 4: q_block(far, 1, rows)},
        scratch=[pltpu.VMEM((2 * half, dbranch.shape[1]), BF)],
        flops=6e9,
    )


def dnormed_body(rows, dx_near, dx_far, dg_near, dg_far, p_near, p_far, q_near, q_far, out_ref):
    total = dot(dx_near[...], p_near[0, 0:rows, :], 1, 1) + dot(dx_far[...], p_far[0, 0:rows, :], 1, 1)
    total = total + dot(dg_near[...], q_near[0], 1, 1) + dot(dg_far[...], q_far[0], 1, 1)
    out_ref[...] = total.astype(BF)


def dnormed_product(lefts, p_near, p_far, q_near, q_far, rows):
    n_dp, _, half = p_near.shape
    n = lefts[0].shape[0]
    left = pl.BlockSpec((n, half), lambda i: (0, 0))
    p_spec = pl.BlockSpec((1, p_near.shape[1], half), lambda i: (i, 0, 0))
    q_spec = pl.BlockSpec((1, rows, half), lambda i: (i, 0, 0))
    return call(
        partial(dnormed_body, rows),
        shape((n, n_dp * rows), BF),
        grid=(n_dp,),
        in_specs=[left] * 4 + [p_spec] * 2 + [q_spec] * 2,
        out_specs=pl.BlockSpec((n, rows), lambda i: (0, i)),
        cost_estimate=cost(8e9),
    )(*lefts, p_near, p_far, q_near, q_far)


def grad_p_body(a_ref, a_far, dx_ref, dx_come, small_ref, small_come, out_ref):
    rows = a_ref.shape[1]
    value = dot(a_ref[...], dx_ref[...], 0, 0) + dot(a_far[...], dx_come[...], 0, 0)
    out_ref[0, 0:rows, :] = value.astype(BF)
    out_ref[0, rows:, :] = (small_ref[...] + small_come[...].astype(F32)).astype(BF)


def grad_p(a, a_far, dx, dx_come, small, small_come, n_dp):
    rows = a.shape[1] // n_dp
    part = small.shape[0] // n_dp
    half = dx.shape[1]
    col = pl.BlockSpec((a.shape[0], rows), lambda i: (0, i))
    whole = pl.BlockSpec(dx.shape, lambda i: (0, 0))
    block = pl.BlockSpec((part, half), lambda i: (i, 0))
    return call(
        grad_p_body,
        shape((n_dp, rows + part, half), BF),
        grid=(n_dp,),
        in_specs=[col, col, whole, whole, block, block],
        out_specs=pl.BlockSpec((1, rows + part, half), lambda i: (i, 0, 0)),
        cost_estimate=cost(5e9),
    )(a, a_far, dx, dx_come, small, small_come)


def grad_q_body(a_ref, a_far, dg_ref, dg_come, gated_ref, gated_come, db_ref, db_far, out_ref):
    rows = a_ref.shape[1]
    sub = gated_ref.shape[1]
    wide = db_ref.shape[1] // 4
    value = dot(a_ref[...], dg_ref[...], 0, 0) + dot(a_far[...], dg_come[...], 0, 0)
    out_ref[0, 0:rows, :] = value.astype(BF)
    value = dot(gated_ref[...], db_ref[...], 0, 0) + dot(gated_come[...], db_far[...], 0, 0)
    for c in range(4):
        out_ref[0, rows + c * sub : rows + (c + 1) * sub, :] = value[:, c * wide : (c + 1) * wide].astype(BF)


def grad_q(a, a_far, dg, dg_come, gated, gated_come, db, db_far, n_dp):
    rows = a.shape[1] // n_dp
    half = dg.shape[1]
    sub = half // n_dp
    col = pl.BlockSpec((a.shape[0], rows), lambda i: (0, i))
    sub_col = pl.BlockSpec((a.shape[0], sub), lambda i: (0, i))

    def whole(v):
        return pl.BlockSpec(v.shape, lambda i: (0, 0))

    return call(
        grad_q_body,
        shape((n_dp, rows + 4 * sub, half), BF),
        grid=(n_dp,),
        in_specs=[col, col, whole(dg), whole(dg), sub_col, sub_col, whole(db), whole(db)],
        out_specs=pl.BlockSpec((1, rows + 4 * sub, half), lambda i: (i, 0, 0)),
        cost_estimate=cost(8e9),
    )(a, a_far, dg, dg_come, gated, gated_come, db, db_far)


def small_grads_body(dsmall, ddt, dconv, dvec, near_ref, far_ref, scr):
    half = near_ref.shape[1]
    sub = half // 4
    part = SMALL // 4
    scr[DOWN:DT, :] = dsmall[0:DT, :]
    scr[DT:VEC, :] = ddt[...]
    rows = [dconv[0:5, :], dvec[0:2, :], jnp.zeros((1, 2 * half), F32)]
    scr[VEC : VEC + 8, :] = jnp.concatenate(rows, axis=0)
    scr[VEC + 8 :, :] = jnp.zeros((SMALL - VEC - 8, 2 * half), F32)
    for block in range(4):
        at = slice(block * part, (block + 1) * part)
        for i in range(4):
            rows = slice(i * part, (i + 1) * part)
            lanes = slice(i * sub, (i + 1) * sub)
            near_ref[at, lanes] = scr[rows, block * sub : (block + 1) * sub]
            far_ref[at, lanes] = scr[rows, half + block * sub : half + (block + 1) * sub].astype(BF)


def small_grads(dsmall, ddt, dconv, dvec):
    half = ddt.shape[1] // 2
    return call(
        small_grads_body,
        (shape((SMALL, half), F32), shape((SMALL, half), BF)),
        scratch_shapes=[pltpu.VMEM((SMALL, 2 * half), F32)],
        cost_estimate=cost(2e9),
    )(dsmall, ddt, dconv, dvec)


def join_values(n_grp, where_ref, parts):
    mine = where_ref[1] == 0
    for d in range(n_grp):
        for h in (0, 1):
            sub = parts[0].shape[2]
            at = pl.ds(pl.multiple_of(((where_ref[0] ^ d) * 2 + h) * sub, sub), sub)
            yield at, jnp.where(mine, parts[d][h], parts[n_grp + d][h]).astype(F32)


def join_p_body(n_grp, n_dp, where_ref, w_ref, gain_ref, *refs):
    parts = refs[: 2 * n_grp]
    out_ref, sum_ref, down_ref, kq_ref, dt_ref, conv_ref, cb_ref, db_ref, skip_ref, small = refs[2 * n_grp + 1 :]
    i = pl.program_id(0)
    rows, sub = w_ref.shape[0], parts[0].shape[2]
    part = parts[0].shape[1] - rows

    @pl.when(i == 0)
    def _():
        sum_ref[...] = jnp.zeros(sum_ref.shape, F32)

    total = None
    for at, value in join_values(n_grp, where_ref, parts):
        out_ref[:, at] = value[:rows] * gain_ref[...]
        term = value[:rows] * w_ref[:, at].astype(F32)
        total = term if total is None else total + term
        small[pl.ds(pl.multiple_of(i * part, 16), part), at] = value[rows:]

    sum_ref[...] += total

    @pl.when(i == n_dp - 1)
    def _():
        for b in range(down_ref.shape[0] // LANES):
            at = slice(b * LANES, (b + 1) * LANES)
            down_ref[at, :] = small[DOWN:KQ, at].T
        kq_ref[...] = small[KQ:DT, :]
        dt_ref[...] = small[DT:VEC, :]
        conv_ref[...] = small[VEC : VEC + 4, :]
        cb_ref[...] = small[VEC + 4 : VEC + 5, :]
        db_ref[...] = small[VEC + 5 : VEC + 6, :]
        skip_ref[...] = small[VEC + 6 : VEC + 7, :]


def join_q_body(n_grp, n_dp, where_ref, w_ref, gain_ref, *refs):
    parts, out_ref, sum_ref, o_ref = refs[: 2 * n_grp], refs[-3], refs[-2], refs[-1]
    i = pl.program_id(0)
    rows, sub = w_ref.shape[0], parts[0].shape[2]
    wide = o_ref.shape[1] // 4

    @pl.when(i == 0)
    def _():
        sum_ref[...] = jnp.zeros(sum_ref.shape, F32)

    for at, value in join_values(n_grp, where_ref, parts):
        out_ref[:, at] = value[:rows] * gain_ref[...]
        sum_ref[...] += value[:rows] * w_ref[:, at].astype(F32)
        for c in range(4):
            lanes = pl.ds(pl.multiple_of(c * wide + i * sub, sub), sub)
            o_ref[at, lanes] = value[rows + c * sub : rows + (c + 1) * sub]


def join_packed(body, where, weight, gain, parts, before, side, n_dp, extras, scratch=()):
    rows = weight.shape[0]
    n_grp = len(parts) // 2
    sub = parts[0].shape[2] // n_dp
    wide = 2 * n_grp * sub
    dims = (2, parts[0].shape[1], sub)
    mine = pl.BlockSpec(dims, lambda i, w: (0, 0, i * (1 - w[1])))
    other = pl.BlockSpec(dims, lambda i, w: (0, 0, i * w[1]))
    last = [] if before is None else [before]
    return call(
        partial(body, n_grp, n_dp),
        (shape(weight.shape, F32), shape((rows, sub), F32), *extras),
        grid_spec=pltpu.PrefetchScalarGridSpec(
            num_scalar_prefetch=1,
            grid=(n_dp,),
            in_specs=[
                pl.BlockSpec((rows, wide), lambda i, w: (0, side * n_dp + i)),
                pl.BlockSpec((rows, 1), lambda i, w: (0, 0)),
            ]
            + [mine] * n_grp
            + [other] * n_grp
            + [pl.BlockSpec(memory_space=pl.ANY)] * len(last),
            out_specs=[
                pl.BlockSpec((rows, wide), lambda i, w: (0, side * n_dp + i)),
                pl.BlockSpec((rows, sub), lambda i, w: (0, 0)),
            ]
            + [pl.BlockSpec(v.shape, lambda i, w: (0, 0)) for v in extras],
            scratch_shapes=list(scratch),
        ),
        input_output_aliases={3 + len(parts): 0} if last else {},
        cost_estimate=cost(8e9),
    )(where, weight, gain, *parts, *last)


def rms_of(hidden):
    return lax.rsqrt(jnp.mean(hidden * hidden, axis=1, keepdims=True) + EPSILON)


def slot_masks(lengths, length):
    ends = jnp.cumsum(lengths, axis=1)
    position = jnp.arange(length, dtype=jnp.int32)
    segment = jnp.sum((position[None, :, None] >= ends[:, None, :]).astype(jnp.int32), axis=2)
    valid = (position[None, :] < ends[:, -1:]).astype(F32)
    same = []
    for lag in (1, 2, 3):
        before = jnp.concatenate([jnp.full((segment.shape[0], lag), -1, jnp.int32), segment[:, :-lag]], axis=1)
        same.append((before == segment).astype(F32))
    stack = jnp.stack([same[0]] + same, axis=2).reshape(-1, 4, 1)
    spread = jnp.broadcast_to(stack, stack.shape[:2] + (LANES,)).reshape(-1, 4 * LANES)
    return spread, valid


def everywhere(value, axis):
    return lax.all_gather(value, "dp", axis=axis, tiled=True)


def after(value, *others):
    return lax.optimization_barrier((value, *others))[0]


def on_any_line(boundary, doc_lengths, norm_gain, in_weight, conv_weight, conv_bias, down_weight, kq_weight,
              dt_weight, dt_bias, skip_weight, out_weight):
    s = lax.axis_index("section")
    g = lax.axis_index("grp")
    n_grp = lax.axis_size("grp")
    n_dp = lax.axis_size("dp")
    length, width = boundary.shape[3], boundary.shape[4]
    inner = in_weight.shape[2] // 2
    block = inner // n_dp
    sub = block // (2 * n_grp)
    half = sub * n_dp
    mine_first = s == 0
    gain = norm_gain[0].astype(F32)[:, None]

    def pick(first, second):
        return jnp.where(mine_first, first, second)

    rows = boundary[0, :, 0]
    traded = swap(pick(rows[1], rows[0]), "section", 1)
    hidden = pick(rows[0], traded)
    cotangent = pick(traded, rows[1])
    lengths = lax.dynamic_index_in_dim(doc_lengths[:, 0], s, 0, keepdims=True)
    all_lengths = jnp.concatenate([lengths] + peers(lengths), axis=0)
    masks, valid = slot_masks(all_lengths, length)
    valid = valid[0][:, None]

    def columns(array):
        blocks = array.shape[1] // block
        view = array.reshape(array.shape[0], blocks, n_grp, 2, sub)
        view = lax.dynamic_index_in_dim(view, g, 2, keepdims=False)
        halves = [view[:, :, h].reshape(array.shape[0], blocks * sub) for h in (0, 1)]
        return pick(*halves), pick(halves[1], halves[0])

    def side(which):
        part = in_weight[0, :, which * inner : (which + 1) * inner]
        return columns((part.astype(F32) * gain).astype(BF))

    def out_side():
        view = lax.dynamic_slice_in_dim(out_weight[0], g * 2 * sub, 2 * sub, 0)
        return pick(view[:sub], view[sub:]), pick(view[sub:], view[:sub])

    def small_side():
        def lanes(array):
            return lax.dynamic_slice_in_dim(array, g * 2 * sub, 2 * sub, 1)

        down = lax.dynamic_slice_in_dim(down_weight[0], g * 2 * sub, 2 * sub, 0).T
        view = jnp.concatenate(
            [down, lanes(kq_weight[0]), jnp.zeros((2 * LANES - RANK - 2 * STATE, 2 * sub), BF), lanes(dt_weight[0]),
             lanes(conv_weight[0]), lanes(conv_bias), lanes(dt_bias), lanes(skip_weight)], axis=0)
        return pick(view[:, :sub], view[:, sub:]), pick(view[:, sub:], view[:, :sub])

    def two_layers(keep, send):
        come = swap(send, "section", 1)
        return pick(keep, come), pick(come, keep)

    x_sides, s_sides = two_layers(*side(0)), two_layers(*small_side())
    g_sides, o_sides = two_layers(*side(1)), two_layers(*out_side())

    def with_far(near):
        return near, swap(near, "section", 1)

    layers = []
    for l in (0, 1):
        w_s = jnp.concatenate(with_far(everywhere(s_sides[l], 1)), axis=1)
        w_x = with_far(everywhere(x_sides[l], 0))
        w_g = with_far(everywhere(g_sides[l], 0))
        w_o = with_far(everywhere(o_sides[l], 0))
        cat = w_s[: 2 * LANES]
        wdt = w_s[2 * LANES : 2 * LANES + RANK]
        tail = w_s[2 * LANES + RANK :].astype(F32)
        vec = jnp.concatenate([tail, jnp.zeros((9, tail.shape[1]), F32)], axis=0)
        layers.append((w_x, w_g, w_o, cat, wdt, vec))

    def group(value):
        return jnp.concatenate([value] + peers(value), axis=0)

    def scatter(value):
        total = value[:length].astype(F32)
        for d in range(1, n_grp):
            total = total + swap(value[d * length : (d + 1) * length], "grp", d).astype(F32)
        return total

    def forward(h, layer):
        w_x, w_g, w_o, cat, wdt, vec = layer
        a = group((h * rms_of(h)).astype(BF))
        x, act, part = proj_conv(n_grp, a, *w_x, masks, vec, cat)
        gate = proj(a, *w_g, 0)
        return a, x, gate, act, [part] + peers(part)

    def gated_back(saved, layer, dgated, y, rec_out):
        gate = saved[2]
        if y is None:
            y = rec_out[5]
        return gate_back(n_grp, y, gate, dgated) + tuple(rec_out)

    def backward(h, dout, dbranch, layer, saved, rec_out):
        w_x, w_g, w_o, cat, wdt, vec = layer
        a, x, gate, act, parts = saved
        gated_near, gated_far, dgate_near, dgate_far, lr, dstate, dpart, ddt, dvec = rec_out[:9]
        dx_near, dx_far, dsmall, dconv = conv_bwd([dpart] + peers(dpart), x, act, dstate, masks, vec, cat)
        scaled = scatter(total_of([dx_near, dx_far, dgate_near, dgate_far], [*w_x, *w_g], 1))
        rms = rms_of(h)
        own = h * rms
        dh = dout + rms * (scaled - own * jnp.mean(scaled * own, axis=1, keepdims=True))

        a_far, dbranch_far = swap(a, "section", 1), swap(dbranch, "section", 1)
        dgate_come, gated_come = swap(dgate_far, "section", 1), swap(gated_far, "section", 1)
        dx_come = swap(dx_far, "section", 1)

        def both(left, right, left_come, right_come):
            return (dot(left, right, 0, 0) + dot(left_come, right_come, 0, 0)).astype(BF)

        grad_g = both(a, dgate_near, a_far, dgate_come)
        grad_o = both(gated_near, dbranch, gated_come, dbranch_far)
        grad_x = both(a, dx_near, a_far, dx_come)
        grad_s = jnp.concatenate([dsmall, ddt, dconv[:5], dvec[:2], jnp.zeros((1, ddt.shape[1]), F32)], axis=0)
        grad_s = grad_s[:, :half] + swap(grad_s[:, half:].astype(BF), "section", 1).astype(F32)
        grad_o = jnp.concatenate([grad_o, grad_s.T.astype(BF)], axis=1)
        return dh, (grad_g, grad_o, grad_x)

    h0 = hidden.astype(F32)
    saved0 = forward(h0, layers[0])
    y0 = rec(saved0[4], saved0[3], None, layers[0][4], layers[0][5], masks, True)
    gated0 = gate_values(y0, saved0[2])[0].astype(BF)
    branch0 = scatter(total_of([gated0[:, :half], gated0[:, half:]], layers[0][2], 0))
    h1 = (h0 + valid * branch0).astype(BF).astype(F32)
    saved1 = forward(h1, layers[1])
    dout1 = cotangent.astype(F32)
    dbranch1 = group((valid * dout1).astype(BF))
    dgated1 = proj(dbranch1, *layers[1][2], 1)
    dy1 = gate_values(dgated1, saved1[2])[0]
    rec1 = rec(saved1[4], saved1[3], dy1, layers[1][4], layers[1][5], masks, True)
    rec1 = gated_back(saved1, layers[1], dgated1, None, rec1)
    branch1 = scatter(total_of(rec1[:2], layers[1][2], 0))
    out1 = h1 + valid * branch1
    dh1, grads1 = backward(h1, dout1, dbranch1, layers[1], saved1, rec1)
    dout0 = dh1.astype(BF).astype(F32)
    dbranch0 = group((valid * dout0).astype(BF))
    dgated0 = proj(dbranch0, *layers[0][2], 1)
    dy0 = gate_values(dgated0, saved0[2])[0]
    rec0 = rec(saved0[4], saved0[3], dy0, layers[0][4], layers[0][5], masks, False)
    rec0 = gated_back(saved0, layers[0], dgated0, y0, rec0)
    dh0, grads0 = backward(h0, dout0, dbranch0, layers[0], saved0, rec0)

    far = swap(pick(out1, dh0), "section", 1)
    result = pick(jnp.stack([dh0, far]), jnp.stack([far, out1]))
    result = result.reshape(1, 2, 1, length, width)

    def collected(l, grad):
        near = lax.psum_scatter(grad, "dp", scatter_dimension=0, tiled=True)
        far = directed(near, "section", [(1 - l, l)])
        halves = jnp.stack([near, far] if l == 0 else [far, near])
        out = [halves]
        for d in range(1, n_grp):
            pairs = [(l * n_grp + i, l * n_grp + (i ^ d)) for i in range(n_grp)]
            out.append(directed(halves, ("section", "grp"), pairs))
        return out

    (g1, o1, x1), (g0, o0, x0) = [[collected(l, grad) for grad in grads] for l, grads in ((1, grads1), (0, grads0))]

    def in_order(firsts, seconds):
        return jnp.stack([pick(a, b) for a, b in zip(firsts, seconds)])[jnp.arange(n_grp) ^ g]

    smalls = in_order([v[:, :, width:] for v in o0], [v[:, :, width:] for v in o1]).astype(F32)
    grad_small = smalls.transpose(3, 0, 1, 2).reshape(smalls.shape[3], block)
    sides = []
    for first, second in ((x0, x1), (g0, g1)):
        value = in_order(first, second).reshape(n_grp, 2, -1, n_dp, sub)
        sides.append(value.transpose(2, 3, 0, 1, 4).reshape(value.shape[2], inner))
    product = jnp.concatenate(sides, axis=1).astype(F32)
    grad_in = product * gain
    grad_gain = jnp.sum(product * in_weight[0].astype(F32), axis=1)
    grad_out = in_order([v[:, :, :width] for v in o0], [v[:, :, :width] for v in o1]).astype(F32).reshape(block, width)
    base = 2 * LANES + RANK
    return (
        result,
        grad_gain[None],
        grad_in[None],
        grad_small[None, base : base + 4],
        grad_small[base + 4][None],
        grad_small[:RANK].T[None],
        grad_small[None, RANK : RANK + 2 * STATE],
        grad_small[None, 2 * LANES : base],
        grad_small[base + 5][None],
        grad_small[base + 6][None],
        grad_out[None],
    )


def on_device(boundary, doc_lengths, norm_gain, in_weight, conv_weight, conv_bias, down_weight, kq_weight,
              dt_weight, dt_bias, skip_weight, out_weight):
    s = lax.axis_index("section")
    g = lax.axis_index("grp")
    n_grp = lax.axis_size("grp")
    n_dp = lax.axis_size("dp")
    length, width = boundary.shape[3], boundary.shape[4]
    inner = in_weight.shape[2] // 2
    block = inner // n_dp
    sub = block // (2 * n_grp)
    n_rows = width // n_dp
    mine_first = s == 0
    where = jnp.stack([g, s]).astype(jnp.int32)
    gain = norm_gain[0].astype(F32)[:, None]

    def pick(first, second):
        return jnp.where(mine_first, first, second)

    def section(value):
        return swap(value, "section", 1)

    def two_layers(keep, send):
        come = section(send)
        return pick(keep, come), pick(come, keep)

    def group(value):
        return jnp.concatenate([value] + peers(value), axis=0)

    def scatter(value):
        total = value[:length].astype(F32)
        come = [swap(value[d * length : (d + 1) * length], "grp", d) for d in range(1, n_grp)]
        for piece in come:
            total = total + piece.astype(F32)
        return total, come

    def line(value):
        return lax.all_gather(value, "dp", axis=0)

    p_sides = two_layers(*cut_small(where, in_weight[0], gain, down_weight[0], kq_weight[0], dt_weight[0],
                                    conv_weight[0], conv_bias, dt_bias, skip_weight, n_dp, n_grp, sub))
    p0 = line(p_sides[0])
    rows = boundary[0, :, 0]
    traded = section(pick(rows[1], rows[0]))
    hidden = pick(rows[0], traded)
    cotangent = pick(traded, rows[1])
    lengths = lax.dynamic_index_in_dim(doc_lengths[:, 0], s, 0, keepdims=True)
    all_lengths = jnp.concatenate([lengths] + peers(lengths), axis=0)
    masks, valid = slot_masks(all_lengths, length)
    valid = valid[0][:, None]
    h0 = hidden.astype(F32)
    a0_parts = peers((h0 * rms_of(h0)).astype(BF))
    a0 = jnp.concatenate([(h0 * rms_of(h0)).astype(BF)] + a0_parts, axis=0)
    q_sides = two_layers(*cut_out(where, in_weight[0], gain, out_weight[0], n_dp, n_grp, sub))
    p0_far = section(after(p0, q_sides[0], *a0_parts))
    q0 = line(after(q_sides[0], p0, a0))
    dout1 = cotangent.astype(F32)

    def input_gradient(h, dout, scaled):
        rms = rms_of(h)
        own = h * rms
        return dout + rms * (scaled - own * jnp.mean(scaled * own, axis=1, keepdims=True))

    def summed(grad):
        return lax.psum_scatter(grad, "dp", scatter_dimension=0, tiled=True)[0]

    def collected(l, near):
        far = directed(near, "section", [(1 - l, l)])
        halves = jnp.stack([near, far] if l == 0 else [far, near])
        out = [halves]
        for d in range(1, n_grp):
            pairs = [(l * n_grp + i, l * n_grp + (i ^ d)) for i in range(n_grp)]
            out.append(directed(halves, ("section", "grp"), pairs))
        return out

    def gradient_q(a, a_far, dbranch, dbranch_far, gated, gated_far, dgate, dgate_far):
        return grad_q(a, a_far, dgate, section(dgate_far), gated, section(gated_far), dbranch, dbranch_far, n_dp)

    def gradient_p(a, a_far, dx_near, dx_far, dsmall, ddt, dconv, dvec):
        small_near, small_far = small_grads(dsmall, ddt, dconv, dvec)
        return grad_p(a, a_far, dx_near, section(dx_far), small_near, section(small_far), n_dp)

    x0, act0, part0, cat0, wdt0, vec0 = first_products(n_grp, a0, masks, p0, p0_far, n_rows)
    parts0 = [part0] + peers(part0)
    y0 = rec(parts0, act0, None, wdt0, vec0, masks, True)
    dbranch1 = group(after((valid * dout1).astype(BF), y0))
    q0_far = section(after(q0, dbranch1))
    p1 = line(after(p_sides[1], q0, dbranch1))
    a0_far = section(after(a0, y0))
    gate0, gated0_near, gated0_far = gate_product(a0, y0, q0, q0_far, n_rows)
    branch0 = scatter(branch_product(gated0_near, gated0_far, q0, q0_far, n_rows))[0]
    h1 = (h0 + valid * branch0).astype(BF).astype(F32)

    p1_far = section(after(p1, h1))
    q1 = line(after(q_sides[1], p1, h1))
    a1 = group((h1 * rms_of(h1)).astype(BF))
    x1, act1, part1, cat1, wdt1, vec1 = first_products(n_grp, a1, masks, p1, p1_far, n_rows)
    parts1 = [part1] + peers(part1)
    a1_far = section(after(a1, part1))
    y1 = rec(parts1, act1, None, wdt1, vec1, masks, True)
    q1_far = section(after(q1, y1))
    dbranch1_far = section(after(dbranch1, y1))
    gate1, gated1_near, gated1_far = gate_product(a1, y1, q1, q1_far, n_rows)

    dy1, dgate1_near, dgate1_far = dgated_product(dbranch1, y1, gate1, q1, q1_far, n_rows)
    gq1 = gradient_q(a1, a1_far, dbranch1, dbranch1_far, gated1_near, gated1_far, dgate1_near, dgate1_far)
    sq1 = summed(gq1)
    branch1 = branch_product(gated1_near, gated1_far, q1, q1_far, n_rows)
    lr1, dstate1, dpart1, ddt1, dvec1 = rec(parts1, act1, after(dy1, gq1, branch1), wdt1, vec1, masks, False)
    out1 = h1 + valid * scatter(branch1)[0]
    dparts1 = [dpart1] + peers(dpart1)
    dstate1 = after(dstate1, out1)
    dx1_near, dx1_far, dsmall1, dconv1 = conv_bwd(dparts1, x1, act1, dstate1, masks, vec1, cat1)
    dnormed1 = dnormed_product(
        [dx1_near, dx1_far, dgate1_near, dgate1_far], p1, p1_far, q1, q1_far, n_rows)
    scaled1, come1 = scatter(dnormed1)
    dh1 = input_gradient(h1, dout1, scaled1)
    gp1 = gradient_p(a1, a1_far, after(dx1_near, come1[0]), dx1_far, dsmall1, ddt1, dconv1, dvec1)
    sp1 = summed(after(gp1, sq1))
    dout0 = dh1.astype(BF).astype(F32)
    dbranch0 = group((valid * dout0).astype(BF))

    q_parts1 = collected(1, after(sq1, dbranch0))
    dbranch0_far = section(dbranch0)
    dy0, dgate0_near, dgate0_far = dgated_product(after(dbranch0, gp1), y0, gate0, q0, q0_far, n_rows)
    gq0 = gradient_q(a0, a0_far, dbranch0, dbranch0_far, gated0_near, gated0_far, dgate0_near, dgate0_far)
    lr0, dstate0, dpart0, ddt0, dvec0 = rec(parts0, act0, after(dy0, gq0, sp1), wdt0, vec0, masks, False)
    p_parts1 = collected(1, sp1)
    sq0 = summed(after(gq0, sp1))
    dparts0 = [dpart0] + peers(dpart0)
    dstate0 = after(dstate0, *q_parts1, *p_parts1)
    dx0_near, dx0_far, dsmall0, dconv0 = conv_bwd(dparts0, x0, act0, dstate0, masks, vec0, cat0)
    gp0 = gradient_p(a0, a0_far, dx0_near, dx0_far, dsmall0, ddt0, dconv0, dvec0)
    sp0 = summed(after(gp0, sq0))
    q_parts0 = collected(0, sq0)
    dnormed0 = dnormed_product(
        [after(dx0_near, gp0), dx0_far, dgate0_near, dgate0_far], p0, p0_far, q0, q0_far, n_rows)
    p_parts0 = collected(0, after(sp0, dnormed0, *q_parts0))
    dh0 = input_gradient(h0, dout0, after(scatter(dnormed0)[0], p_parts0[0]))

    out_far = directed(out1, "section", [(0, 1)])
    dh_far = directed(dh0, "section", [(1, 0)])
    result = jnp.stack([pick(dh0, out_far), pick(dh_far, out1)]).reshape(1, 2, 1, length, width)

    grad_in, sum_q, grad_out = join_packed(
        join_q_body, where, in_weight[0], gain, q_parts0 + q_parts1, None, 1, n_dp, [shape((block, width), F32)])
    smalls = [shape(v, F32) for v in ((block, RANK), (2 * STATE, block), (RANK, block), (4, block))]
    smalls += [shape((1, block), F32)] * 3
    grad_in, sum_p, grad_down, grad_kq, grad_dt, grad_conv, grad_cb, grad_db, grad_skip = join_packed(
        join_p_body, where, in_weight[0], gain, p_parts0 + p_parts1, grad_in, 0, n_dp, smalls,
        [pltpu.VMEM((SMALL, block), F32)])
    grad_gain = jnp.sum(sum_q + sum_p, axis=1)
    return (
        result,
        grad_gain[None],
        grad_in[None],
        grad_conv[None],
        grad_cb,
        grad_down[None],
        grad_kq[None],
        grad_dt[None],
        grad_db,
        grad_skip,
        grad_out[None],
    )


def solution(mesh):
    packed = mesh.shape["dp"] == 4 and mesh.shape["grp"] == 4
    return jax.shard_map(
        on_device if packed else on_any_line,
        mesh=mesh,
        in_specs=(
            P("section", None, ("grp", "dp"), None, None),
            P(None, ("grp", "dp"), None),
            P("section", "dp"),
            P("section", "dp", None),
            P("section", None, "dp"),
            P("section", "dp"),
            P("section", "dp", None),
            P("section", None, "dp"),
            P("section", None, "dp"),
            P("section", "dp"),
            P("section", "dp"),
            P("section", "dp", None),
        ),
        out_specs=(
            P("section", None, ("grp", "dp"), None, None),
            P("section", "dp"),
            P("section", "dp", None),
            P("section", None, "dp"),
            P("section", "dp"),
            P("section", "dp", None),
            P("section", None, "dp"),
            P("section", None, "dp"),
            P("section", "dp"),
            P("section", "dp"),
            P("section", "dp", None),
        ),
        check_vma=False,
    )
```
